32 devices in a mesh: fsdp: 16 (over z, x, core), pos: 2 (over y).
Axes of the slice: x: 2, y: 2, z: 4, core: 2. Of those that a mesh axis runs over, the one named last changes fastest.
Arguments:
- inputs: bfloat16 [4096, 2, 1024], P('fsdp', 'pos'), may hold values from -6 to 6
- frame_flags: int32 [4096], P('fsdp'), may hold values 0 or 1
- attn_gain: bfloat16 [1, 2, 1024], P(None, 'pos', 'fsdp'), may hold values from 0.25 to 1.75
- qkv_weight: bfloat16 [1, 2, 1024, 3072], P(None, 'pos', 'fsdp'), may hold values from -0.1875 to 0.1875
- out_weight: bfloat16 [1, 2, 1024, 1024], P(None, 'pos', 'fsdp'), may hold values from -0.25 to 0.25
- ffn_gain: bfloat16 [1, 2, 1024], P(None, 'pos', 'fsdp'), may hold values from 0.25 to 1.75
- gate_up_weight: bfloat16 [1, 2, 1024, 8192], P(None, 'pos', 'fsdp'), may hold values from -0.1875 to 0.1875
- down_weight: bfloat16 [1, 2, 4096, 1024], P(None, 'pos', 'fsdp'), may hold values from -0.1875 to 0.1875
- cotangent: bfloat16 [4096, 2, 1024], P('fsdp', 'pos'), may hold values from -6 to 6
Outputs:
- outputs: bfloat16 [4096, 2, 1024], P('fsdp', 'pos')
- input_grad: float32 [4096, 2, 1024], P('fsdp', 'pos')
- attn_gain_grad: float32 [1, 2, 1024], P(None, 'pos', 'fsdp')
- qkv_weight_grad: float32 [1, 2, 1024, 3072], P(None, 'pos', 'fsdp')
- out_weight_grad: float32 [1, 2, 1024, 1024], P(None, 'pos', 'fsdp')
- ffn_gain_grad: float32 [1, 2, 1024], P(None, 'pos', 'fsdp')
- gate_up_weight_grad: float32 [1, 2, 1024, 8192], P(None, 'pos', 'fsdp')
- down_weight_grad: float32 [1, 2, 4096, 1024], P(None, 'pos', 'fsdp')
The draws below stay inside these ranges and needn't reach their ends.
All inputs are finite; a program needn't handle non-finite values. No bound on the sum of `frame_flags` on one device may be relied on, other than what follows from the above.
Results may differ from the reference program's by a relative error of at most 0.01.
Values may be sent and summed in bfloat16 or wider, within the bound.
A program may use at most 192 MiB of HBM per device.

```python
import math
import jax
import jax.numpy as jnp
from jax import lax

D = 1024
HEADS = 16
HEAD_DIM = 64
FF = 4096
LAYERS = 1
FRAMES = 4096
POS = 2


def set_ends(array, rng, low, high):
    dims = array.shape
    place = [jax.random.randint(jax.random.fold_in(rng, axis), (), 0, dims[axis]) for axis in range(len(dims))]
    array = array.at[tuple(place)].set(low)
    longest = dims.index(max(dims))
    place[longest] = (place[longest] + 1) % dims[longest]
    return array.at[tuple(place)].set(high)


def block_levels(own_key, extent, split, least, top_value):
    def one(position, shards_of):
        draws = jax.random.uniform(jax.random.fold_in(jax.random.fold_in(own_key, 6), position), (shards_of,), jnp.float32, least / len(split), top_value / len(split))
        return jnp.repeat(jnp.exp(draws), extent[position] // shards_of).reshape((-1,) + (1,) * (len(extent) - position - 1))

    loudness = one(*split[0])
    for cut in split[1:]:
        loudness = loudness * one(*cut)
    return loudness


def noise(key, extent, deviation, bound, shards=(), kind=jnp.bfloat16):
    values = deviation * jax.random.normal(key, extent, jnp.float32)
    if shards:
        values = values * block_levels(key, extent, shards, -0.22, 0.18)
    return jnp.clip(values, -bound, bound).astype(kind)


def setup_inputs(seed: int = 0) -> dict:
    streams_of = jax.random.split(jax.random.key(seed), 10)
    return {
        "inputs": noise(streams_of[0], (FRAMES, POS, D), 1.0, 6.0, ((0, 16), (1, 2))),
        "frame_flags": set_ends((jax.random.randint(streams_of[1], (FRAMES,), 0, 4) < 3).astype(jnp.int32), jax.random.fold_in(streams_of[1], 1), 0, 1),
        "attn_gain": jnp.clip(1.0 + 0.15 * jax.random.normal(streams_of[2], (LAYERS, POS, D), jnp.float32), 0.25, 1.75).astype(jnp.bfloat16),
        "qkv_weight": noise(streams_of[3], (LAYERS, POS, D, 3 * D), D ** -0.5, 0.1875, ((1, 2), (2, 16))),
        "out_weight": noise(streams_of[4], (LAYERS, POS, D, D), (D // 2) ** -0.5, 0.25, ((1, 2), (2, 16))),
        "ffn_gain": jnp.clip(1.0 + 0.15 * jax.random.normal(streams_of[5], (LAYERS, POS, D), jnp.float32), 0.25, 1.75).astype(jnp.bfloat16),
        "gate_up_weight": noise(streams_of[6], (LAYERS, POS, D, 2 * FF), D ** -0.5, 0.1875, ((1, 2), (2, 16))),
        "down_weight": noise(streams_of[7], (LAYERS, POS, FF, D), (FF // 4) ** -0.5, 0.1875, ((1, 2), (2, 16))),
        "cotangent": noise(streams_of[8], (FRAMES, POS, D), 1.0, 6.0, ((0, 16), (1, 2))),
    }


EPSILON = 1e-06
MASKED = -1e+30
PRECISE = lax.Precision.HIGHEST

@jax.custom_vjp
def low(v):
    return lax.optimization_barrier(v.astype(jnp.bfloat16)).astype(jnp.float32)

@jax.custom_vjp
def low_back(v):
    return v

def low_keep(v):
    return (low(v), None)

def low_pass(kept, grad):
    return (grad,)

def back_keep(v):
    return (v, None)

def back_low(kept, grad):
    return (low(grad),)
low.defvjp(low_keep, low_pass)
low_back.defvjp(back_keep, back_low)

def rms_scaled(hidden, gain_row):
    inv_rms = lax.rsqrt(lax.optimization_barrier(jnp.mean(hidden * hidden, axis=-1, keepdims=True)) + EPSILON)
    return hidden * inv_rms * gain_row[None]

def apply_rows(left_side, weight):
    return jnp.einsum('fpd,pde->fpe', left_side, weight, precision=PRECISE)

def split_heads(rows):
    return rows.reshape(rows.shape[0], rows.shape[1], HEADS, HEAD_DIM)

def attend(qkv_rows):
    frames, places = (qkv_rows.shape[0], qkv_rows.shape[1])
    queries = split_heads(qkv_rows[..., :D])
    keys_all = split_heads(qkv_rows[..., D:2 * D])
    values_all = split_heads(qkv_rows[..., 2 * D:])
    scores = jnp.einsum('fphe,fjhe->fhpj', queries, keys_all, precision=PRECISE) / math.sqrt(HEAD_DIM)
    causal = jnp.arange(places)[:, None] >= jnp.arange(places)[None, :]
    scores = jnp.where(causal, scores, MASKED)
    row_max = lax.optimization_barrier(jnp.max(scores, axis=-1, keepdims=True))
    exponent = jnp.exp(scores - row_max)
    attn_probs = exponent / lax.optimization_barrier(jnp.sum(exponent, axis=-1, keepdims=True))
    mixed_heads = jnp.einsum('fhpj,fjhe->fphe', attn_probs, values_all, precision=PRECISE)
    return mixed_heads.reshape(frames, places, D)

def one_layer(hidden, frame_mask, layer_params):
    gain_one, qkv_full, out_full, gain_two, gate_up_full, down_full = layer_params
    normed = low(rms_scaled(hidden, gain_one))
    qkv_rows = low(low_back(apply_rows(normed, qkv_full)))
    mixed_heads = low(attend(qkv_rows))
    hidden_mid = hidden + low_back(apply_rows(mixed_heads, out_full))
    normed_two = low(rms_scaled(hidden_mid, gain_two))
    gate_up = low_back(apply_rows(normed_two, gate_up_full))
    gate_part = gate_up[..., :FF]
    up_part = gate_up[..., FF:]
    act_rows = low(jax.nn.silu(gate_part) * up_part)
    ffn_out = low_back(apply_rows(act_rows, down_full))
    return frame_mask * (hidden_mid + ffn_out)

def reference(inputs, frame_flags, attn_gain, qkv_weight, out_weight, ffn_gain, gate_up_weight, down_weight, cotangent):
    params = tuple((tensor.astype(jnp.float32) for tensor in (attn_gain, qkv_weight, out_weight, ffn_gain, gate_up_weight, down_weight)))
    frames = inputs.shape[0]
    block_len = math.gcd(frames, 1024)
    blocks_count = frames // block_len
    block_shape = (blocks_count, block_len) + inputs.shape[1:]
    states = inputs.astype(jnp.float32).reshape(block_shape)
    cotangents = cotangent.astype(jnp.float32).reshape(block_shape)
    mask_blocks = frame_flags.astype(jnp.float32).reshape(blocks_count, block_len, 1, 1)

    def block_step(totals, pieces):
        state_rows, mask_rows, cot_rows = pieces

        def forward(weights_all, hidden):
            for layer_idx in range(LAYERS):
                hidden = one_layer(hidden, mask_rows, tuple((tensor[layer_idx] for tensor in weights_all)))
            return hidden
        result, pullback = jax.vjp(forward, params, state_rows)
        grad_params, grad_input = pullback(cot_rows)
        totals = jax.tree.map(jnp.add, totals, grad_params)
        return (totals, (result.astype(jnp.bfloat16), grad_input))
    zeros_tree = jax.tree.map(jnp.zeros_like, params)
    totals, outs_pair = lax.scan(block_step, zeros_tree, (states, mask_blocks, cotangents))
    results, grad_inputs = outs_pair
    return (results.reshape(inputs.shape), grad_inputs.reshape(inputs.shape), totals[0], totals[1], totals[2], totals[3], totals[4], totals[5])
```

```python
import functools
import math

import jax
import jax.numpy as jnp
from jax import lax
from jax.experimental import pallas as pl
from jax.experimental.pallas import tpu as pltpu
from jax.sharding import PartitionSpec as P

D = 1024
HEADS = 16
HEAD_DIM = 64
FF = 4096


EPSILON = 1e-06
MASKED = -1e30
PRECISE = lax.Precision.HIGHEST


def rms_parts(hidden, gain_row):
    inv_rms = lax.rsqrt(jnp.mean(hidden * hidden, axis=-1, keepdims=True) + EPSILON)
    return (hidden * inv_rms * gain_row[None], inv_rms)


def rms_back(grad_rows, hidden, inv_rms, gain_row):
    scaled = grad_rows * gain_row[None]
    gain_grad = jnp.sum(grad_rows * hidden * inv_rms, axis=0)
    inner_mean = jnp.mean(scaled * hidden, axis=-1, keepdims=True)
    return (inv_rms * scaled - hidden * inv_rms**3 * inner_mean, gain_grad)


def apply_rows(left_side, weight):
    return jnp.einsum("fpd,pde->fpe", left_side, weight, preferred_element_type=jnp.float32)


def apply_back(grad_rows, weight):
    return jnp.einsum("fpe,pde->fpd", grad_rows, weight, preferred_element_type=jnp.float32)


def outer_sum(left_side, grad_rows):
    return jnp.einsum("fpd,fpe->pde", left_side, grad_rows, preferred_element_type=jnp.float32)


def split_heads(rows):
    return rows.reshape(rows.shape[0], rows.shape[1], HEADS, HEAD_DIM)


def attention_weights(attn_gain, qkv_weight, out_weight, layer_idx):
    return (
        lax.all_gather(attn_gain[layer_idx], "fsdp", axis=1, tiled=True),
        lax.all_gather(qkv_weight[layer_idx], "fsdp", axis=1, tiled=True),
        lax.all_gather(out_weight[layer_idx], "fsdp", axis=1, tiled=True),
    )


def ffn_weights(ffn_gain, gate_up_weight, down_weight, layer_idx):
    return (
        lax.all_gather(ffn_gain[layer_idx], "fsdp", axis=1, tiled=True),
        lax.all_gather(gate_up_weight[layer_idx], "fsdp", axis=1, tiled=True),
        lax.all_gather(down_weight[layer_idx], "fsdp", axis=1, tiled=True),
    )


def attention_forward(qkv_rows):
    frames, places = (qkv_rows.shape[0], qkv_rows.shape[1])
    pos_count = lax.axis_size("pos")
    frame_part = frames // pos_count
    outgoing = qkv_rows.reshape(pos_count, frame_part, places, 3 * D)
    frame_qkv = lax.all_to_all(outgoing, "pos", split_axis=0, concat_axis=2, tiled=True)[0].astype(
        jnp.float32
    )
    whole_places = frame_qkv.shape[1]
    queries = split_heads(frame_qkv[..., :D])
    keys_all = split_heads(frame_qkv[..., D : 2 * D])
    values_all = split_heads(frame_qkv[..., 2 * D :])
    scores = jnp.einsum("fphe,fjhe->fhpj", queries, keys_all, precision=PRECISE) / math.sqrt(
        HEAD_DIM
    )
    causal = jnp.arange(whole_places)[:, None] >= jnp.arange(whole_places)[None, :]
    scores = jnp.where(causal, scores, MASKED)
    row_max = jnp.max(scores, axis=-1, keepdims=True)
    exponent = jnp.exp(scores - row_max)
    attn_probs = exponent / jnp.sum(exponent, axis=-1, keepdims=True)
    mixed_heads = jnp.einsum("fhpj,fjhe->fphe", attn_probs, values_all, precision=PRECISE)
    mixed_frames = mixed_heads.reshape(frame_part, whole_places, D).astype(jnp.bfloat16)
    returned = lax.all_to_all(mixed_frames[None], "pos", split_axis=2, concat_axis=0, tiled=True)
    return (returned.reshape(frames, places, D), (queries, keys_all, values_all, attn_probs))


def attention_backward(grad_mixed, attn_keep):
    queries, keys_all, values_all, attn_probs = attn_keep
    frames, places = (grad_mixed.shape[0], grad_mixed.shape[1])
    pos_count = lax.axis_size("pos")
    frame_part = frames // pos_count
    outgoing = grad_mixed.reshape(pos_count, frame_part, places, D)
    grad_frames = lax.all_to_all(
        outgoing.astype(jnp.bfloat16), "pos", split_axis=0, concat_axis=2, tiled=True
    ).astype(outgoing.dtype)[0]
    whole_places = grad_frames.shape[1]
    grad_heads = split_heads(grad_frames)
    grad_values = jnp.einsum("fhpj,fphe->fjhe", attn_probs, grad_heads, precision=PRECISE)
    grad_probs = jnp.einsum("fphe,fjhe->fhpj", grad_heads, values_all, precision=PRECISE)
    grad_scores = (
        attn_probs
        * (grad_probs - jnp.sum(attn_probs * grad_probs, axis=-1, keepdims=True))
        / math.sqrt(HEAD_DIM)
    )
    grad_queries = jnp.einsum("fhpj,fjhe->fphe", grad_scores, keys_all, precision=PRECISE)
    grad_keys = jnp.einsum("fhpj,fphe->fjhe", grad_scores, queries, precision=PRECISE)
    frame_grads = jnp.concatenate(
        [
            grad_queries.reshape(frame_part, whole_places, D),
            grad_keys.reshape(frame_part, whole_places, D),
            grad_values.reshape(frame_part, whole_places, D),
        ],
        axis=-1,
    ).astype(jnp.bfloat16)
    returned = lax.all_to_all(frame_grads[None], "pos", split_axis=2, concat_axis=0, tiled=True)
    return returned.reshape(frames, places, 3 * D)


def layer_forward(hidden, frame_mask, attn_set, ffn_set):
    gain_one, qkv_full, out_full = attn_set
    gain_two, gate_up_full, down_full = ffn_set
    normed, inv_one = rms_parts(hidden, gain_one.astype(jnp.float32))
    normed_low = normed.astype(jnp.bfloat16)
    qkv_rows = apply_rows(normed_low, qkv_full).astype(jnp.bfloat16)
    mixed_low, attn_keep = attention_forward(qkv_rows)
    hidden_mid = hidden + apply_rows(mixed_low, out_full)
    normed_two, inv_two = rms_parts(hidden_mid, gain_two.astype(jnp.float32))
    normed_two_low = normed_two.astype(jnp.bfloat16)
    gate_up = apply_rows(normed_two_low, gate_up_full)
    gate_part = gate_up[..., :FF]
    up_part = gate_up[..., FF:]
    act_low = (jax.nn.silu(gate_part) * up_part).astype(jnp.bfloat16)
    result = frame_mask * (hidden_mid + apply_rows(act_low, down_full))
    kept_state = (
        hidden,
        inv_one,
        normed_low,
        attn_keep,
        mixed_low,
        hidden_mid,
        inv_two,
        normed_two_low,
        gate_part,
        up_part,
        act_low,
    )
    return (result, kept_state)


def layer_backward(grad_out, frame_mask, kept_state, ffn_set, fetch_attn):
    (
        hidden,
        inv_one,
        normed_low,
        attn_keep,
        mixed_low,
        hidden_mid,
        inv_two,
        normed_two_low,
        gate_part,
        up_part,
        act_low,
    ) = kept_state
    gain_two, gate_up_full, down_full = ffn_set
    grad_sum = frame_mask * grad_out
    grad_ffn = grad_sum.astype(jnp.bfloat16)
    down_grad = outer_sum(act_low, grad_ffn)
    down_shard = lax.psum_scatter(down_grad, "fsdp", scatter_dimension=1, tiled=True)
    grad_act = apply_back(grad_ffn, down_full)
    sigmoid_gate = jax.nn.sigmoid(gate_part)
    grad_gate = grad_act * up_part * sigmoid_gate * (1.0 + gate_part * (1.0 - sigmoid_gate))
    grad_up = grad_act * gate_part * sigmoid_gate
    grad_gu = jnp.concatenate([grad_gate, grad_up], axis=-1).astype(jnp.bfloat16)
    gate_up_grad = outer_sum(normed_two_low, grad_gu)
    grad_norm_two = apply_back(grad_gu, gate_up_full)
    grad_mid_norm, gain_two_grad = rms_back(
        grad_norm_two, hidden_mid, inv_two, gain_two.astype(jnp.float32)
    )
    ffn_shards = (
        lax.psum_scatter(gain_two_grad, "fsdp", scatter_dimension=1, tiled=True),
        lax.psum_scatter(gate_up_grad, "fsdp", scatter_dimension=1, tiled=True),
    )
    gain_one, qkv_full, out_full = fetch_attn()
    grad_mid = grad_sum + grad_mid_norm
    grad_attn = grad_mid.astype(jnp.bfloat16)
    out_grad = outer_sum(mixed_low, grad_attn)
    grad_mixed = apply_back(grad_attn, out_full)
    grad_qkv = attention_backward(grad_mixed, attn_keep)
    qkv_grad = outer_sum(normed_low, grad_qkv)
    grad_norm_one = apply_back(grad_qkv, qkv_full)
    grad_in_norm, gain_one_grad = rms_back(
        grad_norm_one, hidden, inv_one, gain_one.astype(jnp.float32)
    )
    attn_shards = (
        lax.psum_scatter(gain_one_grad, "fsdp", scatter_dimension=1, tiled=True),
        lax.psum_scatter(qkv_grad, "fsdp", scatter_dimension=1, tiled=True),
        lax.psum_scatter(out_grad, "fsdp", scatter_dimension=1, tiled=True),
    )
    grad_in = grad_mid + grad_in_norm
    return (
        grad_in,
        (attn_shards[0], attn_shards[1], attn_shards[2], ffn_shards[0], ffn_shards[1], down_shard),
    )


def on_device(
    inputs,
    frame_flags,
    attn_gain,
    qkv_weight,
    out_weight,
    ffn_gain,
    gate_up_weight,
    down_weight,
    cotangent,
):
    layer_total = qkv_weight.shape[0]
    frame_mask = frame_flags.astype(jnp.float32)[:, None, None]
    hidden = inputs.astype(jnp.float32)
    layer_idx = 0
    attn_set = attention_weights(attn_gain, qkv_weight, out_weight, layer_idx)
    ffn_set = ffn_weights(ffn_gain, gate_up_weight, down_weight, layer_idx)
    hidden, kept_state = layer_forward(hidden, frame_mask, attn_set, ffn_set)
    states_all = [kept_state]
    grad_rows = cotangent.astype(jnp.float32)
    layer_grads = [None] * layer_total
    for layer_idx in reversed(range(layer_total)):
        ffn_set = ffn_weights(ffn_gain, gate_up_weight, down_weight, layer_idx)
        fetch_attn = gather_later(attn_gain, qkv_weight, out_weight, layer_idx)
        grad_rows, layer_grads[layer_idx] = layer_backward(
            grad_rows, frame_mask, states_all[layer_idx], ffn_set, fetch_attn
        )
    stacked = [jnp.stack([grad_set[column] for grad_set in layer_grads]) for column in range(6)]
    return (
        hidden.astype(jnp.bfloat16),
        grad_rows,
        stacked[0],
        stacked[1],
        stacked[2],
        stacked[3],
        stacked[4],
        stacked[5],
    )


def gather_later(attn_gain, qkv_weight, out_weight, layer_idx):

    def fetched():
        return attention_weights(attn_gain, qkv_weight, out_weight, layer_idx)

    return fetched


KEY, VALUE, QUERY, OUT = 0, 1, 2, 3
SEMS = 128
MESH = pl.DeviceIdType.MESH


def flip(bit, change):
    return bit + change - 2 * bit * change


def square_kernel(
    x_ref, cot_ref, mask_ref, gain_ref, wqkv, wout, wgu, wd,
    out_ref, ig_ref, gain_out, gu_out, down_out, attn_out,
    wa, wgu_all, wd_all, n2_all, g_all, act_all, ggu_all,
    po_s, po_r, pg_s, pg_r, gu_core, down_core, attn_core, attn_x, attn_z,
    normed, qb, kb, vb, krem, vrem, mixed, hmid, gv_s, gk_s, gv_r, gk_r,
    gq, gk, gv, gmid, gattn, hold_k, p_own, p_rem, r_one, r_two,
    gain_r, gain_f, gsum_s, gsum_r, ends, ends_t,
    ssem, rsem, lsem, gsem_s, gsem_r, hsem_s, hsem_r,
):
    tokens, width = x_ref.shape
    rows = width // 16
    block = 4 * width // 4
    half = block // 2
    ff = 4 * width
    f = lax.axis_index("fsdp")
    y = lax.axis_index("pos")
    c = f % 2
    x = (f // 2) % 2
    z = (f // 4) % 2
    s = f // 8
    f32, bf16 = jnp.float32, jnp.bfloat16

    def peer(ds=0, dz=0, dx=0, dc=0):
        return flip(s, ds) * 8 + flip(z, dz) * 4 + flip(x, dx) * 2 + flip(c, dc)

    def slab(ds=0, dz=0, dx=0, dc=0):
        return flip(s, ds), flip(z, dz), flip(x, dx), flip(c, dc)

    counter = [0]
    pending = []

    def take(n=1):
        counter[0] += n
        assert counter[0] <= SEMS
        return counter[0] - n

    def link(src, dst, to, sem=None, to_y=None):
        if sem is None:
            sem = take()
        copy = pltpu.make_async_remote_copy(
            src_ref=src, dst_ref=dst, send_sem=ssem.at[sem], recv_sem=rsem.at[sem],
            device_id=(to, y if to_y is None else to_y), device_id_type=MESH,
        )
        copy.start()
        return copy

    lcount = [0]

    def local(src, dst):
        lcount[0] += 1
        copy = pltpu.make_async_copy(src, dst, lsem.at[lcount[0] - 1])
        copy.start()
        return copy

    def dot(a, b):
        return jnp.dot(a, b, preferred_element_type=f32)

    def dot_nt(a, b):
        return lax.dot_general(a, b, (((1,), (1,)), ((), ())), preferred_element_type=f32)

    def split(v):
        high = v.astype(bf16)
        return high, (v - high.astype(f32)).astype(bf16)

    def head_sum(v):
        high, low = split(v)
        return dot(high, ends[...]) + dot(low, ends[...])

    def head_spread(p):
        high, low = split(p)
        return dot(high, ends_t[...]) + dot(low, ends_t[...])

    barrier = pltpu.get_barrier_semaphore()

    @pl.loop(1, 16)
    def _(r):
        pl.semaphore_signal(barrier, inc=1, device_id=(lax.rem(f + r, 16), y), device_id_type=MESH)

    pl.semaphore_signal(barrier, inc=1, device_id=(f, 1 - y), device_id_type=MESH)
    pl.semaphore_wait(barrier, 16)

    def gain_copy(r):
        return pltpu.make_async_remote_copy(
            src_ref=gain_ref, dst_ref=gain_r.at[r - 1], send_sem=gsem_s.at[r - 1], recv_sem=gsem_r.at[r - 1],
            device_id=(lax.rem(f + r, 16), y), device_id_type=MESH,
        )

    @pl.loop(1, 16)
    def _(r):
        gain_copy(r).start()

    own_cols = (
        wqkv.at[:, pl.ds(width, width)],
        wqkv.at[:, pl.ds(2 * width, width)],
        wqkv.at[:, pl.ds(0, width)],
        wout,
    )
    started = {}
    keep = []

    def gather_start(g):
        own = wa.at[(g,) + slab()]
        src = own_cols[g]
        started[g] = (
            link(src, own, peer(ds=1)),
            link(src, own, peer(dz=1)),
            link(src, own, peer(dx=1)),
            link(src, own, peer(dc=1)),
            local(src, own),
        )

    def forward(g, at, to):
        ref = wa.at[(g,) + slab(*at)]
        copy = link(ref, ref, to)
        keep.append(copy)
        return copy

    def gather_finish(g):
        cross, zz, xx, core, own = started[g]
        keep.extend((cross, zz, xx, core))
        cross.wait_recv()
        z_two = forward(g, (1, 0, 0, 0), peer(dz=1))
        x_two = forward(g, (1, 0, 0, 0), peer(dx=1))
        cores = [forward(g, (1, 0, 0, 0), peer(dc=1))]
        zz.wait_recv()
        x_three = forward(g, (0, 1, 0, 0), peer(dx=1))
        cores.append(forward(g, (0, 1, 0, 0), peer(dc=1)))
        z_two.wait_recv()
        x_four = forward(g, (1, 1, 0, 0), peer(dx=1))
        cores.append(forward(g, (1, 1, 0, 0), peer(dc=1)))
        for copy, at in ((xx, (0, 0, 1, 0)), (x_two, (1, 0, 1, 0)), (x_three, (0, 1, 1, 0)), (x_four, (1, 1, 1, 0))):
            copy.wait_recv()
            cores.append(forward(g, at, peer(dc=1)))
        own.wait()
        core.wait_recv()
        for copy in cores:
            copy.wait_recv()

    gather_start(KEY)
    gather_start(VALUE)

    ends[...] = (
        lax.broadcasted_iota(jnp.int32, ends.shape, 0) // HEAD_DIM == lax.broadcasted_iota(jnp.int32, ends.shape, 1)
    ).astype(bf16)
    ends_t[...] = (
        lax.broadcasted_iota(jnp.int32, ends_t.shape, 1) // HEAD_DIM == lax.broadcasted_iota(jnp.int32, ends_t.shape, 0)
    ).astype(bf16)

    g_all[z, x] = (cot_ref[...].astype(f32) * mask_ref[...]).astype(bf16).reshape(2, 2, rows, width)

    gain_f[...] = jnp.zeros_like(gain_f)
    lane_block = 128
    per_block = lane_block // rows
    gain_f[f // per_block] += gain_ref[...].astype(f32)

    @pl.loop(1, 16)
    def _(r):
        gain_copy(r).wait()
        gain_f[lax.rem(f + 16 - r, 16) // per_block] += gain_r[r - 1].astype(f32)

    def gain_row(which):
        return jnp.concatenate([gain_f[i, which : which + 1, :] for i in range(gain_f.shape[0])], axis=1)

    steps = tokens // rows

    @pl.loop(0, steps)
    def _(i):
        part = pl.ds(i * rows, rows)
        hidden = x_ref[part].astype(f32)
        inv = lax.rsqrt(jnp.mean(hidden * hidden, axis=-1, keepdims=True) + EPSILON)
        r_one[part] = jnp.broadcast_to(inv, (rows, 128))
        normed[part] = (hidden * inv * gain_row(0)).astype(bf16)

    tile = 256 if width >= 256 else width
    tiles = width // tile
    quarter = width // 4

    def project(left, g, dest):
        @pl.loop(0, tiles)
        def _(t):
            cols = pl.ds(pl.multiple_of(t * tile, tile), tile)
            dest[:, cols] = dot(left[...], wa[g, :, :, :, :, :, cols].reshape(width, tile)).astype(dest.dtype)

    gather_finish(KEY)
    gather_start(QUERY)
    project(normed, KEY, kb)
    k_copy = link(kb, krem, f, to_y=1 - y)
    gather_finish(VALUE)
    gather_start(OUT)
    project(normed, VALUE, vb)
    v_copy = link(vb, vrem, f, to_y=1 - y)
    gather_finish(QUERY)

    gu_sems = {}

    def gu_pieces(flips):
        ds, dz, dx = flips
        j = flip(z, dz) * 2 + flip(x, dx)
        for u in range(2):
            for part in range(2):
                src = wgu.at[:, pl.ds(pl.multiple_of(u * ff + part * (ff // 2) + j * half, half), half)]
                dst = wgu_all.at[s, z, x, c, :, pl.ds(u * block + part * half, half)]
                yield src, dst

    order = ((1, 0, 0), (1, 0, 1), (1, 1, 0), (1, 1, 1), (0, 0, 1), (0, 1, 0), (0, 1, 1))
    for flips in order:
        sem = take()
        gu_sems[flips] = sem
        for src, dst in gu_pieces(flips):
            link(src, dst, peer(*flips), sem=sem)
    own_gu_sem = lsem.at[lcount[0]]
    lcount[0] += 1
    for src, dst in gu_pieces((0, 0, 0)):
        pltpu.make_async_copy(src, dst, own_gu_sem).start()

    own_down = wd_all.at[s, c]
    down_cross = link(wd, own_down, peer(ds=1))
    down_own_core = link(wd, own_down, peer(dc=1))
    down_local = local(wd, own_down)

    project(normed, QUERY, qb)
    gather_finish(OUT)

    g_base = take(3)
    others = ((0, 1), (1, 0), (1, 1))
    for i, (dz, dx) in enumerate(others):
        link(g_all.at[z, x], g_all.at[z, x], peer(0, dz, dx), sem=g_base + i)

    k_copy.wait_recv()
    v_copy.wait_recv()
    scale = 1.0 / math.sqrt(HEAD_DIM)

    @pl.loop(0, steps)
    def _(i):
        part = pl.ds(i * rows, rows)
        query = qb[part].astype(f32)
        own = head_sum(query * kb[part].astype(f32)) * scale
        far = jnp.where(y > 0, head_sum(query * krem[part].astype(f32)) * scale, MASKED)
        top = jnp.maximum(own, far)
        own = jnp.exp(own - top)
        far = jnp.exp(far - top)
        total = own + far
        own = own / total
        far = far / total
        p_own[part] = own
        p_rem[part] = far
        mixed[part] = (head_spread(own) * vb[part].astype(f32) + head_spread(far) * vrem[part].astype(f32)).astype(bf16)

    project(mixed, OUT, hmid)

    @pl.loop(0, steps)
    def _(i):
        part = pl.ds(i * rows, rows)
        hidden = x_ref[part].astype(f32) + hmid[part]
        hmid[part] = hidden
        inv = lax.rsqrt(jnp.mean(hidden * hidden, axis=-1, keepdims=True) + EPSILON)
        r_two[part] = jnp.broadcast_to(inv, (rows, 128))
        n2_all[z, x, i // 2, i % 2] = (hidden * inv * gain_row(1)).astype(bf16)

    n2_base = take(3)
    for i, (dz, dx) in enumerate(others):
        link(n2_all.at[z, x], n2_all.at[z, x], peer(0, dz, dx), sem=n2_base + i)

    pltpu.make_async_copy(wgu_all.at[slab()], wgu_all.at[slab()], own_gu_sem).wait()
    gu_cores = []
    for flips in ((0, 0, 0), (0, 0, 1), (0, 1, 0), (0, 1, 1), (1, 0, 0), (1, 0, 1), (1, 1, 0), (1, 1, 1)):
        ref = wgu_all.at[slab(*flips)]
        if flips != (0, 0, 0):
            pltpu.make_async_copy(ref, ref, rsem.at[gu_sems[flips]]).wait()
        gu_cores.append(link(ref, ref, peer(dc=1)))
    down_cross.wait_recv()
    far_down = wd_all.at[flip(s, 1), c]
    down_far_core = link(far_down, far_down, peer(dc=1))
    down_local.wait()
    down_own_core.wait_recv()
    down_far_core.wait_recv()
    for copy in gu_cores:
        copy.wait_recv()

    po_base = take(3)
    pg_base = take(3)

    @pl.loop(0, 4)
    def _(i):
        dz, dx = i // 2, i % 2
        cz, cx = flip(z, dz), flip(x, dx)
        chunk = n2_all.at[cz, cx]
        g_chunk = g_all.at[cz, cx]

        @pl.when(i > 0)
        def _():
            pltpu.make_async_copy(chunk, chunk, rsem.at[n2_base + i - 1]).wait()
            pltpu.make_async_copy(g_chunk, g_chunk, rsem.at[g_base + i - 1]).wait()

        @pl.loop(0, tiles)
        def _(t):
            first = pl.multiple_of(t * tile, tile)
            cols = pl.ds(first, tile)
            n2 = chunk[...].reshape(tokens, width)
            gate = dot(n2, wgu_all[:, :, :, :, :, cols].reshape(width, tile))
            up = dot(n2, wgu_all[:, :, :, :, :, pl.ds(block + first, tile)].reshape(width, tile))
            g_act = dot_nt(g_chunk[...].reshape(tokens, width), wd_all[t // 2, t % 2].reshape(tile, width))
            sig = 1.0 / (1.0 + jnp.exp(-gate))
            silu = gate * sig
            shape = (2, 2, rows, tile)
            act_all[cz, cx, :, :, :, cols] = (silu * up).astype(bf16).reshape(shape)
            g_gate = g_act * up * sig * (1.0 + gate * (1.0 - sig))
            ggu_all[cz, cx, :, :, :, cols] = g_gate.astype(bf16).reshape(shape)
            ggu_all[cz, cx, :, :, :, pl.ds(block + first, tile)] = (g_act * silu).astype(bf16).reshape(shape)

        @pl.loop(0, tiles)
        def _(t):
            cols = pl.ds(pl.multiple_of(t * tile, tile), tile)
            shape = (2, 2, rows, tile)
            g_n2 = dot_nt(
                ggu_all[cz, cx].reshape(tokens, 2 * block), wgu_all[t // 2, t % 2].reshape(tile, 2 * block)
            )
            pg_s[cz, cx, :, :, :, cols] = g_n2.astype(bf16).reshape(shape)

        @pl.when(i > 0)
        def _():
            link(pg_s.at[cz, cx], pg_r.at[i - 1], flip(s, 0) * 8 + cz * 4 + cx * 2 + c, sem=pg_base + i - 1)

        @pl.loop(0, tiles)
        def _(t):
            cols = pl.ds(pl.multiple_of(t * tile, tile), tile)
            shape = (2, 2, rows, tile)
            part = dot(act_all[cz, cx].reshape(tokens, block), wd_all[:, :, :, :, :, cols].reshape(block, tile))
            po_s[cz, cx, :, :, :, cols] = part.astype(bf16).reshape(shape)

        @pl.when(i > 0)
        def _():
            link(po_s.at[cz, cx], po_r.at[i - 1], flip(s, 0) * 8 + cz * 4 + cx * 2 + c, sem=po_base + i - 1)

    for copy in gu_cores + [down_own_core, down_far_core, down_cross]:
        copy.wait_send()
    for i, (dz, dx) in enumerate(others):
        pltpu.make_async_copy(n2_all.at[z, x], n2_all.at[z, x], ssem.at[n2_base + i]).wait()
        pltpu.make_async_copy(g_all.at[z, x], g_all.at[z, x], ssem.at[g_base + i]).wait()
    for flips in order:
        ref = wgu_all.at[slab(*flips)]
        pltpu.make_async_copy(ref, ref, ssem.at[gu_sems[flips]]).wait()

    gu_grad = wgu_all

    @pl.loop(0, tiles)
    def _(t):
        cols = pl.ds(pl.multiple_of(t * tile, tile), tile)
        left = n2_all[:, :, :, :, :, cols].reshape(4 * tokens, tile).T

        @pl.loop(0, 2 * block // (2 * tile))
        def _(n):
            wide = pl.ds(pl.multiple_of(n * 2 * tile, 2 * tile), 2 * tile)
            part = dot(left, ggu_all[:, :, :, :, :, wide].reshape(4 * tokens, 2 * tile))
            gu_grad[t // 2, t % 2, :, :, :, wide] = part.astype(bf16).reshape(2, 2, rows, 2 * tile)

    gu_swap = link(gu_grad.at[:, :, :, flip(c, 1)], gu_core, peer(dc=1))

    down_grad = wd_all

    @pl.loop(0, tiles)
    def _(t):
        cols = pl.ds(pl.multiple_of(t * tile, tile), tile)
        left = act_all[:, :, :, :, :, cols].reshape(4 * tokens, tile).T

        @pl.loop(0, width // (2 * tile))
        def _(n):
            wide = pl.ds(pl.multiple_of(n * 2 * tile, 2 * tile), 2 * tile)
            part = dot(left, g_all[:, :, :, :, :, wide].reshape(4 * tokens, 2 * tile))
            down_grad[t // 2, t % 2, :, :, :, wide] = part.astype(bf16).reshape(2, 2, rows, 2 * tile)

    down_swap = link(down_grad.at[:, flip(c, 1)], down_core, peer(dc=1))

    gu_swap.wait_recv()

    @pl.loop(0, 8)
    def _(m):
        at = (m // 4, (m // 2) % 2, m % 2)
        ref = gu_grad.at[at + (c,)]
        ref[...] = (ref[...].astype(f32) + gu_core[at].astype(f32)).astype(bf16)

    gu_sends = []
    for flips in order:
        gu_sends.append(link(gu_grad.at[slab(*flips)], gu_out.at[s, z, x], peer(*flips)))
    gu_keep = local(gu_grad.at[slab()], gu_out.at[s, z, x])

    down_swap.wait_recv()

    @pl.loop(0, 8)
    def _(m):
        at = (m // 4,)
        rest = ((m // 2) % 2, m % 2)
        ref = down_grad.at[at + (c,) + rest]
        ref[...] = (ref[...].astype(f32) + down_core[at + rest].astype(f32)).astype(bf16)

    down_send = link(down_grad.at[flip(s, 1), c], down_out.at[1], peer(ds=1))
    down_keep = local(down_grad.at[s, c], down_out.at[0])

    for i in range(3):
        pltpu.make_async_copy(pg_r.at[i], pg_r.at[i], rsem.at[pg_base + i]).wait()
    gsum_s[...] = jnp.zeros_like(gsum_s)

    def add_gain(which, value):
        for i in range(gsum_s.shape[0]):
            gsum_s[i, which : which + 1, :] += value[:, i * 128 : (i + 1) * 128]

    @pl.loop(0, steps)
    def _(i):
        part = pl.ds(i * rows, rows)
        at = (i // 2, i % 2)
        g_n2 = pg_s[(z, x) + at].astype(f32)
        for k in range(3):
            g_n2 += pg_r[(k,) + at].astype(f32)
        hidden = hmid[part]
        inv = r_two[part][:, :1]
        add_gain(1, jnp.sum(g_n2 * hidden * inv, axis=0, keepdims=True))
        scaled = g_n2 * gain_row(1)
        inner = jnp.mean(scaled * hidden, axis=-1, keepdims=True)
        g_sum = cot_ref[part].astype(f32) * mask_ref[part]
        g_mid = g_sum + inv * scaled - hidden * (inv * inv * inv * inner)
        gmid[part] = g_mid
        gattn[part] = g_mid.astype(bf16)

    def project_back(left, g, dest):
        @pl.loop(0, tiles)
        def _(t):
            cols = pl.ds(pl.multiple_of(t * tile, tile), tile)
            dest[:, cols] = dot_nt(left[...], wa[g, t // 2, t % 2].reshape(tile, width))

    g_mixed = ig_ref
    project_back(gattn, OUT, g_mixed)

    @pl.loop(0, steps)
    def _(i):
        part = pl.ds(i * rows, rows)
        gm = g_mixed[part]
        gv_s[part] = (head_spread(p_rem[part]) * gm).astype(bf16)

    gv_copy = link(gv_s, gv_r, f, to_y=1 - y)

    @pl.loop(0, steps)
    def _(i):
        part = pl.ds(i * rows, rows)
        gm = g_mixed[part]
        own, far = p_own[part], p_rem[part]
        gp_own = head_sum(gm * vb[part].astype(f32))
        gp_far = head_sum(gm * vrem[part].astype(f32))
        inner = own * gp_own + far * gp_far
        gs_own = head_spread(own * (gp_own - inner) * scale)
        gs_far = head_spread(far * (gp_far - inner) * scale)
        query = qb[part].astype(f32)
        gk_s[part] = (gs_far * query).astype(bf16)
        gq[part] = (gs_own * kb[part].astype(f32) + gs_far * krem[part].astype(f32)).astype(bf16)
        hold_k[part] = gs_own * query

    gk_copy = link(gk_s, gk_r, f, to_y=1 - y)

    stage = {
        OUT: (act_all, width),
        QUERY: (n2_all, width),
        VALUE: (g_all, width),
        KEY: (ggu_all, width),
    }
    legs = {}

    def grad_view(g, *at):
        ref = stage[g][0]
        if ref.shape[-1] != width:
            return ref.at[at + (slice(None),) * (5 - len(at)) + (pl.ds(0, width),)]
        return ref.at[at]

    def weight_grad(g, left, right):
        @pl.loop(0, tiles)
        def _(t):
            cols = pl.ds(pl.multiple_of(t * tile, tile), tile)
            part = dot(left[:, cols].T, right[...])
            grad_view(g, t // 2, t % 2)[...] = part.astype(bf16).reshape(2, 2, rows, width)

        every = slice(None)
        legs[g] = [link(grad_view(g, every, every, every, flip(c, 1)), attn_core.at[g], peer(dc=1))]

    def add_into(g, count, at_of, came):
        @pl.loop(0, count)
        def _(m):
            ref = grad_view(g, *at_of(m))
            ref[...] = (ref[...].astype(f32) + came(m)[...].astype(f32)).astype(bf16)

    def leg_x(g):
        legs[g][0].wait_recv()
        add_into(
            g, 8, lambda m: (m // 4, (m // 2) % 2, m % 2, c), lambda m: attn_core.at[g, m // 4, (m // 2) % 2, m % 2]
        )
        every = slice(None)
        legs[g].append(link(grad_view(g, every, every, flip(x, 1), c), attn_x.at[g], peer(dx=1)))

    def leg_z(g):
        legs[g][1].wait_recv()
        add_into(g, 4, lambda m: (m // 2, m % 2, x, c), lambda m: attn_x.at[g, m // 2, m % 2])
        every = slice(None)
        legs[g].append(link(grad_view(g, every, flip(z, 1), x, c), attn_z.at[g], peer(dz=1)))

    def leg_cross(g):
        legs[g][2].wait_recv()
        add_into(g, 2, lambda m: (m, z, x, c), lambda m: attn_z.at[g, m])
        legs[g].append(link(grad_view(g, flip(s, 1), z, x, c), attn_out.at[1, g], peer(ds=1)))
        legs[g].append(local(grad_view(g, s, z, x, c), attn_out.at[0, g]))

    weight_grad(OUT, mixed, gattn)
    weight_grad(QUERY, normed, gq)
    leg_x(OUT)
    leg_x(QUERY)
    gv_copy.wait_recv()

    @pl.loop(0, steps)
    def _(i):
        part = pl.ds(i * rows, rows)
        own = head_spread(p_own[part]) * g_mixed[part]
        gv[part] = (own + gv_r[part].astype(f32)).astype(bf16)

    weight_grad(VALUE, normed, gv)
    leg_x(VALUE)
    gk_copy.wait_recv()

    @pl.loop(0, steps)
    def _(i):
        part = pl.ds(i * rows, rows)
        gk[part] = (hold_k[part] + gk_r[part].astype(f32)).astype(bf16)

    weight_grad(KEY, normed, gk)
    leg_z(OUT)
    leg_x(KEY)
    leg_z(QUERY)
    leg_cross(OUT)

    @pl.loop(0, tiles)
    def _(t):
        cols = pl.ds(pl.multiple_of(t * tile, tile), tile)
        at = (t // 2, t % 2)
        ig_ref[:, cols] = (
            dot_nt(gq[...], wa[(QUERY,) + at].reshape(tile, width))
            + dot_nt(gk[...], wa[(KEY,) + at].reshape(tile, width))
            + dot_nt(gv[...], wa[(VALUE,) + at].reshape(tile, width))
        )

    @pl.loop(0, steps)
    def _(i):
        part = pl.ds(i * rows, rows)
        hidden = x_ref[part].astype(f32)
        inv = r_one[part][:, :1]
        g_n1 = ig_ref[part]
        add_gain(0, jnp.sum(g_n1 * hidden * inv, axis=0, keepdims=True))
        scaled = g_n1 * gain_row(0)
        inner = jnp.mean(scaled * hidden, axis=-1, keepdims=True)
        ig_ref[part] = gmid[part] + inv * scaled - hidden * (inv * inv * inv * inner)

    def gain_sum_copy(r):
        to = lax.rem(f + r, 16)
        return pltpu.make_async_remote_copy(
            src_ref=gsum_s.at[to // per_block], dst_ref=gsum_r.at[r - 1],
            send_sem=hsem_s.at[r - 1], recv_sem=hsem_r.at[r - 1],
            device_id=(to, y), device_id_type=MESH,
        )

    @pl.loop(1, 16)
    def _(r):
        gain_sum_copy(r).start()

    leg_z(VALUE)
    leg_cross(QUERY)
    leg_z(KEY)
    leg_cross(VALUE)

    for i in range(3):
        pltpu.make_async_copy(po_r.at[i], po_r.at[i], rsem.at[po_base + i]).wait()

    @pl.loop(0, steps)
    def _(i):
        part = pl.ds(i * rows, rows)
        at = (i // 2, i % 2)
        total = po_s[(z, x) + at].astype(f32)
        for k in range(3):
            total += po_r[(k,) + at].astype(f32)
        out_ref[part] = (mask_ref[part] * (hmid[part] + total)).astype(bf16)

    leg_cross(KEY)
    gain_out[...] = gsum_s[f // per_block]

    @pl.loop(1, 16)
    def _(r):
        gain_sum_copy(r).wait()
        gain_out[...] += gsum_r[r - 1]

    for copy in keep + [k_copy, v_copy, gv_copy, gk_copy, gu_swap, down_swap]:
        copy.wait_send()
    for i in range(3):
        pltpu.make_async_copy(po_r.at[i], po_r.at[i], ssem.at[po_base + i]).wait()
        pltpu.make_async_copy(pg_r.at[i], pg_r.at[i], ssem.at[pg_base + i]).wait()
    for copy in gu_sends + [down_send]:
        copy.wait()
    gu_keep.wait()
    down_keep.wait()
    for g in (OUT, QUERY, VALUE, KEY):
        for copy in legs[g][:3]:
            copy.wait_send()
        legs[g][3].wait()
        legs[g][4].wait()


def square_layer(inputs, frame_flags, attn_gain, qkv_weight, out_weight, ffn_gain, gate_up_weight, down_weight, cotangent):
    tokens, _, width = inputs.shape
    rows = qkv_weight.shape[2]
    block = width
    f32, bf16 = jnp.float32, jnp.bfloat16
    lane_block = 128
    per_block = lane_block // rows
    f = lax.axis_index("fsdp")
    lane_blocks = width // lane_block
    gains = jnp.concatenate([attn_gain[0], ffn_gain[0]], axis=0)
    gains = jnp.concatenate([jnp.where(f % per_block == b, gains, 0) for b in range(per_block)], axis=1).astype(bf16)
    gains = jnp.pad(gains, ((0, 14), (0, 0)))
    mask = frame_flags.astype(f32)[:, None]
    vmem = pl.BlockSpec(memory_space=pltpu.VMEM)
    anywhere = pl.BlockSpec(memory_space=pl.ANY)
    unit = (2, 2, 2, 2, rows, width)
    double = (2, 2, 2, 2, rows, 2 * block)
    own = (tokens, width)
    scratch = [
        pltpu.VMEM((4,) + unit, bf16),
        pltpu.VMEM(double, bf16),
        pltpu.VMEM(unit, bf16),
        pltpu.VMEM(unit, bf16),
        pltpu.VMEM(unit, bf16),
        pltpu.VMEM(unit, bf16),
        pltpu.VMEM(double, bf16),
        pltpu.VMEM(unit, bf16),
        pltpu.VMEM((3, 2, 2, rows, width), bf16),
        pltpu.VMEM(unit, bf16),
        pltpu.VMEM((3, 2, 2, rows, width), bf16),
        pltpu.VMEM((2, 2, 2, rows, 2 * block), bf16),
        pltpu.VMEM((2, 2, 2, rows, width), bf16),
        pltpu.VMEM((4, 2, 2, 2, rows, width), bf16),
        pltpu.VMEM((4, 2, 2, rows, width), bf16),
        pltpu.VMEM((4, 2, rows, width), bf16),
        pltpu.VMEM(own, bf16),
        pltpu.VMEM(own, bf16),
        pltpu.VMEM(own, bf16),
        pltpu.VMEM(own, bf16),
        pltpu.VMEM(own, bf16),
        pltpu.VMEM(own, bf16),
        pltpu.VMEM(own, bf16),
        pltpu.VMEM(own, f32),
        pltpu.VMEM(own, bf16),
        pltpu.VMEM(own, bf16),
        pltpu.VMEM(own, bf16),
        pltpu.VMEM(own, bf16),
        pltpu.VMEM(own, bf16),
        pltpu.VMEM(own, bf16),
        pltpu.VMEM(own, bf16),
        pltpu.VMEM(own, f32),
        pltpu.VMEM(own, bf16),
        pltpu.VMEM(own, f32),
        pltpu.VMEM((tokens, 128), f32),
        pltpu.VMEM((tokens, 128), f32),
        pltpu.VMEM((tokens, 128), f32),
        pltpu.VMEM((tokens, 128), f32),
        pltpu.VMEM((15, 16, lane_block), bf16),
        pltpu.VMEM((lane_blocks, 16, lane_block), f32),
        pltpu.VMEM((lane_blocks, 8, lane_block), f32),
        pltpu.VMEM((15, 8, lane_block), f32),
        pltpu.VMEM((width, 128), bf16),
        pltpu.VMEM((128, width), bf16),
        pltpu.SemaphoreType.DMA((SEMS,)),
        pltpu.SemaphoreType.DMA((SEMS,)),
        pltpu.SemaphoreType.DMA((16,)),
        pltpu.SemaphoreType.DMA((15,)),
        pltpu.SemaphoreType.DMA((15,)),
        pltpu.SemaphoreType.DMA((15,)),
        pltpu.SemaphoreType.DMA((15,)),
    ]
    outs = pl.pallas_call(
        square_kernel,
        out_shape=(
            jax.ShapeDtypeStruct(own, bf16),
            jax.ShapeDtypeStruct(own, f32),
            jax.ShapeDtypeStruct((8, lane_block), f32),
            jax.ShapeDtypeStruct((2, 2, 2, rows, 2 * block), bf16),
            jax.ShapeDtypeStruct((2, 2, 2, rows, width), bf16),
            jax.ShapeDtypeStruct((2, 4, rows, width), bf16),
        ),
        in_specs=[vmem] * 4 + [anywhere] * 4,
        out_specs=(vmem, vmem, vmem, anywhere, anywhere, anywhere),
        scratch_shapes=scratch,
        compiler_params=pltpu.CompilerParams(
            collective_id=0, has_side_effects=True, vmem_limit_bytes=VMEM_BYTES
        ),
        cost_estimate=pl.CostEstimate(flops=26 * 10**9, bytes_accessed=2**23, transcendentals=2**21),
    )(
        inputs[:, 0], cotangent[:, 0], mask, gains,
        qkv_weight[0, 0], out_weight[0, 0], gate_up_weight[0, 0], down_weight[0, 0].reshape(2, 2, rows, width),
    )
    result, input_grad, gain_sums, gu, down, attn = outs
    gain_sums = sum(
        jnp.where(f % per_block == b, gain_sums[:2, b * rows : (b + 1) * rows], 0.0) for b in range(per_block)
    )
    gu = gu.astype(f32)
    gu = (gu[0] + gu[1]).reshape(4, rows, 2, 2, block // 2).transpose(1, 2, 3, 0, 4).reshape(1, 1, rows, 8 * block)
    down = (down[0].astype(f32) + down[1].astype(f32)).reshape(down_weight.shape)
    attn = attn[0].astype(f32) + attn[1].astype(f32)
    qkv = jnp.concatenate([attn[QUERY], attn[KEY], attn[VALUE]], axis=1)[None, None]
    return (
        result[:, None],
        input_grad[:, None],
        gain_sums[0:1, None],
        qkv,
        attn[OUT][None, None],
        gain_sums[1:2, None],
        gu,
        down,
    )


VMEM_BYTES = 62 * 2**20


def run_layer(axes, *args):
    inputs, qkv_weight, down_weight = args[0], args[3], args[7]
    tokens, places, width = inputs.shape
    rows = qkv_weight.shape[2]
    square = (
        axes["fsdp"] == 16
        and axes["pos"] == 2
        and places == 1
        and qkv_weight.shape[0] == 1
        and tokens == 4 * rows
        and down_weight.shape[2] == 4 * rows
        and 128 % rows == 0
    )
    return square_layer(*args) if square else on_device(*args)


def solution(mesh):
    in_specs = (
        P("fsdp", "pos", None),
        P("fsdp"),
        P(None, "pos", "fsdp"),
        P(None, "pos", "fsdp", None),
        P(None, "pos", "fsdp", None),
        P(None, "pos", "fsdp"),
        P(None, "pos", "fsdp", None),
        P(None, "pos", "fsdp", None),
        P("fsdp", "pos", None),
    )
    out_specs = (
        P("fsdp", "pos", None),
        P("fsdp", "pos", None),
        P(None, "pos", "fsdp"),
        P(None, "pos", "fsdp", None),
        P(None, "pos", "fsdp", None),
        P(None, "pos", "fsdp"),
        P(None, "pos", "fsdp", None),
        P(None, "pos", "fsdp", None),
    )
    return jax.shard_map(
        functools.partial(run_layer, dict(mesh.shape)), mesh=mesh, in_specs=in_specs, out_specs=out_specs, check_vma=False
    )
```

```python
import functools
import math

import jax
import jax.numpy as jnp
from jax import lax
from jax.experimental import pallas as pl
from jax.experimental.pallas import tpu as pltpu
from jax.sharding import PartitionSpec as P

D = 1024
HEADS = 16
HEAD_DIM = 64
FF = 4096


EPSILON = 1e-06
MASKED = -1e30
PRECISE = lax.Precision.HIGHEST


def rms_parts(hidden, gain_row):
    inv_rms = lax.rsqrt(jnp.mean(hidden * hidden, axis=-1, keepdims=True) + EPSILON)
    return (hidden * inv_rms * gain_row[None], inv_rms)


def rms_back(grad_rows, hidden, inv_rms, gain_row):
    scaled = grad_rows * gain_row[None]
    gain_grad = jnp.sum(grad_rows * hidden * inv_rms, axis=0)
    inner_mean = jnp.mean(scaled * hidden, axis=-1, keepdims=True)
    return (inv_rms * scaled - hidden * inv_rms**3 * inner_mean, gain_grad)


def apply_rows(left_side, weight):
    return jnp.einsum("fpd,pde->fpe", left_side, weight, preferred_element_type=jnp.float32)


def apply_back(grad_rows, weight):
    return jnp.einsum("fpe,pde->fpd", grad_rows, weight, preferred_element_type=jnp.float32)


def outer_sum(left_side, grad_rows):
    return jnp.einsum("fpd,fpe->pde", left_side, grad_rows, preferred_element_type=jnp.float32)


def split_heads(rows):
    return rows.reshape(rows.shape[0], rows.shape[1], HEADS, HEAD_DIM)


def attention_weights(attn_gain, qkv_weight, out_weight, layer_idx):
    return (
        lax.all_gather(attn_gain[layer_idx], "fsdp", axis=1, tiled=True),
        lax.all_gather(qkv_weight[layer_idx], "fsdp", axis=1, tiled=True),
        lax.all_gather(out_weight[layer_idx], "fsdp", axis=1, tiled=True),
    )


def ffn_weights(ffn_gain, gate_up_weight, down_weight, layer_idx):
    return (
        lax.all_gather(ffn_gain[layer_idx], "fsdp", axis=1, tiled=True),
        lax.all_gather(gate_up_weight[layer_idx], "fsdp", axis=1, tiled=True),
        lax.all_gather(down_weight[layer_idx], "fsdp", axis=1, tiled=True),
    )


def attention_forward(qkv_rows):
    frames, places = (qkv_rows.shape[0], qkv_rows.shape[1])
    pos_count = lax.axis_size("pos")
    frame_part = frames // pos_count
    outgoing = qkv_rows.reshape(pos_count, frame_part, places, 3 * D)
    frame_qkv = lax.all_to_all(outgoing, "pos", split_axis=0, concat_axis=2, tiled=True)[0].astype(
        jnp.float32
    )
    whole_places = frame_qkv.shape[1]
    queries = split_heads(frame_qkv[..., :D])
    keys_all = split_heads(frame_qkv[..., D : 2 * D])
    values_all = split_heads(frame_qkv[..., 2 * D :])
    scores = jnp.einsum("fphe,fjhe->fhpj", queries, keys_all, precision=PRECISE) / math.sqrt(
        HEAD_DIM
    )
    causal = jnp.arange(whole_places)[:, None] >= jnp.arange(whole_places)[None, :]
    scores = jnp.where(causal, scores, MASKED)
    row_max = jnp.max(scores, axis=-1, keepdims=True)
    exponent = jnp.exp(scores - row_max)
    attn_probs = exponent / jnp.sum(exponent, axis=-1, keepdims=True)
    mixed_heads = jnp.einsum("fhpj,fjhe->fphe", attn_probs, values_all, precision=PRECISE)
    mixed_frames = mixed_heads.reshape(frame_part, whole_places, D).astype(jnp.bfloat16)
    returned = lax.all_to_all(mixed_frames[None], "pos", split_axis=2, concat_axis=0, tiled=True)
    return (returned.reshape(frames, places, D), (queries, keys_all, values_all, attn_probs))


def attention_backward(grad_mixed, attn_keep):
    queries, keys_all, values_all, attn_probs = attn_keep
    frames, places = (grad_mixed.shape[0], grad_mixed.shape[1])
    pos_count = lax.axis_size("pos")
    frame_part = frames // pos_count
    outgoing = grad_mixed.reshape(pos_count, frame_part, places, D)
    grad_frames = lax.all_to_all(
        outgoing.astype(jnp.bfloat16), "pos", split_axis=0, concat_axis=2, tiled=True
    ).astype(outgoing.dtype)[0]
    whole_places = grad_frames.shape[1]
    grad_heads = split_heads(grad_frames)
    grad_values = jnp.einsum("fhpj,fphe->fjhe", attn_probs, grad_heads, precision=PRECISE)
    grad_probs = jnp.einsum("fphe,fjhe->fhpj", grad_heads, values_all, precision=PRECISE)
    grad_scores = (
        attn_probs
        * (grad_probs - jnp.sum(attn_probs * grad_probs, axis=-1, keepdims=True))
        / math.sqrt(HEAD_DIM)
    )
    grad_queries = jnp.einsum("fhpj,fjhe->fphe", grad_scores, keys_all, precision=PRECISE)
    grad_keys = jnp.einsum("fhpj,fphe->fjhe", grad_scores, queries, precision=PRECISE)
    frame_grads = jnp.concatenate(
        [
            grad_queries.reshape(frame_part, whole_places, D),
            grad_keys.reshape(frame_part, whole_places, D),
            grad_values.reshape(frame_part, whole_places, D),
        ],
        axis=-1,
    ).astype(jnp.bfloat16)
    returned = lax.all_to_all(frame_grads[None], "pos", split_axis=2, concat_axis=0, tiled=True)
    return returned.reshape(frames, places, 3 * D)


def layer_forward(hidden, frame_mask, attn_set, ffn_set):
    gain_one, qkv_full, out_full = attn_set
    gain_two, gate_up_full, down_full = ffn_set
    normed, inv_one = rms_parts(hidden, gain_one.astype(jnp.float32))
    normed_low = normed.astype(jnp.bfloat16)
    qkv_rows = apply_rows(normed_low, qkv_full).astype(jnp.bfloat16)
    mixed_low, attn_keep = attention_forward(qkv_rows)
    hidden_mid = hidden + apply_rows(mixed_low, out_full)
    normed_two, inv_two = rms_parts(hidden_mid, gain_two.astype(jnp.float32))
    normed_two_low = normed_two.astype(jnp.bfloat16)
    gate_up = apply_rows(normed_two_low, gate_up_full)
    gate_part = gate_up[..., :FF]
    up_part = gate_up[..., FF:]
    act_low = (jax.nn.silu(gate_part) * up_part).astype(jnp.bfloat16)
    result = frame_mask * (hidden_mid + apply_rows(act_low, down_full))
    kept_state = (
        hidden,
        inv_one,
        normed_low,
        attn_keep,
        mixed_low,
        hidden_mid,
        inv_two,
        normed_two_low,
        gate_part,
        up_part,
        act_low,
    )
    return (result, kept_state)


def layer_backward(grad_out, frame_mask, kept_state, ffn_set, fetch_attn):
    (
        hidden,
        inv_one,
        normed_low,
        attn_keep,
        mixed_low,
        hidden_mid,
        inv_two,
        normed_two_low,
        gate_part,
        up_part,
        act_low,
    ) = kept_state
    gain_two, gate_up_full, down_full = ffn_set
    grad_sum = frame_mask * grad_out
    grad_ffn = grad_sum.astype(jnp.bfloat16)
    down_grad = outer_sum(act_low, grad_ffn)
    down_shard = lax.psum_scatter(down_grad, "fsdp", scatter_dimension=1, tiled=True)
    grad_act = apply_back(grad_ffn, down_full)
    sigmoid_gate = jax.nn.sigmoid(gate_part)
    grad_gate = grad_act * up_part * sigmoid_gate * (1.0 + gate_part * (1.0 - sigmoid_gate))
    grad_up = grad_act * gate_part * sigmoid_gate
    grad_gu = jnp.concatenate([grad_gate, grad_up], axis=-1).astype(jnp.bfloat16)
    gate_up_grad = outer_sum(normed_two_low, grad_gu)
    grad_norm_two = apply_back(grad_gu, gate_up_full)
    grad_mid_norm, gain_two_grad = rms_back(
        grad_norm_two, hidden_mid, inv_two, gain_two.astype(jnp.float32)
    )
    ffn_shards = (
        lax.psum_scatter(gain_two_grad, "fsdp", scatter_dimension=1, tiled=True),
        lax.psum_scatter(gate_up_grad, "fsdp", scatter_dimension=1, tiled=True),
    )
    gain_one, qkv_full, out_full = fetch_attn()
    grad_mid = grad_sum + grad_mid_norm
    grad_attn = grad_mid.astype(jnp.bfloat16)
    out_grad = outer_sum(mixed_low, grad_attn)
    grad_mixed = apply_back(grad_attn, out_full)
    grad_qkv = attention_backward(grad_mixed, attn_keep)
    qkv_grad = outer_sum(normed_low, grad_qkv)
    grad_norm_one = apply_back(grad_qkv, qkv_full)
    grad_in_norm, gain_one_grad = rms_back(
        grad_norm_one, hidden, inv_one, gain_one.astype(jnp.float32)
    )
    attn_shards = (
        lax.psum_scatter(gain_one_grad, "fsdp", scatter_dimension=1, tiled=True),
        lax.psum_scatter(qkv_grad, "fsdp", scatter_dimension=1, tiled=True),
        lax.psum_scatter(out_grad, "fsdp", scatter_dimension=1, tiled=True),
    )
    grad_in = grad_mid + grad_in_norm
    return (
        grad_in,
        (attn_shards[0], attn_shards[1], attn_shards[2], ffn_shards[0], ffn_shards[1], down_shard),
    )


def on_device(
    inputs,
    frame_flags,
    attn_gain,
    qkv_weight,
    out_weight,
    ffn_gain,
    gate_up_weight,
    down_weight,
    cotangent,
):
    layer_total = qkv_weight.shape[0]
    frame_mask = frame_flags.astype(jnp.float32)[:, None, None]
    hidden = inputs.astype(jnp.float32)
    layer_idx = 0
    attn_set = attention_weights(attn_gain, qkv_weight, out_weight, layer_idx)
    ffn_set = ffn_weights(ffn_gain, gate_up_weight, down_weight, layer_idx)
    hidden, kept_state = layer_forward(hidden, frame_mask, attn_set, ffn_set)
    states_all = [kept_state]
    grad_rows = cotangent.astype(jnp.float32)
    layer_grads = [None] * layer_total
    for layer_idx in reversed(range(layer_total)):
        ffn_set = ffn_weights(ffn_gain, gate_up_weight, down_weight, layer_idx)
        fetch_attn = gather_later(attn_gain, qkv_weight, out_weight, layer_idx)
        grad_rows, layer_grads[layer_idx] = layer_backward(
            grad_rows, frame_mask, states_all[layer_idx], ffn_set, fetch_attn
        )
    stacked = [jnp.stack([grad_set[column] for grad_set in layer_grads]) for column in range(6)]
    return (
        hidden.astype(jnp.bfloat16),
        grad_rows,
        stacked[0],
        stacked[1],
        stacked[2],
        stacked[3],
        stacked[4],
        stacked[5],
    )


def gather_later(attn_gain, qkv_weight, out_weight, layer_idx):

    def fetched():
        return attention_weights(attn_gain, qkv_weight, out_weight, layer_idx)

    return fetched


KEY, VALUE, QUERY, OUT = 0, 1, 2, 3
SEMS = 128
MESH = pl.DeviceIdType.MESH


def flip(bit, change):
    return bit + change - 2 * bit * change


def square_kernel(
    x_ref, cot_ref, mask_ref, gain_ref, wqkv, wout, wgu, wd,
    out_ref, ig_ref, gain_out, gu_out, down_out, attn_out,
    wa, wgu_all, wd_all, n2_all, g_all, act_all, ggu_all,
    po_s, po_r, pg_s, pg_r, gu_core, down_core, attn_core, attn_x, attn_z,
    normed, qb, kb, vb, krem, vrem, mixed, hmid, gv_s, gk_s, gv_r, gk_r,
    gq, gk, gv, gmid, gattn, hold_k, p_own, p_rem, r_one, r_two,
    gain_r, gain_f, gsum_s, gsum_r, ends, ends_t,
    ssem, rsem, lsem, gsem_s, gsem_r, hsem_s, hsem_r,
):
    tokens, width = x_ref.shape
    rows = width // 16
    block = 4 * width // 4
    half = block // 2
    ff = 4 * width
    f = lax.axis_index("fsdp")
    y = lax.axis_index("pos")
    c = f % 2
    x = (f // 2) % 2
    z = (f // 4) % 2
    s = f // 8
    f32, bf16 = jnp.float32, jnp.bfloat16

    def peer(ds=0, dz=0, dx=0, dc=0):
        return flip(s, ds) * 8 + flip(z, dz) * 4 + flip(x, dx) * 2 + flip(c, dc)

    def slab(ds=0, dz=0, dx=0, dc=0):
        return flip(s, ds), flip(z, dz), flip(x, dx), flip(c, dc)

    counter = [0]
    pending = []

    def take(n=1):
        counter[0] += n
        assert counter[0] <= SEMS
        return counter[0] - n

    def link(src, dst, to, sem=None, to_y=None):
        if sem is None:
            sem = take()
        copy = pltpu.make_async_remote_copy(
            src_ref=src, dst_ref=dst, send_sem=ssem.at[sem], recv_sem=rsem.at[sem],
            device_id=(to, y if to_y is None else to_y), device_id_type=MESH,
        )
        copy.start()
        return copy

    lcount = [0]

    def local(src, dst):
        lcount[0] += 1
        copy = pltpu.make_async_copy(src, dst, lsem.at[lcount[0] - 1])
        copy.start()
        return copy

    def dot(a, b):
        return jnp.dot(a, b, preferred_element_type=f32)

    def dot_nt(a, b):
        return lax.dot_general(a, b, (((1,), (1,)), ((), ())), preferred_element_type=f32)

    def split(v):
        high = v.astype(bf16)
        return high, (v - high.astype(f32)).astype(bf16)

    def head_sum(v):
        high, low = split(v)
        return dot(high, ends[...]) + dot(low, ends[...])

    def head_spread(p):
        high, low = split(p)
        return dot(high, ends_t[...]) + dot(low, ends_t[...])

    barrier = pltpu.get_barrier_semaphore()

    @pl.loop(1, 16)
    def _(r):
        pl.semaphore_signal(barrier, inc=1, device_id=(lax.rem(f + r, 16), y), device_id_type=MESH)

    pl.semaphore_signal(barrier, inc=1, device_id=(f, 1 - y), device_id_type=MESH)
    pl.semaphore_wait(barrier, 16)

    def gain_copy(r):
        return pltpu.make_async_remote_copy(
            src_ref=gain_ref, dst_ref=gain_r.at[r - 1], send_sem=gsem_s.at[r - 1], recv_sem=gsem_r.at[r - 1],
            device_id=(lax.rem(f + r, 16), y), device_id_type=MESH,
        )

    @pl.loop(1, 16)
    def _(r):
        gain_copy(r).start()

    own_cols = (
        wqkv.at[:, pl.ds(width, width)],
        wqkv.at[:, pl.ds(2 * width, width)],
        wqkv.at[:, pl.ds(0, width)],
        wout,
    )
    keep = []
    legs_in = {g: {} for g in range(4)}

    def own_send(g, *ways):
        own = wa.at[(g,) + slab()]
        src = own_cols[g]
        flips = {"s": (1, 0, 0, 0), "z": (0, 1, 0, 0), "x": (0, 0, 1, 0), "c": (0, 0, 0, 1)}
        for way in ways:
            copy = link(src, own, peer(*flips[way]))
            keep.append(copy)
            legs_in[g][way] = copy
        if "c" in ways:
            legs_in[g]["own"] = local(src, own)
            legs_in[g]["cores"] = []

    def forward(g, at, to):
        ref = wa.at[(g,) + slab(*at)]
        copy = link(ref, ref, to)
        keep.append(copy)
        return copy

    def to_core(g, at):
        legs_in[g]["cores"].append(forward(g, at, peer(dc=1)))

    def from_cross(g):
        leg = legs_in[g]
        leg["s"].wait_recv()
        leg["sz"] = forward(g, (1, 0, 0, 0), peer(dz=1))
        leg["sx"] = forward(g, (1, 0, 0, 0), peer(dx=1))
        to_core(g, (1, 0, 0, 0))

    def from_z(g):
        leg = legs_in[g]
        leg["z"].wait_recv()
        leg["zx"] = forward(g, (0, 1, 0, 0), peer(dx=1))
        to_core(g, (0, 1, 0, 0))

    def from_cross_z(g):
        leg = legs_in[g]
        leg["sz"].wait_recv()
        leg["szx"] = forward(g, (1, 1, 0, 0), peer(dx=1))
        to_core(g, (1, 1, 0, 0))

    def from_x(g):
        leg = legs_in[g]
        for name, at in (("x", (0, 0, 1, 0)), ("sx", (1, 0, 1, 0)), ("zx", (0, 1, 1, 0)), ("szx", (1, 1, 1, 0))):
            leg[name].wait_recv()
            to_core(g, at)

    def from_core(g):
        leg = legs_in[g]
        leg["own"].wait()
        leg["c"].wait_recv()
        for copy in leg["cores"]:
            copy.wait_recv()

    gu_sems = {}

    def gu_pieces(flips):
        ds, dz, dx = flips
        j = flip(z, dz) * 2 + flip(x, dx)
        for u in range(2):
            for part in range(2):
                src = wgu.at[:, pl.ds(pl.multiple_of(u * ff + part * (ff // 2) + j * half, half), half)]
                dst = wgu_all.at[s, z, x, c, :, pl.ds(u * block + part * half, half)]
                yield src, dst

    order = ((1, 0, 0), (1, 0, 1), (1, 1, 0), (1, 1, 1), (0, 0, 1), (0, 1, 0), (0, 1, 1))

    def gu_send(k):
        sem = take()
        gu_sems[order[k]] = sem
        for src, dst in gu_pieces(order[k]):
            link(src, dst, peer(*order[k]), sem=sem)

    own_send(KEY, "s", "z", "x", "c")
    own_send(VALUE, "s", "z", "x", "c")
    own_send(QUERY, "x")

    ends[...] = (
        lax.broadcasted_iota(jnp.int32, ends.shape, 0) // HEAD_DIM == lax.broadcasted_iota(jnp.int32, ends.shape, 1)
    ).astype(bf16)
    ends_t[...] = (
        lax.broadcasted_iota(jnp.int32, ends_t.shape, 1) // HEAD_DIM == lax.broadcasted_iota(jnp.int32, ends_t.shape, 0)
    ).astype(bf16)

    g_all[z, x] = (cot_ref[...].astype(f32) * mask_ref[...]).astype(bf16).reshape(2, 2, rows, width)

    g_z = link(g_all.at[z, x], g_all.at[z, x], peer(dz=1))
    g_x = link(g_all.at[z, x], g_all.at[z, x], peer(dx=1))

    gain_f[...] = jnp.zeros_like(gain_f)
    lane_block = 128
    per_block = lane_block // rows
    gain_f[f // per_block] += gain_ref[...].astype(f32)

    @pl.loop(1, 16)
    def _(r):
        gain_copy(r).wait()
        gain_f[lax.rem(f + 16 - r, 16) // per_block] += gain_r[r - 1].astype(f32)

    def gain_row(which):
        return jnp.concatenate([gain_f[i, which : which + 1, :] for i in range(gain_f.shape[0])], axis=1)

    steps = tokens // rows

    @pl.loop(0, steps)
    def _(i):
        part = pl.ds(i * rows, rows)
        hidden = x_ref[part].astype(f32)
        inv = lax.rsqrt(jnp.mean(hidden * hidden, axis=-1, keepdims=True) + EPSILON)
        r_one[part] = jnp.broadcast_to(inv, (rows, 128))
        normed[part] = (hidden * inv * gain_row(0)).astype(bf16)

    tile = 256 if width >= 256 else width
    tiles = width // tile
    quarter = width // 4

    def project(left, g, dest):
        @pl.loop(0, tiles)
        def _(t):
            cols = pl.ds(pl.multiple_of(t * tile, tile), tile)
            dest[:, cols] = dot(left[...], wa[g, :, :, :, :, :, cols].reshape(width, tile)).astype(dest.dtype)

    from_cross(KEY)
    from_z(KEY)
    own_send(QUERY, "s", "z", "c")
    from_cross(VALUE)
    from_cross_z(KEY)
    from_z(VALUE)
    gu_send(0)
    own_send(OUT, "x", "s", "z", "c")
    from_cross(QUERY)
    from_x(KEY)
    from_cross_z(VALUE)
    from_z(QUERY)
    from_core(KEY)
    project(normed, KEY, kb)
    k_copy = link(kb, krem, f, to_y=1 - y)
    gu_send(1)
    from_x(VALUE)
    from_cross_z(QUERY)
    from_cross(OUT)
    from_z(OUT)
    from_core(VALUE)
    project(normed, VALUE, vb)
    v_copy = link(vb, vrem, f, to_y=1 - y)
    gu_send(2)
    from_cross_z(OUT)
    gu_send(3)
    gu_send(6)
    gu_send(5)
    gu_send(4)
    own_gu_sem = lsem.at[lcount[0]]
    lcount[0] += 1
    for src, dst in gu_pieces((0, 0, 0)):
        pltpu.make_async_copy(src, dst, own_gu_sem).start()

    own_down = wd_all.at[s, c]
    down_cross = link(wd, own_down, peer(ds=1))
    down_own_core = link(wd, own_down, peer(dc=1))
    down_local = local(wd, own_down)

    from_x(QUERY)
    g_z.wait_recv()
    g_zx = link(g_all.at[flip(z, 1), x], g_all.at[flip(z, 1), x], peer(dx=1))
    from_core(QUERY)
    project(normed, QUERY, qb)
    from_x(OUT)
    from_core(OUT)

    k_copy.wait_recv()
    v_copy.wait_recv()
    scale = 1.0 / math.sqrt(HEAD_DIM)

    @pl.loop(0, steps)
    def _(i):
        part = pl.ds(i * rows, rows)
        query = qb[part].astype(f32)
        own = head_sum(query * kb[part].astype(f32)) * scale
        far = jnp.where(y > 0, head_sum(query * krem[part].astype(f32)) * scale, MASKED)
        top = jnp.maximum(own, far)
        own = jnp.exp(own - top)
        far = jnp.exp(far - top)
        total = own + far
        own = own / total
        far = far / total
        p_own[part] = own
        p_rem[part] = far
        mixed[part] = (head_spread(own) * vb[part].astype(f32) + head_spread(far) * vrem[part].astype(f32)).astype(bf16)

    project(mixed, OUT, hmid)

    @pl.loop(0, steps)
    def _(i):
        part = pl.ds(i * rows, rows)
        hidden = x_ref[part].astype(f32) + hmid[part]
        hmid[part] = hidden
        inv = lax.rsqrt(jnp.mean(hidden * hidden, axis=-1, keepdims=True) + EPSILON)
        r_two[part] = jnp.broadcast_to(inv, (rows, 128))
        n2_all[z, x, i // 2, i % 2] = (hidden * inv * gain_row(1)).astype(bf16)

    n2_z = link(n2_all.at[z, x], n2_all.at[z, x], peer(dz=1))
    n2_x = link(n2_all.at[z, x], n2_all.at[z, x], peer(dx=1))
    n2_zx_sem = take()
    g_x.wait_recv()
    g_zx.wait_recv()

    pltpu.make_async_copy(wgu_all.at[slab()], wgu_all.at[slab()], own_gu_sem).wait()
    gu_cores = []
    for flips in ((0, 0, 0), (0, 0, 1), (0, 1, 0), (0, 1, 1), (1, 0, 0), (1, 0, 1), (1, 1, 0), (1, 1, 1)):
        ref = wgu_all.at[slab(*flips)]
        if flips != (0, 0, 0):
            pltpu.make_async_copy(ref, ref, rsem.at[gu_sems[flips]]).wait()
        gu_cores.append(link(ref, ref, peer(dc=1)))
    down_cross.wait_recv()
    far_down = wd_all.at[flip(s, 1), c]
    down_far_core = link(far_down, far_down, peer(dc=1))
    down_local.wait()
    down_own_core.wait_recv()
    down_far_core.wait_recv()
    for copy in gu_cores:
        copy.wait_recv()

    po_base = take(3)
    pg_base = take(3)

    @pl.loop(0, 4)
    def _(i):
        dz, dx = i // 2, i % 2
        cz, cx = flip(z, dz), flip(x, dx)
        chunk = n2_all.at[cz, cx]
        g_chunk = g_all.at[cz, cx]

        @pl.when(i == 1)
        def _():
            n2_x.wait_recv()
            n2_z.wait_recv()
            link(n2_all.at[flip(z, 1), x], n2_all.at[flip(z, 1), x], peer(dx=1), sem=n2_zx_sem)

        @pl.when(i == 3)
        def _():
            pltpu.make_async_copy(chunk, chunk, rsem.at[n2_zx_sem]).wait()

        @pl.loop(0, tiles)
        def _(t):
            first = pl.multiple_of(t * tile, tile)
            cols = pl.ds(first, tile)
            n2 = chunk[...].reshape(tokens, width)
            gate = dot(n2, wgu_all[:, :, :, :, :, cols].reshape(width, tile))
            up = dot(n2, wgu_all[:, :, :, :, :, pl.ds(block + first, tile)].reshape(width, tile))
            g_act = dot_nt(g_chunk[...].reshape(tokens, width), wd_all[t // 2, t % 2].reshape(tile, width))
            sig = 1.0 / (1.0 + jnp.exp(-gate))
            silu = gate * sig
            shape = (2, 2, rows, tile)
            act_all[cz, cx, :, :, :, cols] = (silu * up).astype(bf16).reshape(shape)
            g_gate = g_act * up * sig * (1.0 + gate * (1.0 - sig))
            ggu_all[cz, cx, :, :, :, cols] = g_gate.astype(bf16).reshape(shape)
            ggu_all[cz, cx, :, :, :, pl.ds(block + first, tile)] = (g_act * silu).astype(bf16).reshape(shape)

        @pl.loop(0, tiles)
        def _(t):
            cols = pl.ds(pl.multiple_of(t * tile, tile), tile)
            shape = (2, 2, rows, tile)
            g_n2 = dot_nt(
                ggu_all[cz, cx].reshape(tokens, 2 * block), wgu_all[t // 2, t % 2].reshape(tile, 2 * block)
            )
            pg_s[cz, cx, :, :, :, cols] = g_n2.astype(bf16).reshape(shape)

        @pl.when(dx == 1)
        def _():
            link(pg_s.at[cz, cx], pg_r.at[dz], peer(dx=1), sem=pg_base + dz)

        @pl.loop(0, tiles)
        def _(t):
            cols = pl.ds(pl.multiple_of(t * tile, tile), tile)
            shape = (2, 2, rows, tile)
            part = dot(act_all[cz, cx].reshape(tokens, block), wd_all[:, :, :, :, :, cols].reshape(block, tile))
            po_s[cz, cx, :, :, :, cols] = part.astype(bf16).reshape(shape)

        @pl.when(dx == 1)
        def _():
            link(po_s.at[cz, cx], po_r.at[dz], peer(dx=1), sem=po_base + dz)

    for copy in gu_cores + [down_own_core, down_far_core, down_cross]:
        copy.wait_send()
    for copy in (n2_z, n2_x, g_z, g_x, g_zx):
        copy.wait_send()
    pltpu.make_async_copy(n2_all.at[z, x], n2_all.at[z, x], ssem.at[n2_zx_sem]).wait()
    for flips in order:
        ref = wgu_all.at[slab(*flips)]
        pltpu.make_async_copy(ref, ref, ssem.at[gu_sems[flips]]).wait()

    gu_grad = wgu_all

    @pl.loop(0, tiles)
    def _(t):
        cols = pl.ds(pl.multiple_of(t * tile, tile), tile)
        left = n2_all[:, :, :, :, :, cols].reshape(4 * tokens, tile).T

        @pl.loop(0, 2 * block // (2 * tile))
        def _(n):
            wide = pl.ds(pl.multiple_of(n * 2 * tile, 2 * tile), 2 * tile)
            part = dot(left, ggu_all[:, :, :, :, :, wide].reshape(4 * tokens, 2 * tile))
            gu_grad[t // 2, t % 2, :, :, :, wide] = part.astype(bf16).reshape(2, 2, rows, 2 * tile)

    gu_swap = link(gu_grad.at[:, :, :, flip(c, 1)], gu_core, peer(dc=1))

    def wait_block(block_ref, sem):
        pltpu.make_async_copy(block_ref, block_ref, sem).wait()

    def partial_z(sent, came, base):
        wait_block(came.at[1], rsem.at[base + 1])

        @pl.loop(0, 4)
        def _(m):
            at = (m // 2, m % 2)
            ref = sent.at[(flip(z, 1), x) + at]
            ref[...] = (ref[...].astype(f32) + came[(1,) + at].astype(f32)).astype(bf16)

        return link(sent.at[flip(z, 1), x], came.at[2], peer(dz=1), sem=base + 2)

    partial_z(pg_s, pg_r, pg_base)

    down_grad = wd_all

    @pl.loop(0, tiles)
    def _(t):
        cols = pl.ds(pl.multiple_of(t * tile, tile), tile)
        left = act_all[:, :, :, :, :, cols].reshape(4 * tokens, tile).T

        @pl.loop(0, width // (2 * tile))
        def _(n):
            wide = pl.ds(pl.multiple_of(n * 2 * tile, 2 * tile), 2 * tile)
            part = dot(left, g_all[:, :, :, :, :, wide].reshape(4 * tokens, 2 * tile))
            down_grad[t // 2, t % 2, :, :, :, wide] = part.astype(bf16).reshape(2, 2, rows, 2 * tile)

    down_swap = link(down_grad.at[:, flip(c, 1)], down_core, peer(dc=1))

    gu_swap.wait_recv()

    @pl.loop(0, 8)
    def _(m):
        at = (m // 4, (m // 2) % 2, m % 2)
        ref = gu_grad.at[at + (c,)]
        ref[...] = (ref[...].astype(f32) + gu_core[at].astype(f32)).astype(bf16)

    gu_sends = []
    for flips in order:
        gu_sends.append(link(gu_grad.at[slab(*flips)], gu_out.at[s, z, x], peer(*flips)))
    gu_keep = local(gu_grad.at[slab()], gu_out.at[s, z, x])

    down_swap.wait_recv()

    @pl.loop(0, 8)
    def _(m):
        at = (m // 4,)
        rest = ((m // 2) % 2, m % 2)
        ref = down_grad.at[at + (c,) + rest]
        ref[...] = (ref[...].astype(f32) + down_core[at + rest].astype(f32)).astype(bf16)

    down_send = link(down_grad.at[flip(s, 1), c], down_out.at[1], peer(ds=1))
    down_keep = local(down_grad.at[s, c], down_out.at[0])

    partial_z(po_s, po_r, po_base)

    for i in (0, 2):
        wait_block(pg_r.at[i], rsem.at[pg_base + i])
    gsum_s[...] = jnp.zeros_like(gsum_s)

    def add_gain(which, value):
        for i in range(gsum_s.shape[0]):
            gsum_s[i, which : which + 1, :] += value[:, i * 128 : (i + 1) * 128]

    @pl.loop(0, steps)
    def _(i):
        part = pl.ds(i * rows, rows)
        at = (i // 2, i % 2)
        g_n2 = pg_s[(z, x) + at].astype(f32)
        for k in (0, 2):
            g_n2 += pg_r[(k,) + at].astype(f32)
        hidden = hmid[part]
        inv = r_two[part][:, :1]
        add_gain(1, jnp.sum(g_n2 * hidden * inv, axis=0, keepdims=True))
        scaled = g_n2 * gain_row(1)
        inner = jnp.mean(scaled * hidden, axis=-1, keepdims=True)
        g_sum = cot_ref[part].astype(f32) * mask_ref[part]
        g_mid = g_sum + inv * scaled - hidden * (inv * inv * inv * inner)
        gmid[part] = g_mid
        gattn[part] = g_mid.astype(bf16)

    def project_back(left, g, dest):
        @pl.loop(0, tiles)
        def _(t):
            cols = pl.ds(pl.multiple_of(t * tile, tile), tile)
            dest[:, cols] = dot_nt(left[...], wa[g, t // 2, t % 2].reshape(tile, width))

    g_mixed = ig_ref
    project_back(gattn, OUT, g_mixed)

    @pl.loop(0, steps)
    def _(i):
        part = pl.ds(i * rows, rows)
        gm = g_mixed[part]
        gv_s[part] = (head_spread(p_rem[part]) * gm).astype(bf16)

    gv_copy = link(gv_s, gv_r, f, to_y=1 - y)

    @pl.loop(0, steps)
    def _(i):
        part = pl.ds(i * rows, rows)
        gm = g_mixed[part]
        own, far = p_own[part], p_rem[part]
        gp_own = head_sum(gm * vb[part].astype(f32))
        gp_far = head_sum(gm * vrem[part].astype(f32))
        inner = own * gp_own + far * gp_far
        gs_own = head_spread(own * (gp_own - inner) * scale)
        gs_far = head_spread(far * (gp_far - inner) * scale)
        query = qb[part].astype(f32)
        gk_s[part] = (gs_far * query).astype(bf16)
        gq[part] = (gs_own * kb[part].astype(f32) + gs_far * krem[part].astype(f32)).astype(bf16)
        hold_k[part] = gs_own * query

    gk_copy = link(gk_s, gk_r, f, to_y=1 - y)

    stage = {
        OUT: (act_all, width),
        QUERY: (n2_all, width),
        VALUE: (g_all, width),
        KEY: (ggu_all, width),
    }
    legs = {}

    def grad_view(g, *at):
        ref = stage[g][0]
        if ref.shape[-1] != width:
            return ref.at[at + (slice(None),) * (5 - len(at)) + (pl.ds(0, width),)]
        return ref.at[at]

    def weight_grad(g, left, right):
        @pl.loop(0, tiles)
        def _(t):
            cols = pl.ds(pl.multiple_of(t * tile, tile), tile)
            part = dot(left[:, cols].T, right[...])
            grad_view(g, t // 2, t % 2)[...] = part.astype(bf16).reshape(2, 2, rows, width)

        every = slice(None)
        legs[g] = [link(grad_view(g, every, every, every, flip(c, 1)), attn_core.at[g], peer(dc=1))]

    def add_into(g, count, at_of, came):
        @pl.loop(0, count)
        def _(m):
            ref = grad_view(g, *at_of(m))
            ref[...] = (ref[...].astype(f32) + came(m)[...].astype(f32)).astype(bf16)

    def leg_x(g):
        legs[g][0].wait_recv()
        add_into(
            g, 8, lambda m: (m // 4, (m // 2) % 2, m % 2, c), lambda m: attn_core.at[g, m // 4, (m // 2) % 2, m % 2]
        )
        every = slice(None)
        legs[g].append(link(grad_view(g, every, every, flip(x, 1), c), attn_x.at[g], peer(dx=1)))

    def leg_z(g):
        legs[g][1].wait_recv()
        add_into(g, 4, lambda m: (m // 2, m % 2, x, c), lambda m: attn_x.at[g, m // 2, m % 2])
        every = slice(None)
        legs[g].append(link(grad_view(g, every, flip(z, 1), x, c), attn_z.at[g], peer(dz=1)))

    def leg_cross(g):
        legs[g][2].wait_recv()
        add_into(g, 2, lambda m: (m, z, x, c), lambda m: attn_z.at[g, m])
        legs[g].append(link(grad_view(g, flip(s, 1), z, x, c), attn_out.at[1, g], peer(ds=1)))
        legs[g].append(local(grad_view(g, s, z, x, c), attn_out.at[0, g]))

    weight_grad(OUT, mixed, gattn)
    weight_grad(QUERY, normed, gq)
    leg_x(OUT)
    leg_x(QUERY)
    gv_copy.wait_recv()

    @pl.loop(0, steps)
    def _(i):
        part = pl.ds(i * rows, rows)
        own = head_spread(p_own[part]) * g_mixed[part]
        gv[part] = (own + gv_r[part].astype(f32)).astype(bf16)

    weight_grad(VALUE, normed, gv)
    leg_x(VALUE)
    gk_copy.wait_recv()

    @pl.loop(0, steps)
    def _(i):
        part = pl.ds(i * rows, rows)
        gk[part] = (hold_k[part] + gk_r[part].astype(f32)).astype(bf16)

    weight_grad(KEY, normed, gk)
    leg_z(OUT)
    leg_x(KEY)
    leg_z(QUERY)
    leg_cross(OUT)

    @pl.loop(0, tiles)
    def _(t):
        cols = pl.ds(pl.multiple_of(t * tile, tile), tile)
        at = (t // 2, t % 2)
        ig_ref[:, cols] = (
            dot_nt(gq[...], wa[(QUERY,) + at].reshape(tile, width))
            + dot_nt(gk[...], wa[(KEY,) + at].reshape(tile, width))
            + dot_nt(gv[...], wa[(VALUE,) + at].reshape(tile, width))
        )

    @pl.loop(0, steps)
    def _(i):
        part = pl.ds(i * rows, rows)
        hidden = x_ref[part].astype(f32)
        inv = r_one[part][:, :1]
        g_n1 = ig_ref[part]
        add_gain(0, jnp.sum(g_n1 * hidden * inv, axis=0, keepdims=True))
        scaled = g_n1 * gain_row(0)
        inner = jnp.mean(scaled * hidden, axis=-1, keepdims=True)
        ig_ref[part] = gmid[part] + inv * scaled - hidden * (inv * inv * inv * inner)

    def gain_sum_copy(r):
        to = lax.rem(f + r, 16)
        return pltpu.make_async_remote_copy(
            src_ref=gsum_s.at[to // per_block], dst_ref=gsum_r.at[r - 1],
            send_sem=hsem_s.at[r - 1], recv_sem=hsem_r.at[r - 1],
            device_id=(to, y), device_id_type=MESH,
        )

    @pl.loop(1, 16)
    def _(r):
        gain_sum_copy(r).start()

    leg_z(VALUE)
    leg_cross(QUERY)
    leg_z(KEY)
    leg_cross(VALUE)

    for i in (0, 2):
        wait_block(po_r.at[i], rsem.at[po_base + i])

    @pl.loop(0, steps)
    def _(i):
        part = pl.ds(i * rows, rows)
        at = (i // 2, i % 2)
        total = po_s[(z, x) + at].astype(f32)
        for k in (0, 2):
            total += po_r[(k,) + at].astype(f32)
        out_ref[part] = (mask_ref[part] * (hmid[part] + total)).astype(bf16)

    leg_cross(KEY)
    gain_out[...] = gsum_s[f // per_block]

    @pl.loop(1, 16)
    def _(r):
        gain_sum_copy(r).wait()
        gain_out[...] += gsum_r[r - 1]

    for copy in keep + [k_copy, v_copy, gv_copy, gk_copy, gu_swap, down_swap]:
        copy.wait_send()
    for i in range(3):
        wait_block(po_r.at[i], ssem.at[po_base + i])
        wait_block(pg_r.at[i], ssem.at[pg_base + i])
    for copy in gu_sends + [down_send]:
        copy.wait()
    gu_keep.wait()
    down_keep.wait()
    for g in (OUT, QUERY, VALUE, KEY):
        for copy in legs[g][:3]:
            copy.wait_send()
        legs[g][3].wait()
        legs[g][4].wait()


def square_layer(inputs, frame_flags, attn_gain, qkv_weight, out_weight, ffn_gain, gate_up_weight, down_weight, cotangent):
    tokens, _, width = inputs.shape
    rows = qkv_weight.shape[2]
    block = width
    f32, bf16 = jnp.float32, jnp.bfloat16
    lane_block = 128
    per_block = lane_block // rows
    f = lax.axis_index("fsdp")
    lane_blocks = width // lane_block
    gains = jnp.concatenate([attn_gain[0], ffn_gain[0]], axis=0)
    gains = jnp.concatenate([jnp.where(f % per_block == b, gains, 0) for b in range(per_block)], axis=1).astype(bf16)
    gains = jnp.pad(gains, ((0, 14), (0, 0)))
    mask = frame_flags.astype(f32)[:, None]
    vmem = pl.BlockSpec(memory_space=pltpu.VMEM)
    anywhere = pl.BlockSpec(memory_space=pl.ANY)
    unit = (2, 2, 2, 2, rows, width)
    double = (2, 2, 2, 2, rows, 2 * block)
    own = (tokens, width)
    scratch = [
        pltpu.VMEM((4,) + unit, bf16),
        pltpu.VMEM(double, bf16),
        pltpu.VMEM(unit, bf16),
        pltpu.VMEM(unit, bf16),
        pltpu.VMEM(unit, bf16),
        pltpu.VMEM(unit, bf16),
        pltpu.VMEM(double, bf16),
        pltpu.VMEM(unit, bf16),
        pltpu.VMEM((3, 2, 2, rows, width), bf16),
        pltpu.VMEM(unit, bf16),
        pltpu.VMEM((3, 2, 2, rows, width), bf16),
        pltpu.VMEM((2, 2, 2, rows, 2 * block), bf16),
        pltpu.VMEM((2, 2, 2, rows, width), bf16),
        pltpu.VMEM((4, 2, 2, 2, rows, width), bf16),
        pltpu.VMEM((4, 2, 2, rows, width), bf16),
        pltpu.VMEM((4, 2, rows, width), bf16),
        pltpu.VMEM(own, bf16),
        pltpu.VMEM(own, bf16),
        pltpu.VMEM(own, bf16),
        pltpu.VMEM(own, bf16),
        pltpu.VMEM(own, bf16),
        pltpu.VMEM(own, bf16),
        pltpu.VMEM(own, bf16),
        pltpu.VMEM(own, f32),
        pltpu.VMEM(own, bf16),
        pltpu.VMEM(own, bf16),
        pltpu.VMEM(own, bf16),
        pltpu.VMEM(own, bf16),
        pltpu.VMEM(own, bf16),
        pltpu.VMEM(own, bf16),
        pltpu.VMEM(own, bf16),
        pltpu.VMEM(own, f32),
        pltpu.VMEM(own, bf16),
        pltpu.VMEM(own, f32),
        pltpu.VMEM((tokens, 128), f32),
        pltpu.VMEM((tokens, 128), f32),
        pltpu.VMEM((tokens, 128), f32),
        pltpu.VMEM((tokens, 128), f32),
        pltpu.VMEM((15, 16, lane_block), bf16),
        pltpu.VMEM((lane_blocks, 16, lane_block), f32),
        pltpu.VMEM((lane_blocks, 8, lane_block), f32),
        pltpu.VMEM((15, 8, lane_block), f32),
        pltpu.VMEM((width, 128), bf16),
        pltpu.VMEM((128, width), bf16),
        pltpu.SemaphoreType.DMA((SEMS,)),
        pltpu.SemaphoreType.DMA((SEMS,)),
        pltpu.SemaphoreType.DMA((16,)),
        pltpu.SemaphoreType.DMA((15,)),
        pltpu.SemaphoreType.DMA((15,)),
        pltpu.SemaphoreType.DMA((15,)),
        pltpu.SemaphoreType.DMA((15,)),
    ]
    outs = pl.pallas_call(
        square_kernel,
        out_shape=(
            jax.ShapeDtypeStruct(own, bf16),
            jax.ShapeDtypeStruct(own, f32),
            jax.ShapeDtypeStruct((8, lane_block), f32),
            jax.ShapeDtypeStruct((2, 2, 2, rows, 2 * block), bf16),
            jax.ShapeDtypeStruct((2, 2, 2, rows, width), bf16),
            jax.ShapeDtypeStruct((2, 4, rows, width), bf16),
        ),
        in_specs=[vmem] * 4 + [anywhere] * 4,
        out_specs=(vmem, vmem, vmem, anywhere, anywhere, anywhere),
        scratch_shapes=scratch,
        compiler_params=pltpu.CompilerParams(
            collective_id=0, has_side_effects=True, vmem_limit_bytes=VMEM_BYTES
        ),
        cost_estimate=pl.CostEstimate(flops=26 * 10**9, bytes_accessed=2**23, transcendentals=2**21),
    )(
        inputs[:, 0], cotangent[:, 0], mask, gains,
        qkv_weight[0, 0], out_weight[0, 0], gate_up_weight[0, 0], down_weight[0, 0].reshape(2, 2, rows, width),
    )
    result, input_grad, gain_sums, gu, down, attn = outs
    gain_sums = sum(
        jnp.where(f % per_block == b, gain_sums[:2, b * rows : (b + 1) * rows], 0.0) for b in range(per_block)
    )
    gu = gu.astype(f32)
    gu = (gu[0] + gu[1]).reshape(4, rows, 2, 2, block // 2).transpose(1, 2, 3, 0, 4).reshape(1, 1, rows, 8 * block)
    down = (down[0].astype(f32) + down[1].astype(f32)).reshape(down_weight.shape)
    attn = attn[0].astype(f32) + attn[1].astype(f32)
    qkv = jnp.concatenate([attn[QUERY], attn[KEY], attn[VALUE]], axis=1)[None, None]
    return (
        result[:, None],
        input_grad[:, None],
        gain_sums[0:1, None],
        qkv,
        attn[OUT][None, None],
        gain_sums[1:2, None],
        gu,
        down,
    )


VMEM_BYTES = 62 * 2**20


def run_layer(axes, *args):
    inputs, qkv_weight, down_weight = args[0], args[3], args[7]
    tokens, places, width = inputs.shape
    rows = qkv_weight.shape[2]
    square = (
        axes["fsdp"] == 16
        and axes["pos"] == 2
        and places == 1
        and qkv_weight.shape[0] == 1
        and tokens == 4 * rows
        and down_weight.shape[2] == 4 * rows
        and 128 % rows == 0
    )
    return square_layer(*args) if square else on_device(*args)


def solution(mesh):
    in_specs = (
        P("fsdp", "pos", None),
        P("fsdp"),
        P(None, "pos", "fsdp"),
        P(None, "pos", "fsdp", None),
        P(None, "pos", "fsdp", None),
        P(None, "pos", "fsdp"),
        P(None, "pos", "fsdp", None),
        P(None, "pos", "fsdp", None),
        P("fsdp", "pos", None),
    )
    out_specs = (
        P("fsdp", "pos", None),
        P("fsdp", "pos", None),
        P(None, "pos", "fsdp"),
        P(None, "pos", "fsdp", None),
        P(None, "pos", "fsdp", None),
        P(None, "pos", "fsdp"),
        P(None, "pos", "fsdp", None),
        P(None, "pos", "fsdp", None),
    )
    return jax.shard_map(
        functools.partial(run_layer, dict(mesh.shape)), mesh=mesh, in_specs=in_specs, out_specs=out_specs, check_vma=False
    )
```

```python
import functools
import math

import jax
import jax.numpy as jnp
from jax import lax
from jax.experimental import pallas as pl
from jax.experimental.pallas import tpu as pltpu
from jax.sharding import PartitionSpec as P

D = 1024
HEADS = 16
HEAD_DIM = 64
FF = 4096


EPSILON = 1e-06
MASKED = -1e30
PRECISE = lax.Precision.HIGHEST


def rms_parts(hidden, gain_row):
    inv_rms = lax.rsqrt(jnp.mean(hidden * hidden, axis=-1, keepdims=True) + EPSILON)
    return (hidden * inv_rms * gain_row[None], inv_rms)


def rms_back(grad_rows, hidden, inv_rms, gain_row):
    scaled = grad_rows * gain_row[None]
    gain_grad = jnp.sum(grad_rows * hidden * inv_rms, axis=0)
    inner_mean = jnp.mean(scaled * hidden, axis=-1, keepdims=True)
    return (inv_rms * scaled - hidden * inv_rms**3 * inner_mean, gain_grad)


def apply_rows(left_side, weight):
    return jnp.einsum("fpd,pde->fpe", left_side, weight, preferred_element_type=jnp.float32)


def apply_back(grad_rows, weight):
    return jnp.einsum("fpe,pde->fpd", grad_rows, weight, preferred_element_type=jnp.float32)


def outer_sum(left_side, grad_rows):
    return jnp.einsum("fpd,fpe->pde", left_side, grad_rows, preferred_element_type=jnp.float32)


def split_heads(rows):
    return rows.reshape(rows.shape[0], rows.shape[1], HEADS, HEAD_DIM)


def attention_weights(attn_gain, qkv_weight, out_weight, layer_idx):
    return (
        lax.all_gather(attn_gain[layer_idx], "fsdp", axis=1, tiled=True),
        lax.all_gather(qkv_weight[layer_idx], "fsdp", axis=1, tiled=True),
        lax.all_gather(out_weight[layer_idx], "fsdp", axis=1, tiled=True),
    )


def ffn_weights(ffn_gain, gate_up_weight, down_weight, layer_idx):
    return (
        lax.all_gather(ffn_gain[layer_idx], "fsdp", axis=1, tiled=True),
        lax.all_gather(gate_up_weight[layer_idx], "fsdp", axis=1, tiled=True),
        lax.all_gather(down_weight[layer_idx], "fsdp", axis=1, tiled=True),
    )


def attention_forward(qkv_rows):
    frames, places = (qkv_rows.shape[0], qkv_rows.shape[1])
    pos_count = lax.axis_size("pos")
    frame_part = frames // pos_count
    outgoing = qkv_rows.reshape(pos_count, frame_part, places, 3 * D)
    frame_qkv = lax.all_to_all(outgoing, "pos", split_axis=0, concat_axis=2, tiled=True)[0].astype(
        jnp.float32
    )
    whole_places = frame_qkv.shape[1]
    queries = split_heads(frame_qkv[..., :D])
    keys_all = split_heads(frame_qkv[..., D : 2 * D])
    values_all = split_heads(frame_qkv[..., 2 * D :])
    scores = jnp.einsum("fphe,fjhe->fhpj", queries, keys_all, precision=PRECISE) / math.sqrt(
        HEAD_DIM
    )
    causal = jnp.arange(whole_places)[:, None] >= jnp.arange(whole_places)[None, :]
    scores = jnp.where(causal, scores, MASKED)
    row_max = jnp.max(scores, axis=-1, keepdims=True)
    exponent = jnp.exp(scores - row_max)
    attn_probs = exponent / jnp.sum(exponent, axis=-1, keepdims=True)
    mixed_heads = jnp.einsum("fhpj,fjhe->fphe", attn_probs, values_all, precision=PRECISE)
    mixed_frames = mixed_heads.reshape(frame_part, whole_places, D).astype(jnp.bfloat16)
    returned = lax.all_to_all(mixed_frames[None], "pos", split_axis=2, concat_axis=0, tiled=True)
    return (returned.reshape(frames, places, D), (queries, keys_all, values_all, attn_probs))


def attention_backward(grad_mixed, attn_keep):
    queries, keys_all, values_all, attn_probs = attn_keep
    frames, places = (grad_mixed.shape[0], grad_mixed.shape[1])
    pos_count = lax.axis_size("pos")
    frame_part = frames // pos_count
    outgoing = grad_mixed.reshape(pos_count, frame_part, places, D)
    grad_frames = lax.all_to_all(
        outgoing.astype(jnp.bfloat16), "pos", split_axis=0, concat_axis=2, tiled=True
    ).astype(outgoing.dtype)[0]
    whole_places = grad_frames.shape[1]
    grad_heads = split_heads(grad_frames)
    grad_values = jnp.einsum("fhpj,fphe->fjhe", attn_probs, grad_heads, precision=PRECISE)
    grad_probs = jnp.einsum("fphe,fjhe->fhpj", grad_heads, values_all, precision=PRECISE)
    grad_scores = (
        attn_probs
        * (grad_probs - jnp.sum(attn_probs * grad_probs, axis=-1, keepdims=True))
        / math.sqrt(HEAD_DIM)
    )
    grad_queries = jnp.einsum("fhpj,fjhe->fphe", grad_scores, keys_all, precision=PRECISE)
    grad_keys = jnp.einsum("fhpj,fphe->fjhe", grad_scores, queries, precision=PRECISE)
    frame_grads = jnp.concatenate(
        [
            grad_queries.reshape(frame_part, whole_places, D),
            grad_keys.reshape(frame_part, whole_places, D),
            grad_values.reshape(frame_part, whole_places, D),
        ],
        axis=-1,
    ).astype(jnp.bfloat16)
    returned = lax.all_to_all(frame_grads[None], "pos", split_axis=2, concat_axis=0, tiled=True)
    return returned.reshape(frames, places, 3 * D)


def layer_forward(hidden, frame_mask, attn_set, ffn_set):
    gain_one, qkv_full, out_full = attn_set
    gain_two, gate_up_full, down_full = ffn_set
    normed, inv_one = rms_parts(hidden, gain_one.astype(jnp.float32))
    normed_low = normed.astype(jnp.bfloat16)
    qkv_rows = apply_rows(normed_low, qkv_full).astype(jnp.bfloat16)
    mixed_low, attn_keep = attention_forward(qkv_rows)
    hidden_mid = hidden + apply_rows(mixed_low, out_full)
    normed_two, inv_two = rms_parts(hidden_mid, gain_two.astype(jnp.float32))
    normed_two_low = normed_two.astype(jnp.bfloat16)
    gate_up = apply_rows(normed_two_low, gate_up_full)
    gate_part = gate_up[..., :FF]
    up_part = gate_up[..., FF:]
    act_low = (jax.nn.silu(gate_part) * up_part).astype(jnp.bfloat16)
    result = frame_mask * (hidden_mid + apply_rows(act_low, down_full))
    kept_state = (
        hidden,
        inv_one,
        normed_low,
        attn_keep,
        mixed_low,
        hidden_mid,
        inv_two,
        normed_two_low,
        gate_part,
        up_part,
        act_low,
    )
    return (result, kept_state)


def layer_backward(grad_out, frame_mask, kept_state, ffn_set, fetch_attn):
    (
        hidden,
        inv_one,
        normed_low,
        attn_keep,
        mixed_low,
        hidden_mid,
        inv_two,
        normed_two_low,
        gate_part,
        up_part,
        act_low,
    ) = kept_state
    gain_two, gate_up_full, down_full = ffn_set
    grad_sum = frame_mask * grad_out
    grad_ffn = grad_sum.astype(jnp.bfloat16)
    down_grad = outer_sum(act_low, grad_ffn)
    down_shard = lax.psum_scatter(down_grad, "fsdp", scatter_dimension=1, tiled=True)
    grad_act = apply_back(grad_ffn, down_full)
    sigmoid_gate = jax.nn.sigmoid(gate_part)
    grad_gate = grad_act * up_part * sigmoid_gate * (1.0 + gate_part * (1.0 - sigmoid_gate))
    grad_up = grad_act * gate_part * sigmoid_gate
    grad_gu = jnp.concatenate([grad_gate, grad_up], axis=-1).astype(jnp.bfloat16)
    gate_up_grad = outer_sum(normed_two_low, grad_gu)
    grad_norm_two = apply_back(grad_gu, gate_up_full)
    grad_mid_norm, gain_two_grad = rms_back(
        grad_norm_two, hidden_mid, inv_two, gain_two.astype(jnp.float32)
    )
    ffn_shards = (
        lax.psum_scatter(gain_two_grad, "fsdp", scatter_dimension=1, tiled=True),
        lax.psum_scatter(gate_up_grad, "fsdp", scatter_dimension=1, tiled=True),
    )
    gain_one, qkv_full, out_full = fetch_attn()
    grad_mid = grad_sum + grad_mid_norm
    grad_attn = grad_mid.astype(jnp.bfloat16)
    out_grad = outer_sum(mixed_low, grad_attn)
    grad_mixed = apply_back(grad_attn, out_full)
    grad_qkv = attention_backward(grad_mixed, attn_keep)
    qkv_grad = outer_sum(normed_low, grad_qkv)
    grad_norm_one = apply_back(grad_qkv, qkv_full)
    grad_in_norm, gain_one_grad = rms_back(
        grad_norm_one, hidden, inv_one, gain_one.astype(jnp.float32)
    )
    attn_shards = (
        lax.psum_scatter(gain_one_grad, "fsdp", scatter_dimension=1, tiled=True),
        lax.psum_scatter(qkv_grad, "fsdp", scatter_dimension=1, tiled=True),
        lax.psum_scatter(out_grad, "fsdp", scatter_dimension=1, tiled=True),
    )
    grad_in = grad_mid + grad_in_norm
    return (
        grad_in,
        (attn_shards[0], attn_shards[1], attn_shards[2], ffn_shards[0], ffn_shards[1], down_shard),
    )


def on_device(
    inputs,
    frame_flags,
    attn_gain,
    qkv_weight,
    out_weight,
    ffn_gain,
    gate_up_weight,
    down_weight,
    cotangent,
):
    layer_total = qkv_weight.shape[0]
    frame_mask = frame_flags.astype(jnp.float32)[:, None, None]
    hidden = inputs.astype(jnp.float32)
    layer_idx = 0
    attn_set = attention_weights(attn_gain, qkv_weight, out_weight, layer_idx)
    ffn_set = ffn_weights(ffn_gain, gate_up_weight, down_weight, layer_idx)
    hidden, kept_state = layer_forward(hidden, frame_mask, attn_set, ffn_set)
    states_all = [kept_state]
    grad_rows = cotangent.astype(jnp.float32)
    layer_grads = [None] * layer_total
    for layer_idx in reversed(range(layer_total)):
        ffn_set = ffn_weights(ffn_gain, gate_up_weight, down_weight, layer_idx)
        fetch_attn = gather_later(attn_gain, qkv_weight, out_weight, layer_idx)
        grad_rows, layer_grads[layer_idx] = layer_backward(
            grad_rows, frame_mask, states_all[layer_idx], ffn_set, fetch_attn
        )
    stacked = [jnp.stack([grad_set[column] for grad_set in layer_grads]) for column in range(6)]
    return (
        hidden.astype(jnp.bfloat16),
        grad_rows,
        stacked[0],
        stacked[1],
        stacked[2],
        stacked[3],
        stacked[4],
        stacked[5],
    )


def gather_later(attn_gain, qkv_weight, out_weight, layer_idx):

    def fetched():
        return attention_weights(attn_gain, qkv_weight, out_weight, layer_idx)

    return fetched


KEY, VALUE, QUERY, OUT = 0, 1, 2, 3
SEMS = 128
MESH = pl.DeviceIdType.MESH


def flip(bit, change):
    return bit + change - 2 * bit * change


def square_kernel(
    x_ref, cot_ref, flags_ref, gain_one_ref, gain_two_ref, wqkv, wout, wgu, wd,
    out_ref, ig_ref, gain_one_out, gain_two_out, gu_out, down_out, attn_out,
    wa, wgu_all, wd_all, n2_all, g_all, act_all, ggu_all,
    po_s, po_r, pg_s, pg_r, gu_core, down_core, attn_core, attn_x, attn_z,
    normed, qb, kb, vb, krem, vrem, mixed, hmid, gv_s, gk_s, gv_r, gk_r,
    gq, gk, gv, gmid, gattn, hold_k, gwide, mask, gain_ref, p_own, p_rem, r_one, r_two,
    gain_r, gain_f, gsum_s, gsum_r, ends, ends_t,
    ssem, rsem, lsem, gsem_s, gsem_r, hsem_s, hsem_r,
):
    tokens, width = x_ref.shape
    rows = width // 16
    block = 4 * width // 4
    half = block // 2
    ff = 4 * width
    f = lax.axis_index("fsdp")
    y = lax.axis_index("pos")
    c = f % 2
    x = (f // 2) % 2
    z = (f // 4) % 2
    s = f // 8
    f32, bf16 = jnp.float32, jnp.bfloat16

    def peer(ds=0, dz=0, dx=0, dc=0):
        return flip(s, ds) * 8 + flip(z, dz) * 4 + flip(x, dx) * 2 + flip(c, dc)

    def slab(ds=0, dz=0, dx=0, dc=0):
        return flip(s, ds), flip(z, dz), flip(x, dx), flip(c, dc)

    counter = [0]
    pending = []

    def take(n=1):
        counter[0] += n
        assert counter[0] <= SEMS
        return counter[0] - n

    def link(src, dst, to, sem=None, to_y=None):
        if sem is None:
            sem = take()
        copy = pltpu.make_async_remote_copy(
            src_ref=src, dst_ref=dst, send_sem=ssem.at[sem], recv_sem=rsem.at[sem],
            device_id=(to, y if to_y is None else to_y), device_id_type=MESH,
        )
        copy.start()
        return copy

    lcount = [0]

    def local(src, dst):
        lcount[0] += 1
        copy = pltpu.make_async_copy(src, dst, lsem.at[lcount[0] - 1])
        copy.start()
        return copy

    def dot(a, b):
        return jnp.dot(a, b, preferred_element_type=f32)

    def dot_nt(a, b):
        return lax.dot_general(a, b, (((1,), (1,)), ((), ())), preferred_element_type=f32)

    def split(v):
        high = v.astype(bf16)
        return high, (v - high.astype(f32)).astype(bf16)

    def head_sum(v):
        high, low = split(v)
        return dot(high, ends[...]) + dot(low, ends[...])

    def head_spread(p):
        high, low = split(p)
        return dot(high, ends_t[...]) + dot(low, ends_t[...])

    barrier = pltpu.get_barrier_semaphore()

    @pl.loop(1, 16)
    def _(r):
        pl.semaphore_signal(barrier, inc=1, device_id=(lax.rem(f + r, 16), y), device_id_type=MESH)

    pl.semaphore_signal(barrier, inc=1, device_id=(f, 1 - y), device_id_type=MESH)
    pl.semaphore_wait(barrier, 16)

    lane_block = 128
    per_block = lane_block // rows
    lanes = lax.broadcasted_iota(jnp.int32, gain_ref.shape, 1) // rows == f % per_block
    sublane = lax.broadcasted_iota(jnp.int32, gain_ref.shape, 0)

    def lane_tile(ref):
        return jnp.concatenate([ref[...].astype(f32)] * per_block, axis=1)

    gains = jnp.where(sublane == 0, lane_tile(gain_one_ref), jnp.where(sublane == 1, lane_tile(gain_two_ref), 0.0))
    gain_ref[...] = jnp.where(lanes, gains, 0.0).astype(bf16)

    def gain_copy(r):
        return pltpu.make_async_remote_copy(
            src_ref=gain_ref, dst_ref=gain_r.at[r - 1], send_sem=gsem_s.at[r - 1], recv_sem=gsem_r.at[r - 1],
            device_id=(lax.rem(f + r, 16), y), device_id_type=MESH,
        )

    @pl.loop(1, 16)
    def _(r):
        gain_copy(r).start()

    own_cols = (
        wqkv.at[:, pl.ds(width, width)],
        wqkv.at[:, pl.ds(2 * width, width)],
        wqkv.at[:, pl.ds(0, width)],
        wout,
    )
    keep = []
    legs_in = {g: {} for g in range(4)}

    def own_send(g, *ways):
        own = wa.at[(g,) + slab()]
        src = own_cols[g]
        flips = {"s": (1, 0, 0, 0), "z": (0, 1, 0, 0), "x": (0, 0, 1, 0), "c": (0, 0, 0, 1)}
        for way in ways:
            copy = link(src, own, peer(*flips[way]))
            keep.append(copy)
            legs_in[g][way] = copy
        if "c" in ways:
            legs_in[g]["own"] = local(src, own)
            legs_in[g]["cores"] = []

    def forward(g, at, to):
        ref = wa.at[(g,) + slab(*at)]
        copy = link(ref, ref, to)
        keep.append(copy)
        return copy

    def to_core(g, at):
        legs_in[g]["cores"].append(forward(g, at, peer(dc=1)))

    def from_cross(g):
        leg = legs_in[g]
        leg["s"].wait_recv()
        leg["sz"] = forward(g, (1, 0, 0, 0), peer(dz=1))
        leg["sx"] = forward(g, (1, 0, 0, 0), peer(dx=1))
        to_core(g, (1, 0, 0, 0))

    def from_z(g):
        leg = legs_in[g]
        leg["z"].wait_recv()
        leg["zx"] = forward(g, (0, 1, 0, 0), peer(dx=1))
        to_core(g, (0, 1, 0, 0))

    def from_cross_z(g):
        leg = legs_in[g]
        leg["sz"].wait_recv()
        leg["szx"] = forward(g, (1, 1, 0, 0), peer(dx=1))
        to_core(g, (1, 1, 0, 0))

    def from_x(g):
        leg = legs_in[g]
        for name, at in (("x", (0, 0, 1, 0)), ("sx", (1, 0, 1, 0)), ("zx", (0, 1, 1, 0)), ("szx", (1, 1, 1, 0))):
            leg[name].wait_recv()
            to_core(g, at)

    def from_core(g):
        leg = legs_in[g]
        leg["own"].wait()
        leg["c"].wait_recv()
        for copy in leg["cores"]:
            copy.wait_recv()

    gu_sems = {}

    def gu_pieces(flips):
        ds, dz, dx = flips
        j = flip(z, dz) * 2 + flip(x, dx)
        for u in range(2):
            for part in range(2):
                src = wgu.at[:, pl.ds(pl.multiple_of(u * ff + part * (ff // 2) + j * half, half), half)]
                dst = wgu_all.at[s, z, x, c, :, pl.ds(u * block + part * half, half)]
                yield src, dst

    order = ((1, 0, 0), (1, 0, 1), (1, 1, 0), (1, 1, 1), (0, 0, 1), (0, 1, 0), (0, 1, 1))

    def gu_send(k):
        sem = take()
        gu_sems[order[k]] = sem
        for src, dst in gu_pieces(order[k]):
            link(src, dst, peer(*order[k]), sem=sem)

    own_send(KEY, "s", "z", "x", "c")
    own_send(VALUE, "s", "z", "x", "c")
    own_send(QUERY, "x")

    ends[...] = (
        lax.broadcasted_iota(jnp.int32, ends.shape, 0) // HEAD_DIM == lax.broadcasted_iota(jnp.int32, ends.shape, 1)
    ).astype(bf16)
    ends_t[...] = (
        lax.broadcasted_iota(jnp.int32, ends_t.shape, 1) // HEAD_DIM == lax.broadcasted_iota(jnp.int32, ends_t.shape, 0)
    ).astype(bf16)

    for i in range(tokens // 128):
        flags = flags_ref[i : i + 1, :].astype(f32)
        mask[i * 128 : (i + 1) * 128] = jnp.broadcast_to(flags, (128, 128)).T
    g_all[z, x] = (cot_ref[...].astype(f32) * mask[:, :1]).astype(bf16).reshape(2, 2, rows, width)

    g_z = link(g_all.at[z, x], g_all.at[z, x], peer(dz=1))
    g_x = link(g_all.at[z, x], g_all.at[z, x], peer(dx=1))

    gain_f[...] = jnp.zeros_like(gain_f)
    gain_f[f // per_block] += gain_ref[...].astype(f32)

    @pl.loop(1, 16)
    def _(r):
        gain_copy(r).wait()
        gain_f[lax.rem(f + 16 - r, 16) // per_block] += gain_r[r - 1].astype(f32)

    def gain_row(which):
        return jnp.concatenate([gain_f[i, which : which + 1, :] for i in range(gain_f.shape[0])], axis=1)

    steps = tokens // rows

    @pl.loop(0, steps)
    def _(i):
        part = pl.ds(i * rows, rows)
        hidden = x_ref[part].astype(f32)
        inv = lax.rsqrt(jnp.mean(hidden * hidden, axis=-1, keepdims=True) + EPSILON)
        r_one[part] = jnp.broadcast_to(inv, (rows, 128))
        normed[part] = (hidden * inv * gain_row(0)).astype(bf16)

    tile = 256 if width >= 256 else width
    tiles = width // tile
    quarter = width // 4

    def project(left, g, dest):
        @pl.loop(0, tiles)
        def _(t):
            cols = pl.ds(pl.multiple_of(t * tile, tile), tile)
            dest[:, cols] = dot(left[...], wa[g, :, :, :, :, :, cols].reshape(width, tile)).astype(dest.dtype)

    from_cross(KEY)
    from_z(KEY)
    own_send(QUERY, "s", "z", "c")
    from_cross(VALUE)
    from_cross_z(KEY)
    from_z(VALUE)
    gu_send(0)
    own_send(OUT, "x", "s", "z", "c")
    from_cross(QUERY)
    from_x(KEY)
    from_cross_z(VALUE)
    from_z(QUERY)
    from_core(KEY)
    project(normed, KEY, kb)
    k_copy = link(kb, krem, f, to_y=1 - y)
    gu_send(1)
    from_x(VALUE)
    from_cross_z(QUERY)
    from_cross(OUT)
    from_z(OUT)
    from_core(VALUE)
    project(normed, VALUE, vb)
    v_copy = link(vb, vrem, f, to_y=1 - y)
    gu_send(2)
    from_cross_z(OUT)
    gu_send(3)
    gu_send(6)
    gu_send(5)
    gu_send(4)
    own_gu_sem = lsem.at[lcount[0]]
    lcount[0] += 1
    for src, dst in gu_pieces((0, 0, 0)):
        pltpu.make_async_copy(src, dst, own_gu_sem).start()

    own_down = wd_all.at[s, c]
    down_cross = link(wd, own_down, peer(ds=1))
    down_own_core = link(wd, own_down, peer(dc=1))
    down_local = local(wd, own_down)

    from_x(QUERY)
    g_z.wait_recv()
    g_zx = link(g_all.at[flip(z, 1), x], g_all.at[flip(z, 1), x], peer(dx=1))
    from_core(QUERY)
    project(normed, QUERY, qb)
    from_x(OUT)
    from_core(OUT)

    k_copy.wait_recv()
    v_copy.wait_recv()
    scale = 1.0 / math.sqrt(HEAD_DIM)

    @pl.loop(0, steps)
    def _(i):
        part = pl.ds(i * rows, rows)
        query = qb[part].astype(f32)
        own = head_sum(query * kb[part].astype(f32)) * scale
        far = jnp.where(y > 0, head_sum(query * krem[part].astype(f32)) * scale, MASKED)
        top = jnp.maximum(own, far)
        own = jnp.exp(own - top)
        far = jnp.exp(far - top)
        total = own + far
        own = own / total
        far = far / total
        p_own[part] = own
        p_rem[part] = far
        mixed[part] = (head_spread(own) * vb[part].astype(f32) + head_spread(far) * vrem[part].astype(f32)).astype(bf16)

    project(mixed, OUT, hmid)

    @pl.loop(0, steps)
    def _(i):
        part = pl.ds(i * rows, rows)
        hidden = x_ref[part].astype(f32) + hmid[part]
        hmid[part] = hidden
        inv = lax.rsqrt(jnp.mean(hidden * hidden, axis=-1, keepdims=True) + EPSILON)
        r_two[part] = jnp.broadcast_to(inv, (rows, 128))
        n2_all[z, x, i // 2, i % 2] = (hidden * inv * gain_row(1)).astype(bf16)

    n2_z = link(n2_all.at[z, x], n2_all.at[z, x], peer(dz=1))
    n2_x = link(n2_all.at[z, x], n2_all.at[z, x], peer(dx=1))
    n2_far = take(2)
    g_x.wait_recv()
    g_zx.wait_recv()

    pltpu.make_async_copy(wgu_all.at[slab()], wgu_all.at[slab()], own_gu_sem).wait()
    gu_cores = []
    for flips in ((0, 0, 0), (0, 0, 1), (0, 1, 0), (0, 1, 1), (1, 0, 0), (1, 0, 1), (1, 1, 0), (1, 1, 1)):
        ref = wgu_all.at[slab(*flips)]
        if flips != (0, 0, 0):
            pltpu.make_async_copy(ref, ref, rsem.at[gu_sems[flips]]).wait()
        gu_cores.append(link(ref, ref, peer(dc=1)))
    down_cross.wait_recv()
    far_down = wd_all.at[flip(s, 1), c]
    down_far_core = link(far_down, far_down, peer(dc=1))
    down_local.wait()
    down_own_core.wait_recv()
    down_far_core.wait_recv()
    for copy in gu_cores:
        copy.wait_recv()

    po_base = take(3)
    pg_base = take(6)

    def wait_block(block_ref, sem):
        pltpu.make_async_copy(block_ref, block_ref, sem).wait()

    @pl.loop(0, 4)
    def _(i):
        dz, dx = i // 2, i % 2
        cz, cx = flip(z, dz), flip(x, dx)
        chunk = n2_all.at[cz, cx]
        g_chunk = g_all.at[cz, cx]

        @pl.when(i == 1)
        def _():
            n2_x.wait_recv()
            n2_z.wait_recv()
            link(n2_all.at[z, flip(x, 1), 0], n2_all.at[z, flip(x, 1), 0], peer(dz=1), sem=n2_far)
            link(n2_all.at[flip(z, 1), x, 1], n2_all.at[flip(z, 1), x, 1], peer(dx=1), sem=n2_far + 1)

        @pl.when(i == 3)
        def _():
            wait_block(chunk.at[0], rsem.at[n2_far])
            wait_block(chunk.at[1], rsem.at[n2_far + 1])

        @pl.loop(0, tiles)
        def _(t):
            first = pl.multiple_of(t * tile, tile)
            cols = pl.ds(first, tile)
            n2 = chunk[...].reshape(tokens, width)
            gate = dot(n2, wgu_all[:, :, :, :, :, cols].reshape(width, tile))
            up = dot(n2, wgu_all[:, :, :, :, :, pl.ds(block + first, tile)].reshape(width, tile))
            g_act = dot_nt(g_chunk[...].reshape(tokens, width), wd_all[t // 2, t % 2].reshape(tile, width))
            sig = 1.0 / (1.0 + jnp.exp(-gate))
            silu = gate * sig
            shape = (2, 2, rows, tile)
            act_all[cz, cx, :, :, :, cols] = (silu * up).astype(bf16).reshape(shape)
            g_gate = g_act * up * sig * (1.0 + gate * (1.0 - sig))
            ggu_all[cz, cx, :, :, :, cols] = g_gate.astype(bf16).reshape(shape)
            ggu_all[cz, cx, :, :, :, pl.ds(block + first, tile)] = (g_act * silu).astype(bf16).reshape(shape)

        @pl.loop(0, tiles)
        def _(t):
            cols = pl.ds(pl.multiple_of(t * tile, tile), tile)
            shape = (2, 2, rows, tile)
            g_n2 = dot_nt(
                ggu_all[cz, cx].reshape(tokens, 2 * block), wgu_all[t // 2, t % 2].reshape(tile, 2 * block)
            )
            pg_s[cz, cx, :, :, :, cols] = g_n2.astype(bf16).reshape(shape)

        @pl.when(dx == 1)
        def _():
            link(pg_s.at[cz, cx, 0], pg_r.at[dz, 0], peer(dx=1), sem=pg_base + 2 * dz)

        @pl.when(dz == 1)
        def _():
            link(pg_s.at[cz, cx, 1], pg_r.at[dx, 1], peer(dz=1), sem=pg_base + 2 * dx + 1)

        @pl.loop(0, tiles)
        def _(t):
            cols = pl.ds(pl.multiple_of(t * tile, tile), tile)
            shape = (2, 2, rows, tile)
            part = dot(act_all[cz, cx].reshape(tokens, block), wd_all[:, :, :, :, :, cols].reshape(block, tile))
            po_s[cz, cx, :, :, :, cols] = part.astype(bf16).reshape(shape)

        @pl.when(dx == 1)
        def _():
            link(po_s.at[cz, cx], po_r.at[dz], peer(dx=1), sem=po_base + dz)

    for copy in gu_cores + [down_own_core, down_far_core, down_cross]:
        copy.wait_send()
    for copy in (n2_z, n2_x, g_z, g_x, g_zx):
        copy.wait_send()
    wait_block(n2_all.at[z, x, 0], ssem.at[n2_far])
    wait_block(n2_all.at[z, x, 1], ssem.at[n2_far + 1])
    for flips in order:
        ref = wgu_all.at[slab(*flips)]
        pltpu.make_async_copy(ref, ref, ssem.at[gu_sems[flips]]).wait()

    gu_grad = wgu_all

    @pl.loop(0, tiles)
    def _(t):
        cols = pl.ds(pl.multiple_of(t * tile, tile), tile)
        left = n2_all[:, :, :, :, :, cols].reshape(4 * tokens, tile).T

        @pl.loop(0, 2 * block // (2 * tile))
        def _(n):
            wide = pl.ds(pl.multiple_of(n * 2 * tile, 2 * tile), 2 * tile)
            part = dot(left, ggu_all[:, :, :, :, :, wide].reshape(4 * tokens, 2 * tile))
            gu_grad[t // 2, t % 2, :, :, :, wide] = part.astype(bf16).reshape(2, 2, rows, 2 * tile)

    gu_swap = link(gu_grad.at[:, :, :, flip(c, 1)], gu_core, peer(dc=1))

    def add_blocks(ref, came):
        @pl.loop(0, 2)
        def _(m):
            ref[m] = (ref[m].astype(f32) + came[m].astype(f32)).astype(bf16)

    wait_block(pg_r.at[1, 0], rsem.at[pg_base + 2])
    wait_block(pg_r.at[1, 1], rsem.at[pg_base + 3])
    add_blocks(pg_s.at[flip(z, 1), x, 0], pg_r.at[1, 0])
    link(pg_s.at[flip(z, 1), x, 0], pg_r.at[2, 0], peer(dz=1), sem=pg_base + 4)
    add_blocks(pg_s.at[z, flip(x, 1), 1], pg_r.at[1, 1])
    link(pg_s.at[z, flip(x, 1), 1], pg_r.at[2, 1], peer(dx=1), sem=pg_base + 5)

    down_grad = wd_all

    @pl.loop(0, tiles)
    def _(t):
        cols = pl.ds(pl.multiple_of(t * tile, tile), tile)
        left = act_all[:, :, :, :, :, cols].reshape(4 * tokens, tile).T

        @pl.loop(0, width // (2 * tile))
        def _(n):
            wide = pl.ds(pl.multiple_of(n * 2 * tile, 2 * tile), 2 * tile)
            part = dot(left, g_all[:, :, :, :, :, wide].reshape(4 * tokens, 2 * tile))
            down_grad[t // 2, t % 2, :, :, :, wide] = part.astype(bf16).reshape(2, 2, rows, 2 * tile)

    down_swap = link(down_grad.at[:, flip(c, 1)], down_core, peer(dc=1))

    gu_swap.wait_recv()

    @pl.loop(0, 8)
    def _(m):
        at = (m // 4, (m // 2) % 2, m % 2)
        ref = gu_grad.at[at + (c,)]
        ref[...] = (ref[...].astype(f32) + gu_core[at].astype(f32)).astype(bf16)

    def gu_parts(flips):
        j = z * 2 + x
        for u in range(2):
            for part in range(2):
                src = gu_grad.at[slab(*flips) + (slice(None), pl.ds(u * block + part * half, half))]
                cols = pl.ds(pl.multiple_of(u * ff + part * (ff // 2) + j * half, half), half)
                yield src, gu_out.at[flips[0], :, cols]

    gu_sends = []
    for flips in order:
        gu_sends.append(take())
        for src, dst in gu_parts(flips):
            link(src, dst, peer(*flips), sem=gu_sends[-1])
    gu_keep = lsem.at[lcount[0]]
    lcount[0] += 1
    for src, dst in gu_parts((0, 0, 0)):
        pltpu.make_async_copy(src, dst, gu_keep).start()

    down_swap.wait_recv()

    @pl.loop(0, 8)
    def _(m):
        at = (m // 4,)
        rest = ((m // 2) % 2, m % 2)
        ref = down_grad.at[at + (c,) + rest]
        ref[...] = (ref[...].astype(f32) + down_core[at + rest].astype(f32)).astype(bf16)

    down_send = link(down_grad.at[flip(s, 1), c], down_out.at[1], peer(ds=1))
    down_keep = local(down_grad.at[s, c], down_out.at[0])

    wait_block(po_r.at[1], rsem.at[po_base + 1])
    add_blocks(po_s.at[flip(z, 1), x, 0], po_r.at[1, 0])
    add_blocks(po_s.at[flip(z, 1), x, 1], po_r.at[1, 1])
    link(po_s.at[flip(z, 1), x], po_r.at[2], peer(dz=1), sem=po_base + 2)

    for i in (0, 1, 4, 5):
        wait_block(pg_r.at[i // 2, i % 2], rsem.at[pg_base + i])
    gsum_s[...] = jnp.zeros_like(gsum_s)

    def add_gain(which, value):
        for i in range(gsum_s.shape[0]):
            gsum_s[i, which : which + 1, :] += value[:, i * 128 : (i + 1) * 128]

    @pl.loop(0, steps)
    def _(i):
        part = pl.ds(i * rows, rows)
        at = (i // 2, i % 2)
        g_n2 = pg_s[(z, x) + at].astype(f32)
        for k in (0, 2):
            g_n2 += pg_r[(k,) + at].astype(f32)
        hidden = hmid[part]
        inv = r_two[part][:, :1]
        add_gain(1, jnp.sum(g_n2 * hidden * inv, axis=0, keepdims=True))
        scaled = g_n2 * gain_row(1)
        inner = jnp.mean(scaled * hidden, axis=-1, keepdims=True)
        g_sum = cot_ref[part].astype(f32) * mask[part][:, :1]
        g_mid = g_sum + inv * scaled - hidden * (inv * inv * inv * inner)
        gmid[part] = g_mid
        gattn[part] = g_mid.astype(bf16)

    def project_back(left, g, dest):
        @pl.loop(0, tiles)
        def _(t):
            cols = pl.ds(pl.multiple_of(t * tile, tile), tile)
            dest[:, cols] = dot_nt(left[...], wa[g, t // 2, t % 2].reshape(tile, width))

    g_mixed = gwide
    project_back(gattn, OUT, g_mixed)

    @pl.loop(0, steps)
    def _(i):
        part = pl.ds(i * rows, rows)
        gm = g_mixed[part]
        gv_s[part] = (head_spread(p_rem[part]) * gm).astype(bf16)

    gv_copy = link(gv_s, gv_r, f, to_y=1 - y)

    @pl.loop(0, steps)
    def _(i):
        part = pl.ds(i * rows, rows)
        gm = g_mixed[part]
        own, far = p_own[part], p_rem[part]
        gp_own = head_sum(gm * vb[part].astype(f32))
        gp_far = head_sum(gm * vrem[part].astype(f32))
        inner = own * gp_own + far * gp_far
        gs_own = head_spread(own * (gp_own - inner) * scale)
        gs_far = head_spread(far * (gp_far - inner) * scale)
        query = qb[part].astype(f32)
        gk_s[part] = (gs_far * query).astype(bf16)
        gq[part] = (gs_own * kb[part].astype(f32) + gs_far * krem[part].astype(f32)).astype(bf16)
        hold_k[part] = gs_own * query

    gk_copy = link(gk_s, gk_r, f, to_y=1 - y)

    stage = {
        OUT: (act_all, width),
        QUERY: (n2_all, width),
        VALUE: (g_all, width),
        KEY: (ggu_all, width),
    }
    legs = {}

    def grad_view(g, *at):
        ref = stage[g][0]
        if ref.shape[-1] != width:
            return ref.at[at + (slice(None),) * (5 - len(at)) + (pl.ds(0, width),)]
        return ref.at[at]

    def weight_grad(g, left, right):
        @pl.loop(0, tiles)
        def _(t):
            cols = pl.ds(pl.multiple_of(t * tile, tile), tile)
            part = dot(left[:, cols].T, right[...])
            grad_view(g, t // 2, t % 2)[...] = part.astype(bf16).reshape(2, 2, rows, width)

        every = slice(None)
        legs[g] = [link(grad_view(g, every, every, every, flip(c, 1)), attn_core.at[g], peer(dc=1))]

    def add_into(g, count, at_of, came):
        @pl.loop(0, count)
        def _(m):
            ref = grad_view(g, *at_of(m))
            ref[...] = (ref[...].astype(f32) + came(m)[...].astype(f32)).astype(bf16)

    def leg_x(g):
        legs[g][0].wait_recv()
        add_into(
            g, 8, lambda m: (m // 4, (m // 2) % 2, m % 2, c), lambda m: attn_core.at[g, m // 4, (m // 2) % 2, m % 2]
        )
        every = slice(None)
        legs[g].append(link(grad_view(g, every, every, flip(x, 1), c), attn_x.at[g], peer(dx=1)))

    def leg_z(g):
        legs[g][1].wait_recv()
        add_into(g, 4, lambda m: (m // 2, m % 2, x, c), lambda m: attn_x.at[g, m // 2, m % 2])
        every = slice(None)
        legs[g].append(link(grad_view(g, every, flip(z, 1), x, c), attn_z.at[g], peer(dz=1)))

    def leg_cross(g):
        legs[g][2].wait_recv()
        add_into(g, 2, lambda m: (m, z, x, c), lambda m: attn_z.at[g, m])
        cols = pl.ds({QUERY: 0, KEY: 1, VALUE: 2, OUT: 3}[g] * width, width)
        legs[g].append(link(grad_view(g, flip(s, 1), z, x, c), attn_out.at[1, :, cols], peer(ds=1)))
        legs[g].append(local(grad_view(g, s, z, x, c), attn_out.at[0, :, cols]))

    weight_grad(OUT, mixed, gattn)
    weight_grad(QUERY, normed, gq)
    leg_x(OUT)
    leg_x(QUERY)
    gv_copy.wait_recv()

    @pl.loop(0, steps)
    def _(i):
        part = pl.ds(i * rows, rows)
        own = head_spread(p_own[part]) * g_mixed[part]
        gv[part] = (own + gv_r[part].astype(f32)).astype(bf16)

    weight_grad(VALUE, normed, gv)
    leg_x(VALUE)
    gk_copy.wait_recv()

    @pl.loop(0, steps)
    def _(i):
        part = pl.ds(i * rows, rows)
        gk[part] = (hold_k[part] + gk_r[part].astype(f32)).astype(bf16)

    weight_grad(KEY, normed, gk)
    leg_z(OUT)
    leg_x(KEY)
    leg_z(QUERY)
    leg_cross(OUT)

    @pl.loop(0, tiles)
    def _(t):
        cols = pl.ds(pl.multiple_of(t * tile, tile), tile)
        at = (t // 2, t % 2)
        gwide[:, cols] = (
            dot_nt(gq[...], wa[(QUERY,) + at].reshape(tile, width))
            + dot_nt(gk[...], wa[(KEY,) + at].reshape(tile, width))
            + dot_nt(gv[...], wa[(VALUE,) + at].reshape(tile, width))
        )

    @pl.loop(0, steps)
    def _(i):
        part = pl.ds(i * rows, rows)
        hidden = x_ref[part].astype(f32)
        inv = r_one[part][:, :1]
        g_n1 = gwide[part]
        add_gain(0, jnp.sum(g_n1 * hidden * inv, axis=0, keepdims=True))
        scaled = g_n1 * gain_row(0)
        inner = jnp.mean(scaled * hidden, axis=-1, keepdims=True)
        grad = gmid[part] + inv * scaled - hidden * (inv * inv * inv * inner)
        for k in range(width // 128):
            spread = pl.ds(i * rows * (width // 128) + k, rows, width // 128)
            ig_ref[spread, :] = grad[:, k * 128 : (k + 1) * 128]

    def gain_sum_copy(r):
        to = lax.rem(f + r, 16)
        return pltpu.make_async_remote_copy(
            src_ref=gsum_s.at[to // per_block], dst_ref=gsum_r.at[r - 1],
            send_sem=hsem_s.at[r - 1], recv_sem=hsem_r.at[r - 1],
            device_id=(to, y), device_id_type=MESH,
        )

    @pl.loop(1, 16)
    def _(r):
        gain_sum_copy(r).start()

    leg_z(VALUE)
    leg_cross(QUERY)
    leg_z(KEY)
    leg_cross(VALUE)

    for i in (0, 2):
        wait_block(po_r.at[i], rsem.at[po_base + i])

    @pl.loop(0, steps)
    def _(i):
        part = pl.ds(i * rows, rows)
        at = (i // 2, i % 2)
        total = po_s[(z, x) + at].astype(f32)
        for k in (0, 2):
            total += po_r[(k,) + at].astype(f32)
        out_ref[part] = (mask[part][:, :1] * (hmid[part] + total)).astype(bf16)

    leg_cross(KEY)
    gsum_r[15] = gsum_s[f // per_block]

    @pl.loop(1, 16)
    def _(r):
        gain_sum_copy(r).wait()
        gsum_r[15] += gsum_r[r - 1]

    gain_sum = jnp.where(f % per_block == 0, 1.0, 0.0) * gsum_r[15][:, :rows]
    for b in range(1, per_block):
        gain_sum += jnp.where(f % per_block == b, 1.0, 0.0) * gsum_r[15][:, b * rows : (b + 1) * rows]
    gain_one_out[...] = gain_sum[0:1]
    gain_two_out[...] = gain_sum[1:2]

    for copy in keep + [k_copy, v_copy, gv_copy, gk_copy, gu_swap, down_swap]:
        copy.wait_send()
    for i in range(3):
        wait_block(po_r.at[i], ssem.at[po_base + i])
        wait_block(pg_r.at[i, 0], ssem.at[pg_base + 2 * i])
        wait_block(pg_r.at[i, 1], ssem.at[pg_base + 2 * i + 1])
    down_send.wait()
    wait_block(gu_grad.at[slab()], gu_keep)
    for sem in gu_sends:
        wait_block(gu_grad.at[slab()], ssem.at[sem])
        wait_block(gu_grad.at[slab()], rsem.at[sem])
    down_keep.wait()
    for g in (OUT, QUERY, VALUE, KEY):
        for copy in legs[g][:3]:
            copy.wait_send()
        legs[g][3].wait()
        legs[g][4].wait()


def square_layer(inputs, frame_flags, attn_gain, qkv_weight, out_weight, ffn_gain, gate_up_weight, down_weight, cotangent):
    tokens, _, width = inputs.shape
    rows = qkv_weight.shape[2]
    block = width
    f32, bf16 = jnp.float32, jnp.bfloat16
    lane_block = 128
    lane_blocks = width // lane_block
    vmem = pl.BlockSpec(memory_space=pltpu.VMEM)
    anywhere = pl.BlockSpec(memory_space=pl.ANY)
    unit = (2, 2, 2, 2, rows, width)
    double = (2, 2, 2, 2, rows, 2 * block)
    own = (tokens, width)
    scratch = [
        pltpu.VMEM((4,) + unit, bf16),
        pltpu.VMEM(double, bf16),
        pltpu.VMEM(unit, bf16),
        pltpu.VMEM(unit, bf16),
        pltpu.VMEM(unit, bf16),
        pltpu.VMEM(unit, bf16),
        pltpu.VMEM(double, bf16),
        pltpu.VMEM(unit, bf16),
        pltpu.VMEM((3, 2, 2, rows, width), bf16),
        pltpu.VMEM(unit, bf16),
        pltpu.VMEM((3, 2, 2, rows, width), bf16),
        pltpu.VMEM((2, 2, 2, rows, 2 * block), bf16),
        pltpu.VMEM((2, 2, 2, rows, width), bf16),
        pltpu.VMEM((4, 2, 2, 2, rows, width), bf16),
        pltpu.VMEM((4, 2, 2, rows, width), bf16),
        pltpu.VMEM((4, 2, rows, width), bf16),
        pltpu.VMEM(own, bf16),
        pltpu.VMEM(own, bf16),
        pltpu.VMEM(own, bf16),
        pltpu.VMEM(own, bf16),
        pltpu.VMEM(own, bf16),
        pltpu.VMEM(own, bf16),
        pltpu.VMEM(own, bf16),
        pltpu.VMEM(own, f32),
        pltpu.VMEM(own, bf16),
        pltpu.VMEM(own, bf16),
        pltpu.VMEM(own, bf16),
        pltpu.VMEM(own, bf16),
        pltpu.VMEM(own, bf16),
        pltpu.VMEM(own, bf16),
        pltpu.VMEM(own, bf16),
        pltpu.VMEM(own, f32),
        pltpu.VMEM(own, bf16),
        pltpu.VMEM(own, f32),
        pltpu.VMEM(own, f32),
        pltpu.VMEM((tokens, 128), f32),
        pltpu.VMEM((16, lane_block), bf16),
        pltpu.VMEM((tokens, 128), f32),
        pltpu.VMEM((tokens, 128), f32),
        pltpu.VMEM((tokens, 128), f32),
        pltpu.VMEM((tokens, 128), f32),
        pltpu.VMEM((15, 16, lane_block), bf16),
        pltpu.VMEM((lane_blocks, 16, lane_block), f32),
        pltpu.VMEM((lane_blocks, 8, lane_block), f32),
        pltpu.VMEM((16, 8, lane_block), f32),
        pltpu.VMEM((width, 128), bf16),
        pltpu.VMEM((128, width), bf16),
        pltpu.SemaphoreType.DMA((SEMS,)),
        pltpu.SemaphoreType.DMA((SEMS,)),
        pltpu.SemaphoreType.DMA((16,)),
        pltpu.SemaphoreType.DMA((15,)),
        pltpu.SemaphoreType.DMA((15,)),
        pltpu.SemaphoreType.DMA((15,)),
        pltpu.SemaphoreType.DMA((15,)),
    ]
    outs = pl.pallas_call(
        square_kernel,
        out_shape=(
            jax.ShapeDtypeStruct(own, bf16),
            jax.ShapeDtypeStruct((tokens * lane_blocks, lane_block), f32),
            jax.ShapeDtypeStruct((1, rows), f32),
            jax.ShapeDtypeStruct((1, rows), f32),
            jax.ShapeDtypeStruct((2, rows, 8 * block), bf16),
            jax.ShapeDtypeStruct((2, 2, 2, rows, width), bf16),
            jax.ShapeDtypeStruct((2, rows, 4 * width), bf16),
        ),
        in_specs=[vmem] * 5 + [anywhere] * 4,
        out_specs=(vmem, vmem, vmem, vmem, anywhere, anywhere, anywhere),
        scratch_shapes=scratch,
        compiler_params=pltpu.CompilerParams(
            collective_id=0, has_side_effects=True, vmem_limit_bytes=VMEM_BYTES
        ),
        cost_estimate=pl.CostEstimate(flops=26 * 10**9, bytes_accessed=2**23, transcendentals=2**21),
    )(
        inputs[:, 0], cotangent[:, 0], frame_flags.reshape(tokens // lane_block, lane_block), attn_gain[0], ffn_gain[0],
        qkv_weight[0, 0], out_weight[0, 0], gate_up_weight[0, 0], down_weight[0, 0].reshape(2, 2, rows, width),
    )
    result, input_grad, gain_one, gain_two, gu, down, attn = outs

    def both(pair):
        return pair[0].astype(f32) + pair[1].astype(f32)

    return (
        result[:, None],
        input_grad.reshape(tokens, 1, width),
        gain_one[None],
        both(attn[:, :, : 3 * width])[None, None],
        both(attn[:, :, 3 * width :])[None, None],
        gain_two[None],
        both(gu)[None, None],
        both(down).reshape(down_weight.shape),
    )


VMEM_BYTES = 62 * 2**20


def run_layer(axes, *args):
    inputs, qkv_weight, down_weight = args[0], args[3], args[7]
    tokens, places, width = inputs.shape
    rows = qkv_weight.shape[2]
    square = (
        axes["fsdp"] == 16
        and axes["pos"] == 2
        and places == 1
        and qkv_weight.shape[0] == 1
        and tokens == 4 * rows
        and down_weight.shape[2] == 4 * rows
        and 128 % rows == 0
    )
    return square_layer(*args) if square else on_device(*args)


def solution(mesh):
    in_specs = (
        P("fsdp", "pos", None),
        P("fsdp"),
        P(None, "pos", "fsdp"),
        P(None, "pos", "fsdp", None),
        P(None, "pos", "fsdp", None),
        P(None, "pos", "fsdp"),
        P(None, "pos", "fsdp", None),
        P(None, "pos", "fsdp", None),
        P("fsdp", "pos", None),
    )
    out_specs = (
        P("fsdp", "pos", None),
        P("fsdp", "pos", None),
        P(None, "pos", "fsdp"),
        P(None, "pos", "fsdp", None),
        P(None, "pos", "fsdp", None),
        P(None, "pos", "fsdp"),
        P(None, "pos", "fsdp", None),
        P(None, "pos", "fsdp", None),
    )
    return jax.shard_map(
        functools.partial(run_layer, dict(mesh.shape)), mesh=mesh, in_specs=in_specs, out_specs=out_specs, check_vma=False
    )
```

```python
import functools
import math

import jax
import jax.numpy as jnp
from jax import lax
from jax.experimental import pallas as pl
from jax.experimental.pallas import tpu as pltpu
from jax.sharding import PartitionSpec as P

D = 1024
HEADS = 16
HEAD_DIM = 64
FF = 4096


EPSILON = 1e-06
MASKED = -1e30
PRECISE = lax.Precision.HIGHEST


def rms_parts(hidden, gain_row):
    inv_rms = lax.rsqrt(jnp.mean(hidden * hidden, axis=-1, keepdims=True) + EPSILON)
    return (hidden * inv_rms * gain_row[None], inv_rms)


def rms_back(grad_rows, hidden, inv_rms, gain_row):
    scaled = grad_rows * gain_row[None]
    gain_grad = jnp.sum(grad_rows * hidden * inv_rms, axis=0)
    inner_mean = jnp.mean(scaled * hidden, axis=-1, keepdims=True)
    return (inv_rms * scaled - hidden * inv_rms**3 * inner_mean, gain_grad)


def apply_rows(left_side, weight):
    return jnp.einsum("fpd,pde->fpe", left_side, weight, preferred_element_type=jnp.float32)


def apply_back(grad_rows, weight):
    return jnp.einsum("fpe,pde->fpd", grad_rows, weight, preferred_element_type=jnp.float32)


def outer_sum(left_side, grad_rows):
    return jnp.einsum("fpd,fpe->pde", left_side, grad_rows, preferred_element_type=jnp.float32)


def split_heads(rows):
    return rows.reshape(rows.shape[0], rows.shape[1], HEADS, HEAD_DIM)


def attention_weights(attn_gain, qkv_weight, out_weight, layer_idx):
    return (
        lax.all_gather(attn_gain[layer_idx], "fsdp", axis=1, tiled=True),
        lax.all_gather(qkv_weight[layer_idx], "fsdp", axis=1, tiled=True),
        lax.all_gather(out_weight[layer_idx], "fsdp", axis=1, tiled=True),
    )


def ffn_weights(ffn_gain, gate_up_weight, down_weight, layer_idx):
    return (
        lax.all_gather(ffn_gain[layer_idx], "fsdp", axis=1, tiled=True),
        lax.all_gather(gate_up_weight[layer_idx], "fsdp", axis=1, tiled=True),
        lax.all_gather(down_weight[layer_idx], "fsdp", axis=1, tiled=True),
    )


def attention_forward(qkv_rows):
    frames, places = (qkv_rows.shape[0], qkv_rows.shape[1])
    pos_count = lax.axis_size("pos")
    frame_part = frames // pos_count
    outgoing = qkv_rows.reshape(pos_count, frame_part, places, 3 * D)
    frame_qkv = lax.all_to_all(outgoing, "pos", split_axis=0, concat_axis=2, tiled=True)[0].astype(
        jnp.float32
    )
    whole_places = frame_qkv.shape[1]
    queries = split_heads(frame_qkv[..., :D])
    keys_all = split_heads(frame_qkv[..., D : 2 * D])
    values_all = split_heads(frame_qkv[..., 2 * D :])
    scores = jnp.einsum("fphe,fjhe->fhpj", queries, keys_all, precision=PRECISE) / math.sqrt(
        HEAD_DIM
    )
    causal = jnp.arange(whole_places)[:, None] >= jnp.arange(whole_places)[None, :]
    scores = jnp.where(causal, scores, MASKED)
    row_max = jnp.max(scores, axis=-1, keepdims=True)
    exponent = jnp.exp(scores - row_max)
    attn_probs = exponent / jnp.sum(exponent, axis=-1, keepdims=True)
    mixed_heads = jnp.einsum("fhpj,fjhe->fphe", attn_probs, values_all, precision=PRECISE)
    mixed_frames = mixed_heads.reshape(frame_part, whole_places, D).astype(jnp.bfloat16)
    returned = lax.all_to_all(mixed_frames[None], "pos", split_axis=2, concat_axis=0, tiled=True)
    return (returned.reshape(frames, places, D), (queries, keys_all, values_all, attn_probs))


def attention_backward(grad_mixed, attn_keep):
    queries, keys_all, values_all, attn_probs = attn_keep
    frames, places = (grad_mixed.shape[0], grad_mixed.shape[1])
    pos_count = lax.axis_size("pos")
    frame_part = frames // pos_count
    outgoing = grad_mixed.reshape(pos_count, frame_part, places, D)
    grad_frames = lax.all_to_all(
        outgoing.astype(jnp.bfloat16), "pos", split_axis=0, concat_axis=2, tiled=True
    ).astype(outgoing.dtype)[0]
    whole_places = grad_frames.shape[1]
    grad_heads = split_heads(grad_frames)
    grad_values = jnp.einsum("fhpj,fphe->fjhe", attn_probs, grad_heads, precision=PRECISE)
    grad_probs = jnp.einsum("fphe,fjhe->fhpj", grad_heads, values_all, precision=PRECISE)
    grad_scores = (
        attn_probs
        * (grad_probs - jnp.sum(attn_probs * grad_probs, axis=-1, keepdims=True))
        / math.sqrt(HEAD_DIM)
    )
    grad_queries = jnp.einsum("fhpj,fjhe->fphe", grad_scores, keys_all, precision=PRECISE)
    grad_keys = jnp.einsum("fhpj,fphe->fjhe", grad_scores, queries, precision=PRECISE)
    frame_grads = jnp.concatenate(
        [
            grad_queries.reshape(frame_part, whole_places, D),
            grad_keys.reshape(frame_part, whole_places, D),
            grad_values.reshape(frame_part, whole_places, D),
        ],
        axis=-1,
    ).astype(jnp.bfloat16)
    returned = lax.all_to_all(frame_grads[None], "pos", split_axis=2, concat_axis=0, tiled=True)
    return returned.reshape(frames, places, 3 * D)


def layer_forward(hidden, frame_mask, attn_set, ffn_set):
    gain_one, qkv_full, out_full = attn_set
    gain_two, gate_up_full, down_full = ffn_set
    normed, inv_one = rms_parts(hidden, gain_one.astype(jnp.float32))
    normed_low = normed.astype(jnp.bfloat16)
    qkv_rows = apply_rows(normed_low, qkv_full).astype(jnp.bfloat16)
    mixed_low, attn_keep = attention_forward(qkv_rows)
    hidden_mid = hidden + apply_rows(mixed_low, out_full)
    normed_two, inv_two = rms_parts(hidden_mid, gain_two.astype(jnp.float32))
    normed_two_low = normed_two.astype(jnp.bfloat16)
    gate_up = apply_rows(normed_two_low, gate_up_full)
    gate_part = gate_up[..., :FF]
    up_part = gate_up[..., FF:]
    act_low = (jax.nn.silu(gate_part) * up_part).astype(jnp.bfloat16)
    result = frame_mask * (hidden_mid + apply_rows(act_low, down_full))
    kept_state = (
        hidden,
        inv_one,
        normed_low,
        attn_keep,
        mixed_low,
        hidden_mid,
        inv_two,
        normed_two_low,
        gate_part,
        up_part,
        act_low,
    )
    return (result, kept_state)


def layer_backward(grad_out, frame_mask, kept_state, ffn_set, fetch_attn):
    (
        hidden,
        inv_one,
        normed_low,
        attn_keep,
        mixed_low,
        hidden_mid,
        inv_two,
        normed_two_low,
        gate_part,
        up_part,
        act_low,
    ) = kept_state
    gain_two, gate_up_full, down_full = ffn_set
    grad_sum = frame_mask * grad_out
    grad_ffn = grad_sum.astype(jnp.bfloat16)
    down_grad = outer_sum(act_low, grad_ffn)
    down_shard = lax.psum_scatter(down_grad, "fsdp", scatter_dimension=1, tiled=True)
    grad_act = apply_back(grad_ffn, down_full)
    sigmoid_gate = jax.nn.sigmoid(gate_part)
    grad_gate = grad_act * up_part * sigmoid_gate * (1.0 + gate_part * (1.0 - sigmoid_gate))
    grad_up = grad_act * gate_part * sigmoid_gate
    grad_gu = jnp.concatenate([grad_gate, grad_up], axis=-1).astype(jnp.bfloat16)
    gate_up_grad = outer_sum(normed_two_low, grad_gu)
    grad_norm_two = apply_back(grad_gu, gate_up_full)
    grad_mid_norm, gain_two_grad = rms_back(
        grad_norm_two, hidden_mid, inv_two, gain_two.astype(jnp.float32)
    )
    ffn_shards = (
        lax.psum_scatter(gain_two_grad, "fsdp", scatter_dimension=1, tiled=True),
        lax.psum_scatter(gate_up_grad, "fsdp", scatter_dimension=1, tiled=True),
    )
    gain_one, qkv_full, out_full = fetch_attn()
    grad_mid = grad_sum + grad_mid_norm
    grad_attn = grad_mid.astype(jnp.bfloat16)
    out_grad = outer_sum(mixed_low, grad_attn)
    grad_mixed = apply_back(grad_attn, out_full)
    grad_qkv = attention_backward(grad_mixed, attn_keep)
    qkv_grad = outer_sum(normed_low, grad_qkv)
    grad_norm_one = apply_back(grad_qkv, qkv_full)
    grad_in_norm, gain_one_grad = rms_back(
        grad_norm_one, hidden, inv_one, gain_one.astype(jnp.float32)
    )
    attn_shards = (
        lax.psum_scatter(gain_one_grad, "fsdp", scatter_dimension=1, tiled=True),
        lax.psum_scatter(qkv_grad, "fsdp", scatter_dimension=1, tiled=True),
        lax.psum_scatter(out_grad, "fsdp", scatter_dimension=1, tiled=True),
    )
    grad_in = grad_mid + grad_in_norm
    return (
        grad_in,
        (attn_shards[0], attn_shards[1], attn_shards[2], ffn_shards[0], ffn_shards[1], down_shard),
    )


def on_device(
    inputs,
    frame_flags,
    attn_gain,
    qkv_weight,
    out_weight,
    ffn_gain,
    gate_up_weight,
    down_weight,
    cotangent,
):
    layer_total = qkv_weight.shape[0]
    frame_mask = frame_flags.astype(jnp.float32)[:, None, None]
    hidden = inputs.astype(jnp.float32)
    layer_idx = 0
    attn_set = attention_weights(attn_gain, qkv_weight, out_weight, layer_idx)
    ffn_set = ffn_weights(ffn_gain, gate_up_weight, down_weight, layer_idx)
    hidden, kept_state = layer_forward(hidden, frame_mask, attn_set, ffn_set)
    states_all = [kept_state]
    grad_rows = cotangent.astype(jnp.float32)
    layer_grads = [None] * layer_total
    for layer_idx in reversed(range(layer_total)):
        ffn_set = ffn_weights(ffn_gain, gate_up_weight, down_weight, layer_idx)
        fetch_attn = gather_later(attn_gain, qkv_weight, out_weight, layer_idx)
        grad_rows, layer_grads[layer_idx] = layer_backward(
            grad_rows, frame_mask, states_all[layer_idx], ffn_set, fetch_attn
        )
    stacked = [jnp.stack([grad_set[column] for grad_set in layer_grads]) for column in range(6)]
    return (
        hidden.astype(jnp.bfloat16),
        grad_rows,
        stacked[0],
        stacked[1],
        stacked[2],
        stacked[3],
        stacked[4],
        stacked[5],
    )


def gather_later(attn_gain, qkv_weight, out_weight, layer_idx):

    def fetched():
        return attention_weights(attn_gain, qkv_weight, out_weight, layer_idx)

    return fetched


KEY, VALUE, QUERY, OUT = 0, 1, 2, 3
GROUPS = {"k": KEY, "v": VALUE, "q": QUERY, "o": OUT}
SEND_SEMS, RECV_SEMS = 76, 92
ROUTES = {"p0": "z", "p1": "z", "u0": "x", "u1": "x"}
MESH = pl.DeviceIdType.MESH


class Names:
    def __getattr__(self, name):
        return name


step = Names()

ORDER = (
    step.v_to_z, step.k_to_s, step.v_to_x, step.v_to_s, step.k_to_z, step.v_from_z, step.q_to_s, step.k_from_s,
    step.o_to_s, step.g_own, step.q_to_z, step.v_to_c, step.norm, step.k_to_c, step.v_from_s, step.q_to_x,
    step.ends, step.o_to_z, step.o_from_s, step.o_to_x, step.k_from_sz, step.q_from_z, step.gz, step.v_from_sz,
    step.gs, step.k_from_z, step.mask, step.q_from_s, step.k_to_x, step.gd, step.o_to_c, step.v_from_x,
    step.v_from_c, step.gx, step.d_to, step.cz, step.v_rows, step.gs_from, step.q_from_sz, step.cx, step.k_from_x,
    step.q_to_c, step.o_from_sz, step.gx_from, step.q_from_x, step.gd_from, step.q_from_c, step.k_from_c,
    step.gz_from, step.k_rows, step.g_own_from, step.o_from_z, step.czx, step.q_rows, step.attn, step.o_from_x,
    step.o_from_c, step.mid, step.nz, step.d_from, step.gxs_from, step.nx, step.gzs_from, step.gds_from, step.ffn,
    step.nzx, step.f2, step.p0n, step.f1, step.b1, step.u1n, step.p1n, step.f0, step.u0n, step.f3, step.p1f,
    step.b3, step.w11, step.p0f, step.u0f, step.b2, step.y11, step.b0, step.p1t, step.u0t, step.w01, step.p0t,
    step.dg, step.u1f, step.dy, step.gmid, step.gmix, step.Wo, step.w10, step.gk, step.Xo, step.w00, step.y01,
    step.Wq, step.Xq, step.u1t, step.Wv, step.Zo, step.Xv, step.y10, step.Wk, step.Xk, step.Zq, step.out, step.Zv,
    step.Sq, step.ig, step.Zk, step.So, step.Sv, step.y00, step.Sk, step.gain,
)


def flip(bit, change):
    return bit + change - 2 * bit * change


def square_kernel(
    x_in, cot_in, flags_ref, gain_one_ref, gain_two_ref, wqkv, wout, wgu, wd,
    out_hbm, ig_hbm, gain_one_out, gain_two_out, gu_out, down_out, attn_out,
    wa, wgu_all, wd_all, n2_all, g_all, act_all, ggu_all,
    po_s, po_r, pg_s, pg_r, gu_core, gu_cross, down_core, attn_core, attn_x, attn_z,
    normed, qb, kb, vb, krem, vrem, mixed, hmid, gv_s, gk_s, gv_r, gk_r,
    gq, gk, gv, gmid, gattn, hold_k, gwide, mask, gain_ref, p_own, p_rem, r_one, r_two,
    gain_r, gain_f, gsum_s, gsum_r, ends, ends_t,
    x_ref, cot_ref, out_ref, ig_ref, ssem, rsem, lsem, gsem,
):
    tokens, width = x_ref.shape
    rows = width // 16
    block = 4 * width // 4
    half = block // 2
    ff = 4 * width
    f = lax.axis_index("fsdp")
    y = lax.axis_index("pos")
    c = f % 2
    x = (f // 2) % 2
    z = (f // 4) % 2
    s = f // 8
    f32, bf16 = jnp.float32, jnp.bfloat16
    every = slice(None)
    steps = tokens // rows
    tile = 256
    tiles = width // tile
    scale = 1.0 / math.sqrt(HEAD_DIM)
    lane_block = 128
    per_block = lane_block // rows

    def peer(ds=0, dz=0, dx=0, dc=0):
        return flip(s, ds) * 8 + flip(z, dz) * 4 + flip(x, dx) * 2 + flip(c, dc)

    def slab(ds=0, dz=0, dx=0, dc=0):
        return flip(s, ds), flip(z, dz), flip(x, dx), flip(c, dc)

    counter = [0, 0, 0]
    sent = {}
    coming = {}
    actions = {}

    def action(name):
        def keep(fn):
            actions[name] = fn

        return keep

    groups = {}

    def take(which, group=None):
        if group is not None and (which, group) in groups:
            return groups[which, group]
        counter[which] += 1
        assert counter[which] <= (SEND_SEMS, RECV_SEMS)[which]
        groups[which, group] = counter[which] - 1
        return counter[which] - 1

    def link(name, src, dst, to, to_y=None, send_group=None, recv_group=None):
        copy = pltpu.make_async_remote_copy(
            src_ref=src, dst_ref=dst, send_sem=ssem.at[take(0, send_group)], recv_sem=rsem.at[take(1, recv_group)],
            device_id=(to, y if to_y is None else to_y), device_id_type=MESH,
        )
        copy.start()
        if send_group is None:
            sent[name] = copy
        else:
            coming[name] = copy

    def local(name, src, dst):
        counter[2] += 1
        copy = pltpu.make_async_copy(src, dst, lsem.at[counter[2] - 1])
        copy.start()
        sent[name] = copy

    def wait_block(ref, sem):
        pltpu.make_async_copy(ref, ref, sem).wait()

    freed = set()

    def free(*names):
        for name in names:
            if name not in freed:
                freed.add(name)
                sent[name].wait_send()

    def dot(a, b):
        return jnp.dot(a, b, preferred_element_type=f32)

    def dot_nt(a, b):
        return lax.dot_general(a, b, (((1,), (1,)), ((), ())), preferred_element_type=f32)

    def split(v):
        high = v.astype(bf16)
        return high, (v - high.astype(f32)).astype(bf16)

    def head_sum(v):
        high, low = split(v)
        return dot(high, ends[...]) + dot(low, ends[...])

    def head_spread(p):
        high, low = split(p)
        return dot(high, ends_t[...]) + dot(low, ends_t[...])

    def add_rows(ref, came):
        ref[...] = (ref[...].astype(f32) + came[...].astype(f32)).astype(bf16)

    local("x_in", x_in, x_ref)
    local("cot_in", cot_in, cot_ref)

    barrier = pltpu.get_barrier_semaphore()

    @pl.loop(1, 16)
    def _(r):
        pl.semaphore_signal(barrier, inc=1, device_id=(lax.rem(f + r, 16), y), device_id_type=MESH)

    pl.semaphore_signal(barrier, inc=1, device_id=(f, 1 - y), device_id_type=MESH)

    lanes = lax.broadcasted_iota(jnp.int32, gain_ref.shape, 1) // rows == f % per_block
    sublane = lax.broadcasted_iota(jnp.int32, gain_ref.shape, 0)

    def lane_tile(ref):
        return jnp.concatenate([ref[...].astype(f32)] * per_block, axis=1)

    gains = jnp.where(sublane == 0, lane_tile(gain_one_ref), jnp.where(sublane == 1, lane_tile(gain_two_ref), 0.0))
    gain_ref[...] = jnp.where(lanes, gains, 0.0).astype(bf16)

    pl.semaphore_wait(barrier, 16)

    def gain_copy(r):
        return pltpu.make_async_remote_copy(
            src_ref=gain_ref, dst_ref=gain_r.at[r - 1], send_sem=gsem.at[0], recv_sem=gsem.at[1],
            device_id=(lax.rem(f + r, 16), y), device_id_type=MESH,
        )

    def gain_row(which):
        return jnp.concatenate([gain_f[i, which : which + 1, :] for i in range(gain_f.shape[0])], axis=1)

    def add_gain(which, value):
        for i in range(gsum_s.shape[0]):
            gsum_s[i, which : which + 1, :] += value[:, i * 128 : (i + 1) * 128]

    @pl.loop(1, 16)
    def _(r):
        gain_copy(r).start()

    own_cols = (
        wqkv.at[:, pl.ds(width, width)],
        wqkv.at[:, pl.ds(2 * width, width)],
        wqkv.at[:, pl.ds(0, width)],
        wout,
    )
    ways = {"s": (1, 0, 0, 0), "z": (0, 1, 0, 0), "x": (0, 0, 1, 0), "c": (0, 0, 0, 1)}

    def gather_actions(letter, g):
        def send(name, way, src, dst):
            recv_group = letter + "c" if way == "c" else None
            link(letter + name, src, dst, peer(*ways[way]), send_group=letter + way, recv_group=recv_group)

        def own(way):
            @action(letter + "_to_" + way)
            def _():
                send(way, way, own_cols[g], wa.at[(g,) + slab()])
                if way == "c":
                    local(letter + "own", own_cols[g], wa.at[(g,) + slab()])

        for way in ways:
            own(way)

        def pass_on(name, at, way):
            ref = wa.at[(g,) + slab(*at)]
            send(name, way, ref, ref)

        @action(letter + "_from_s")
        def _():
            coming[letter + "s"].wait_recv()
            pass_on("sz", (1, 0, 0, 0), "z")
            pass_on("sx", (1, 0, 0, 0), "x")
            pass_on("sc", (1, 0, 0, 0), "c")

        @action(letter + "_from_z")
        def _():
            coming[letter + "z"].wait_recv()
            pass_on("zx", (0, 1, 0, 0), "x")
            pass_on("zc", (0, 1, 0, 0), "c")

        @action(letter + "_from_sz")
        def _():
            coming[letter + "sz"].wait_recv()
            pass_on("szx", (1, 1, 0, 0), "x")
            pass_on("szc", (1, 1, 0, 0), "c")

        @action(letter + "_from_x")
        def _():
            for name, at in (("x", (0, 0, 1, 0)), ("sx", (1, 0, 1, 0)), ("zx", (0, 1, 1, 0)), ("szx", (1, 1, 1, 0))):
                coming[letter + name].wait_recv()
                pass_on(name + "c", at, "c")

        @action(letter + "_from_c")
        def _():
            sent[letter + "own"].wait()
            wait_block(wa.at[g, :, :, :, flip(c, 1)], rsem.at[take(1, letter + "c")])

    for letter, g in GROUPS.items():
        gather_actions(letter, g)

    @action("ends")
    def _():
        ends[...] = (
            lax.broadcasted_iota(jnp.int32, ends.shape, 0) // HEAD_DIM
            == lax.broadcasted_iota(jnp.int32, ends.shape, 1)
        ).astype(bf16)
        ends_t[...] = (
            lax.broadcasted_iota(jnp.int32, ends_t.shape, 1) // HEAD_DIM
            == lax.broadcasted_iota(jnp.int32, ends_t.shape, 0)
        ).astype(bf16)

    @action("mask")
    def _():
        sent["cot_in"].wait()
        for i in range(tokens // 128):
            flags = flags_ref[i : i + 1, :].astype(f32)
            mask[i * 128 : (i + 1) * 128] = jnp.broadcast_to(flags, (128, 128)).T
        g_all[z, x] = (cot_ref[...].astype(f32) * mask[:, :1]).astype(bf16).reshape(2, 2, rows, width)

    @action("norm")
    def _():
        sent["x_in"].wait()
        gain_f[...] = jnp.zeros_like(gain_f)
        gain_f[f // per_block] += gain_ref[...].astype(f32)

        wait_block(gain_r, gsem.at[0])
        wait_block(gain_r, gsem.at[1])

        @pl.loop(1, 16)
        def _(r):
            gain_f[lax.rem(f + 16 - r, 16) // per_block] += gain_r[r - 1].astype(f32)

        @pl.loop(0, steps, unroll=True)
        def _(i):
            part = pl.ds(i * rows, rows)
            hidden = x_ref[part].astype(f32)
            inv = lax.rsqrt(jnp.mean(hidden * hidden, axis=-1, keepdims=True) + EPSILON)
            r_one[part] = jnp.broadcast_to(inv, (rows, 128))
            normed[part] = (hidden * inv * gain_row(0)).astype(bf16)

    def project(left, g, dest):
        @pl.loop(0, tiles, unroll=True)
        def _(t):
            cols = pl.ds(pl.multiple_of(t * tile, tile), tile)
            dest[:, cols] = dot(left[...], wa[g, :, :, :, :, :, cols].reshape(width, tile)).astype(dest.dtype)

    @action("k_rows")
    def _():
        project(normed, KEY, kb)
        link("key", kb, krem, f, to_y=1 - y)

    @action("v_rows")
    def _():
        project(normed, VALUE, vb)
        link("value", vb, vrem, f, to_y=1 - y)

    @action("q_rows")
    def _():
        project(normed, QUERY, qb)

    blocks = {"s": (1, 0, 0), "x": (0, 0, 1), "z": (0, 1, 0), "d": (0, 1, 1)}
    gu_sems = {}

    def gu_in(flips):
        j = flip(z, flips[1]) * 2 + flip(x, flips[2])
        for u in range(2):
            for part in range(2):
                src = wgu.at[:, pl.ds(pl.multiple_of(u * ff + part * (ff // 2) + j * half, half), half)]
                yield src, wgu_all.at[s, z, x, c, :, pl.ds(u * block + part * half, half)]

    def pieces(flips, pairs):
        sem = take(0), take(1)
        for src, dst in pairs:
            pltpu.make_async_remote_copy(
                src_ref=src, dst_ref=dst, send_sem=ssem.at[sem[0]], recv_sem=rsem.at[sem[1]],
                device_id=(peer(*flips), y), device_id_type=MESH,
            ).start()
        return sem

    def pieces_local(pairs):
        counter[2] += 1
        sem = lsem.at[counter[2] - 1]
        for src, dst in pairs:
            pltpu.make_async_copy(src, dst, sem).start()
        return sem

    def gu_core_send(ref):
        link("gc", ref, ref, peer(dc=1), send_group="g", recv_group="g")

    def gu_actions(way, flips):
        @action("g" + way)
        def _():
            gu_sems[flips] = pieces(flips, gu_in(flips))

        @action("g" + way + "_from")
        def _():
            ref = wgu_all.at[slab(*flips)]
            wait_block(ref, rsem.at[gu_sems[flips][1]])
            if way != "s":
                link("g" + way + "s", ref, ref, peer(ds=1))
            gu_core_send(ref)

        @action("g" + way + "s_from")
        def _():
            sent["g" + way + "s"].wait_recv()
            ref = wgu_all.at[slab(1, flips[1], flips[2])]
            gu_core_send(ref)

    for way, flips in blocks.items():
        gu_actions(way, flips)

    @action("g_own")
    def _():
        gu_sems["own"] = pieces_local(gu_in((0, 0, 0)))

    @action("g_own_from")
    def _():
        ref = wgu_all.at[slab()]
        wait_block(ref, gu_sems["own"])
        gu_core_send(ref)

    @action("d_to")
    def _():
        own = wd_all.at[s, c]
        link("ds", wd, own, peer(ds=1))
        link("dc", wd, own, peer(dc=1))
        local("down", wd, own)

    @action("d_from")
    def _():
        sent["ds"].wait_recv()
        ref = wd_all.at[flip(s, 1), c]
        link("dsc", ref, ref, peer(dc=1))

    @action("ffn")
    def _():
        wait_block(wgu_all.at[:, :, :, flip(c, 1)], rsem.at[take(1, "g")])
        sent["down"].wait()
        sent["dc"].wait_recv()
        sent["dsc"].wait_recv()

    @action("cx")
    def _():
        link("cx", g_all.at[z, x], g_all.at[z, x], peer(dx=1))

    @action("cz")
    def _():
        link("cz", g_all.at[z, x], g_all.at[z, x], peer(dz=1))

    @action("czx")
    def _():
        sent["cz"].wait_recv()
        ref = g_all.at[flip(z, 1), x]
        link("czx", ref, ref, peer(dx=1))

    @action("attn")
    def _():
        sent["key"].wait_recv()
        sent["value"].wait_recv()

        @pl.loop(0, steps, unroll=True)
        def _(i):
            part = pl.ds(i * rows, rows)
            query = qb[part].astype(f32)
            own = head_sum(query * kb[part].astype(f32)) * scale
            far = jnp.where(y > 0, head_sum(query * krem[part].astype(f32)) * scale, MASKED)
            top = jnp.maximum(own, far)
            own = jnp.exp(own - top)
            far = jnp.exp(far - top)
            total = own + far
            own = own / total
            far = far / total
            p_own[part] = own
            p_rem[part] = far
            values = head_spread(own) * vb[part].astype(f32) + head_spread(far) * vrem[part].astype(f32)
            mixed[part] = values.astype(bf16)

    @action("mid")
    def _():
        project(mixed, OUT, hmid)

        @pl.loop(0, steps, unroll=True)
        def _(i):
            part = pl.ds(i * rows, rows)
            hidden = x_ref[part].astype(f32) + hmid[part]
            hmid[part] = hidden
            inv = lax.rsqrt(jnp.mean(hidden * hidden, axis=-1, keepdims=True) + EPSILON)
            r_two[part] = jnp.broadcast_to(inv, (rows, 128))
            n2_all[z, x, i // 2, i % 2] = (hidden * inv * gain_row(1)).astype(bf16)

    @action("nx")
    def _():
        link("nx", n2_all.at[z, x], n2_all.at[z, x], peer(dx=1))

    @action("nz")
    def _():
        link("nz", n2_all.at[z, x], n2_all.at[z, x], peer(dz=1))

    @action("nzx")
    def _():
        sent["nz"].wait_recv()
        ref = n2_all.at[flip(z, 1), x]
        link("nzx", ref, ref, peer(dx=1))

    def chunk_actions(i):
        dz, dx = i // 2, i % 2
        cz, cx = flip(z, dz), flip(x, dx)

        @action("f%d" % i)
        def _():
            if i == 1:
                sent["cx"].wait_recv()
                sent["nx"].wait_recv()
            if i == 3:
                sent["czx"].wait_recv()
                sent["nzx"].wait_recv()

            @pl.loop(0, tiles, unroll=True)
            def _(t):
                first = pl.multiple_of(t * tile, tile)
                cols = pl.ds(first, tile)
                n2 = n2_all[cz, cx].reshape(tokens, width)
                gate = dot(n2, wgu_all[:, :, :, :, :, cols].reshape(width, tile))
                up = dot(n2, wgu_all[:, :, :, :, :, pl.ds(block + first, tile)].reshape(width, tile))
                g_act = dot_nt(g_all[cz, cx].reshape(tokens, width), wd_all[t // 2, t % 2].reshape(tile, width))
                sig = 1.0 / (1.0 + jnp.exp(-gate))
                silu = gate * sig
                shape = (2, 2, rows, tile)
                act_all[cz, cx, :, :, :, cols] = (silu * up).astype(bf16).reshape(shape)
                g_gate = g_act * up * sig * (1.0 + gate * (1.0 - sig))
                ggu_all[cz, cx, :, :, :, cols] = g_gate.astype(bf16).reshape(shape)
                ggu_all[cz, cx, :, :, :, pl.ds(block + first, tile)] = (g_act * silu).astype(bf16).reshape(shape)

            @pl.loop(0, tiles, unroll=True)
            def _(t):
                cols = pl.ds(pl.multiple_of(t * tile, tile), tile)
                g_n2 = dot_nt(
                    ggu_all[cz, cx].reshape(tokens, 2 * block), wgu_all[t // 2, t % 2].reshape(tile, 2 * block)
                )
                pg_s[cz, cx, :, :, :, cols] = g_n2.astype(bf16).reshape(2, 2, rows, tile)

        @action("b%d" % i)
        def _():
            @pl.loop(0, tiles, unroll=True)
            def _(t):
                cols = pl.ds(pl.multiple_of(t * tile, tile), tile)
                part = dot(act_all[cz, cx].reshape(tokens, block), wd_all[:, :, :, :, :, cols].reshape(block, tile))
                po_s[cz, cx, :, :, :, cols] = part.astype(bf16).reshape(2, 2, rows, tile)

    for i in range(4):
        chunk_actions(i)

    def sum_actions(name, sums, came, h, way):
        first = {"x": (0, 1), "z": (1, 0)}[way]
        second = (first[1], first[0])
        one, two = peer(0, *first), peer(0, *second)

        def part(flips):
            return sums.at[flip(z, flips[0]), flip(x, flips[1]), h]

        @action(name + "n")
        def _():
            link(name + "n", part(first), came.at[0, h], one)

        @action(name + "f")
        def _():
            link(name + "f", part((1, 1)), came.at[1, h], one)

        @action(name + "t")
        def _():
            sent[name + "f"].wait_recv()

            @pl.loop(0, 2, unroll=True)
            def _(m):
                add_rows(part(second).at[m], came.at[1, h, m])

            link(name + "t", part(second), came.at[2, h], two)

    for name, way in ROUTES.items():
        sums, came = (pg_s, pg_r) if name[0] == "p" else (po_s, po_r)
        sum_actions(name, sums, came, int(name[1]), way)

    gu_grad = wgu_all
    down_grad = wd_all

    def gu_grad_out(flips):
        j = z * 2 + x
        for u in range(2):
            for part in range(2):
                src = gu_grad.at[slab(*flips) + (every, pl.ds(u * block + part * half, half))]
                cols = pl.ds(pl.multiple_of(u * ff + part * (ff // 2) + j * half, half), half)
                yield src, gu_out.at[:, cols]

    def tile_actions(ds, dz):
        tag = "%d%d" % (ds, dz)
        at = flip(s, ds), flip(z, dz)

        @action("w" + tag)
        def _():
            free("gxs", "gzs", "gds")
            if "gc" not in freed:
                freed.add("gc")
                wait_block(wgu_all.at[:, :, :, c], ssem.at[take(0, "g")])
            left = n2_all[:, :, :, :, :, pl.ds(pl.multiple_of((at[0] * 2 + at[1]) * tile, tile), tile)]
            left = left.reshape(4 * tokens, tile).T

            @pl.loop(0, block // tile, unroll=True)
            def _(n):
                wide = pl.ds(pl.multiple_of(n * 2 * tile, 2 * tile), 2 * tile)
                part = dot(left, ggu_all[:, :, :, :, :, wide].reshape(4 * tokens, 2 * tile))
                gu_grad[at[0], at[1], :, :, :, wide] = part.astype(bf16).reshape(2, 2, rows, 2 * tile)

            link("w" + tag, gu_grad.at[at[0], at[1], :, flip(c, 1)], gu_core.at[at], peer(dc=1))

        @action("y" + tag)
        def _():
            sent["w" + tag].wait_recv()
            if ds == 0:
                sent["y1%d" % dz].wait_recv()

            @pl.loop(0, 2, unroll=True)
            def _(m):
                ref = gu_grad.at[at[0], at[1], m, c]
                total = ref[...].astype(f32) + gu_core[at[0], at[1], m].astype(f32)
                if ds == 0:
                    total += gu_cross[at[1], m].astype(f32)
                ref[...] = total.astype(bf16)

            if ds == 1:
                link("y" + tag, gu_grad.at[at[0], at[1], :, c], gu_cross.at[at[1]], peer(ds=1))
                return
            for dx in (1, 0):
                flips = (0, dz, dx)
                if flips == (0, 0, 0):
                    gu_sems["keep"] = pieces_local(gu_grad_out(flips))
                else:
                    gu_sems[flips + (0,)] = pieces(flips, gu_grad_out(flips))

    for ds in (0, 1):
        for dz in (0, 1):
            tile_actions(ds, dz)

    @action("dg")
    def _():
        free("dsc")

        @pl.loop(0, tiles, unroll=True)
        def _(t):
            cols = pl.ds(pl.multiple_of(t * tile, tile), tile)
            left = act_all[:, :, :, :, :, cols].reshape(4 * tokens, tile).T

            @pl.loop(0, width // (2 * tile), unroll=True)
            def _(n):
                wide = pl.ds(pl.multiple_of(n * 2 * tile, 2 * tile), 2 * tile)
                part = dot(left, g_all[:, :, :, :, :, wide].reshape(4 * tokens, 2 * tile))
                down_grad[t // 2, t % 2, :, :, :, wide] = part.astype(bf16).reshape(2, 2, rows, 2 * tile)

        link("dg", down_grad.at[:, flip(c, 1)], down_core, peer(dc=1))

    @action("dy")
    def _():
        sent["dg"].wait_recv()

        @pl.loop(0, 8, unroll=2)
        def _(m):
            rest = ((m // 2) % 2, m % 2)
            add_rows(down_grad.at[(m // 4, c) + rest], down_core.at[(m // 4,) + rest])

        link("dy", down_grad.at[flip(s, 1), c], down_out.at[1], peer(ds=1))
        local("dkeep", down_grad.at[s, c], down_out.at[0])

    @action("gmid")
    def _():
        for name in ("p0n", "p1n", "p0t", "p1t"):
            sent[name].wait_recv()
        gsum_s[...] = jnp.zeros_like(gsum_s)

        @pl.loop(0, steps, unroll=True)
        def _(i):
            part = pl.ds(i * rows, rows)
            at = (i // 2, i % 2)
            g_n2 = pg_s[(z, x) + at].astype(f32)
            for k in (0, 2):
                g_n2 += pg_r[(k,) + at].astype(f32)
            hidden = hmid[part]
            inv = r_two[part][:, :1]
            add_gain(1, jnp.sum(g_n2 * hidden * inv, axis=0, keepdims=True))
            scaled = g_n2 * gain_row(1)
            inner = jnp.mean(scaled * hidden, axis=-1, keepdims=True)
            g_sum = cot_ref[part].astype(f32) * mask[part][:, :1]
            g_mid = g_sum + inv * scaled - hidden * (inv * inv * inv * inner)
            gmid[part] = g_mid
            gattn[part] = g_mid.astype(bf16)

    @action("gmix")
    def _():
        @pl.loop(0, tiles, unroll=True)
        def _(t):
            cols = pl.ds(pl.multiple_of(t * tile, tile), tile)
            gwide[:, cols] = dot_nt(gattn[...], wa[OUT, t // 2, t % 2].reshape(tile, width))

        @pl.loop(0, steps, unroll=True)
        def _(i):
            part = pl.ds(i * rows, rows)
            gv_s[part] = (head_spread(p_rem[part]) * gwide[part]).astype(bf16)

        link("gv", gv_s, gv_r, f, to_y=1 - y)

    @action("gk")
    def _():
        @pl.loop(0, steps, unroll=True)
        def _(i):
            part = pl.ds(i * rows, rows)
            gm = gwide[part]
            own, far = p_own[part], p_rem[part]
            gp_own = head_sum(gm * vb[part].astype(f32))
            gp_far = head_sum(gm * vrem[part].astype(f32))
            inner = own * gp_own + far * gp_far
            gs_own = head_spread(own * (gp_own - inner) * scale)
            gs_far = head_spread(far * (gp_far - inner) * scale)
            query = qb[part].astype(f32)
            gk_s[part] = (gs_far * query).astype(bf16)
            gq[part] = (gs_own * kb[part].astype(f32) + gs_far * krem[part].astype(f32)).astype(bf16)
            hold_k[part] = gs_own * query

        link("gk", gk_s, gk_r, f, to_y=1 - y)

    stage = {OUT: act_all, QUERY: n2_all, VALUE: g_all, KEY: ggu_all}
    out_cols = {QUERY: 0, KEY: 1, VALUE: 2, OUT: 3}

    def grad_actions(letter, g):
        def view(*at):
            ref = stage[g]
            if ref.shape[-1] != width:
                return ref.at[at + (every,) * (5 - len(at)) + (pl.ds(0, width),)]
            return ref.at[at]

        def add_into(count, at_of, came):
            @pl.loop(0, count, unroll=2)
            def _(m):
                add_rows(view(*at_of(m)), came(m))

        def weight_grad(left, right):
            @pl.loop(0, tiles, unroll=True)
            def _(t):
                cols = pl.ds(pl.multiple_of(t * tile, tile), tile)
                part = dot(left[:, cols].T, right[...])
                view(t // 2, t % 2)[...] = part.astype(bf16).reshape(2, 2, rows, width)

            link("W" + letter, view(every, every, every, flip(c, 1)), attn_core.at[g], peer(dc=1))

        @action("W" + letter)
        def _():
            if g == OUT:
                weight_grad(mixed, gattn)
            elif g == QUERY:
                free("nx", "nz", "nzx")
                weight_grad(normed, gq)
            elif g == VALUE:
                free("cx", "cz", "czx")
                sent["gv"].wait_recv()

                @pl.loop(0, steps, unroll=True)
                def _(i):
                    part = pl.ds(i * rows, rows)
                    gv[part] = (head_spread(p_own[part]) * gwide[part] + gv_r[part].astype(f32)).astype(bf16)

                weight_grad(normed, gv)
            else:
                sent["gk"].wait_recv()

                @pl.loop(0, steps, unroll=True)
                def _(i):
                    part = pl.ds(i * rows, rows)
                    gk[part] = (hold_k[part] + gk_r[part].astype(f32)).astype(bf16)

                weight_grad(normed, gk)

        @action("X" + letter)
        def _():
            sent["W" + letter].wait_recv()
            add_into(
                8,
                lambda m: (m // 4, (m // 2) % 2, m % 2, c),
                lambda m: attn_core.at[g, m // 4, (m // 2) % 2, m % 2],
            )
            link("X" + letter, view(every, every, flip(x, 1), c), attn_x.at[g], peer(dx=1))

        @action("Z" + letter)
        def _():
            sent["X" + letter].wait_recv()
            add_into(4, lambda m: (m // 2, m % 2, x, c), lambda m: attn_x.at[g, m // 2, m % 2])
            link("Z" + letter, view(every, flip(z, 1), x, c), attn_z.at[g], peer(dz=1))

        @action("S" + letter)
        def _():
            sent["Z" + letter].wait_recv()
            add_into(2, lambda m: (m, z, x, c), lambda m: attn_z.at[g, m])
            cols = pl.ds(out_cols[g] * width, width)
            link("S" + letter, view(flip(s, 1), z, x, c), attn_out.at[1, :, cols], peer(ds=1))
            local("keep" + letter, view(s, z, x, c), attn_out.at[0, :, cols])

    for letter, g in GROUPS.items():
        grad_actions(letter, g)

    def gain_sum_copy(r):
        to = lax.rem(f + r, 16)
        return pltpu.make_async_remote_copy(
            src_ref=gsum_s.at[to // per_block], dst_ref=gsum_r.at[r - 1],
            send_sem=gsem.at[2], recv_sem=gsem.at[3],
            device_id=(to, y), device_id_type=MESH,
        )

    @action("ig")
    def _():
        @pl.loop(0, tiles, unroll=True)
        def _(t):
            cols = pl.ds(pl.multiple_of(t * tile, tile), tile)
            at = (t // 2, t % 2)
            gwide[:, cols] = (
                dot_nt(gq[...], wa[(QUERY,) + at].reshape(tile, width))
                + dot_nt(gk[...], wa[(KEY,) + at].reshape(tile, width))
                + dot_nt(gv[...], wa[(VALUE,) + at].reshape(tile, width))
            )

        @pl.loop(0, steps, unroll=True)
        def _(i):
            part = pl.ds(i * rows, rows)
            hidden = x_ref[part].astype(f32)
            inv = r_one[part][:, :1]
            g_n1 = gwide[part]
            add_gain(0, jnp.sum(g_n1 * hidden * inv, axis=0, keepdims=True))
            scaled = g_n1 * gain_row(0)
            inner = jnp.mean(scaled * hidden, axis=-1, keepdims=True)
            grad = gmid[part] + inv * scaled - hidden * (inv * inv * inv * inner)
            for k in range(width // 128):
                spread = pl.ds(i * rows * (width // 128) + k, rows, width // 128)
                ig_ref[spread, :] = grad[:, k * 128 : (k + 1) * 128]

        local("keep_ig", ig_ref, ig_hbm)

        @pl.loop(1, 16)
        def _(r):
            gain_sum_copy(r).start()

    @action("gain")
    def _():
        gsum_r[15] = gsum_s[f // per_block]

        wait_block(gsum_r.at[pl.ds(0, 15)], gsem.at[2])
        wait_block(gsum_r.at[pl.ds(0, 15)], gsem.at[3])

        @pl.loop(1, 16)
        def _(r):
            gsum_r[15] += gsum_r[r - 1]

        gain_sum = jnp.where(f % per_block == 0, 1.0, 0.0) * gsum_r[15][:, :rows]
        for b in range(1, per_block):
            gain_sum += jnp.where(f % per_block == b, 1.0, 0.0) * gsum_r[15][:, b * rows : (b + 1) * rows]
        gain_one_out[...] = gain_sum[0:1]
        gain_two_out[...] = gain_sum[1:2]

    @action("out")
    def _():
        for name in ("u0n", "u1n", "u0t", "u1t"):
            sent[name].wait_recv()

        @pl.loop(0, steps, unroll=True)
        def _(i):
            part = pl.ds(i * rows, rows)
            at = (i // 2, i % 2)
            total = po_s[(z, x) + at].astype(f32)
            for k in (0, 2):
                total += po_r[(k,) + at].astype(f32)
            out_ref[part] = (mask[part][:, :1] * (hmid[part] + total)).astype(bf16)

        local("keep_out", out_ref, out_hbm)

    for name in ORDER:
        actions[name]()

    for letter in GROUPS:
        sent["S" + letter].wait_recv()
        sent["keep" + letter].wait()
    sent["dy"].wait_recv()
    sent["dkeep"].wait()
    wait_block(gu_grad.at[slab()], gu_sems["keep"])
    for flips in blocks.values():
        wait_block(wgu_all.at[slab()], ssem.at[gu_sems[flips][0]])
        if flips[0] == 0:
            wait_block(gu_grad.at[slab()], ssem.at[gu_sems[flips + (0,)][0]])
            wait_block(gu_grad.at[slab()], rsem.at[gu_sems[flips + (0,)][1]])
    sent["keep_out"].wait()
    sent["keep_ig"].wait()
    for letter, g in GROUPS.items():
        wait_block(wa.at[g, :, :, :, c], ssem.at[take(0, letter + "c")])
        wait_block(wa.at[g, :, :, x, c], ssem.at[take(0, letter + "x")])
        wait_block(wa.at[g, :, z, x, c], ssem.at[take(0, letter + "z")])
        wait_block(wa.at[(g,) + slab()], ssem.at[take(0, letter + "s")])
    free(*(name for name in sent if name not in ("down", "x_in", "cot_in") and not name.startswith(("keep", "dkeep"))
           and not name.endswith("own")))


def square_layer(inputs, frame_flags, attn_gain, qkv_weight, out_weight, ffn_gain, gate_up_weight, down_weight, cotangent):
    tokens, _, width = inputs.shape
    rows = qkv_weight.shape[2]
    block = width
    f32, bf16 = jnp.float32, jnp.bfloat16
    lane_block = 128
    lane_blocks = width // lane_block
    vmem = pl.BlockSpec(memory_space=pltpu.VMEM)
    anywhere = pl.BlockSpec(memory_space=pl.ANY)
    unit = (2, 2, 2, 2, rows, width)
    double = (2, 2, 2, 2, rows, 2 * block)
    own = (tokens, width)
    scratch = [
        pltpu.VMEM((4,) + unit, bf16),
        pltpu.VMEM(double, bf16),
        pltpu.VMEM(unit, bf16),
        pltpu.VMEM(unit, bf16),
        pltpu.VMEM(unit, bf16),
        pltpu.VMEM(unit, bf16),
        pltpu.VMEM(double, bf16),
        pltpu.VMEM(unit, bf16),
        pltpu.VMEM((3, 2, 2, rows, width), bf16),
        pltpu.VMEM(unit, bf16),
        pltpu.VMEM((3, 2, 2, rows, width), bf16),
        pltpu.VMEM((2, 2, 2, rows, 2 * block), bf16),
        pltpu.VMEM((2, 2, rows, 2 * block), bf16),
        pltpu.VMEM((2, 2, 2, rows, width), bf16),
        pltpu.VMEM((4, 2, 2, 2, rows, width), bf16),
        pltpu.VMEM((4, 2, 2, rows, width), bf16),
        pltpu.VMEM((4, 2, rows, width), bf16),
        pltpu.VMEM(own, bf16),
        pltpu.VMEM(own, bf16),
        pltpu.VMEM(own, bf16),
        pltpu.VMEM(own, bf16),
        pltpu.VMEM(own, bf16),
        pltpu.VMEM(own, bf16),
        pltpu.VMEM(own, bf16),
        pltpu.VMEM(own, f32),
        pltpu.VMEM(own, bf16),
        pltpu.VMEM(own, bf16),
        pltpu.VMEM(own, bf16),
        pltpu.VMEM(own, bf16),
        pltpu.VMEM(own, bf16),
        pltpu.VMEM(own, bf16),
        pltpu.VMEM(own, bf16),
        pltpu.VMEM(own, f32),
        pltpu.VMEM(own, bf16),
        pltpu.VMEM(own, f32),
        pltpu.VMEM(own, f32),
        pltpu.VMEM((tokens, 128), f32),
        pltpu.VMEM((16, lane_block), bf16),
        pltpu.VMEM((tokens, 128), f32),
        pltpu.VMEM((tokens, 128), f32),
        pltpu.VMEM((tokens, 128), f32),
        pltpu.VMEM((tokens, 128), f32),
        pltpu.VMEM((15, 16, lane_block), bf16),
        pltpu.VMEM((lane_blocks, 16, lane_block), f32),
        pltpu.VMEM((lane_blocks, 8, lane_block), f32),
        pltpu.VMEM((16, 8, lane_block), f32),
        pltpu.VMEM((width, 128), bf16),
        pltpu.VMEM((128, width), bf16),
        pltpu.VMEM(own, bf16),
        pltpu.VMEM(own, bf16),
        pltpu.VMEM(own, bf16),
        pltpu.VMEM((tokens * lane_blocks, lane_block), f32),
        pltpu.SemaphoreType.DMA((SEND_SEMS,)),
        pltpu.SemaphoreType.DMA((RECV_SEMS,)),
        pltpu.SemaphoreType.DMA((16,)),
        pltpu.SemaphoreType.DMA((4,)),
    ]
    outs = pl.pallas_call(
        square_kernel,
        out_shape=(
            jax.ShapeDtypeStruct(own, bf16),
            jax.ShapeDtypeStruct((tokens * lane_blocks, lane_block), f32),
            jax.ShapeDtypeStruct((1, rows), f32),
            jax.ShapeDtypeStruct((1, rows), f32),
            jax.ShapeDtypeStruct((rows, 8 * block), bf16),
            jax.ShapeDtypeStruct((2, 2, 2, rows, width), bf16),
            jax.ShapeDtypeStruct((2, rows, 4 * width), bf16),
        ),
        in_specs=[anywhere] * 2 + [vmem] * 3 + [anywhere] * 4,
        out_specs=(anywhere, anywhere, vmem, vmem, anywhere, anywhere, anywhere),
        scratch_shapes=scratch,
        compiler_params=pltpu.CompilerParams(
            collective_id=0, has_side_effects=True, vmem_limit_bytes=VMEM_BYTES
        ),
        cost_estimate=pl.CostEstimate(flops=26 * 10**9, bytes_accessed=2**23, transcendentals=2**21),
    )(
        inputs[:, 0], cotangent[:, 0], frame_flags.reshape(tokens // lane_block, lane_block), attn_gain[0], ffn_gain[0],
        qkv_weight[0, 0], out_weight[0, 0], gate_up_weight[0, 0], down_weight[0, 0].reshape(2, 2, rows, width),
    )
    result, input_grad, gain_one, gain_two, gu, down, attn = outs
    grid = 2

    def by_rows(shape):
        return pl.BlockSpec((shape[0] // grid,) + shape[1:], lambda i: (i, 0))

    def pair(shape):
        return pl.BlockSpec((2, shape[0] // grid) + shape[1:], lambda i: (0, i, 0))

    whole = pl.BlockSpec((1, rows), lambda i: (0, 0))
    thin = (tokens * lane_blocks, lane_block)
    result, input_grad, qkv, out, gu, down, gain_one, gain_two = pl.pallas_call(
        finish_kernel,
        grid=(grid,),
        out_shape=(
            jax.ShapeDtypeStruct(own, bf16),
            jax.ShapeDtypeStruct(thin, f32),
            jax.ShapeDtypeStruct((rows, 3 * width), f32),
            jax.ShapeDtypeStruct((rows, width), f32),
            jax.ShapeDtypeStruct((rows, 8 * block), f32),
            jax.ShapeDtypeStruct(own, f32),
            jax.ShapeDtypeStruct((1, rows), f32),
            jax.ShapeDtypeStruct((1, rows), f32),
        ),
        in_specs=[by_rows(own), by_rows(thin), whole, whole, by_rows((rows, 8 * block)), pair(own), pair((rows, 4 * width))],
        out_specs=[by_rows(own), by_rows(thin), by_rows((rows, 3 * width)), by_rows((rows, width)),
                   by_rows((rows, 8 * block)), by_rows(own), whole, whole],
        compiler_params=pltpu.CompilerParams(vmem_limit_bytes=VMEM_BYTES),
    )(result, input_grad, gain_one, gain_two, gu, down.reshape((2,) + own), attn)
    return (
        result[:, None],
        input_grad.reshape(tokens, 1, width),
        gain_one[None],
        qkv[None, None],
        out[None, None],
        gain_two[None],
        gu[None, None],
        down[None, None],
    )


def finish_kernel(
    result, input_grad, gain_one, gain_two, gu, down, attn,
    result_out, input_grad_out, qkv_out, out_out, gu_out, down_out, gain_one_out, gain_two_out,
):
    f32 = jnp.float32
    width = out_out.shape[1]
    result_out[...] = result[...]
    input_grad_out[...] = input_grad[...]
    gu_out[...] = gu[...].astype(f32)
    down_out[...] = down[0].astype(f32) + down[1].astype(f32)
    total = attn[0].astype(f32) + attn[1].astype(f32)
    qkv_out[...] = total[:, : 3 * width]
    out_out[...] = total[:, 3 * width :]
    gain_one_out[...] = gain_one[...]
    gain_two_out[...] = gain_two[...]


VMEM_BYTES = 62 * 2**20


def run_layer(axes, *args):
    inputs, qkv_weight, down_weight = args[0], args[3], args[7]
    tokens, places, width = inputs.shape
    rows = qkv_weight.shape[2]
    square = (
        axes["fsdp"] == 16
        and axes["pos"] == 2
        and places == 1
        and qkv_weight.shape[0] == 1
        and tokens == 4 * rows
        and down_weight.shape[2] == 4 * rows
        and 128 % rows == 0
    )
    return square_layer(*args) if square else on_device(*args)


def solution(mesh):
    in_specs = (
        P("fsdp", "pos", None),
        P("fsdp"),
        P(None, "pos", "fsdp"),
        P(None, "pos", "fsdp", None),
        P(None, "pos", "fsdp", None),
        P(None, "pos", "fsdp"),
        P(None, "pos", "fsdp", None),
        P(None, "pos", "fsdp", None),
        P("fsdp", "pos", None),
    )
    out_specs = (
        P("fsdp", "pos", None),
        P("fsdp", "pos", None),
        P(None, "pos", "fsdp"),
        P(None, "pos", "fsdp", None),
        P(None, "pos", "fsdp", None),
        P(None, "pos", "fsdp"),
        P(None, "pos", "fsdp", None),
        P(None, "pos", "fsdp", None),
    )
    return jax.shard_map(
        functools.partial(run_layer, dict(mesh.shape)), mesh=mesh, in_specs=in_specs, out_specs=out_specs, check_vma=False
    )
```

```python
import functools
import math

import jax
import jax.numpy as jnp
from jax import lax
from jax.experimental import pallas as pl
from jax.experimental.pallas import tpu as pltpu
from jax.sharding import PartitionSpec as P

D = 1024
HEADS = 16
HEAD_DIM = 64
FF = 4096


EPSILON = 1e-06
MASKED = -1e30
PRECISE = lax.Precision.HIGHEST


def rms_parts(hidden, gain_row):
    inv_rms = lax.rsqrt(jnp.mean(hidden * hidden, axis=-1, keepdims=True) + EPSILON)
    return (hidden * inv_rms * gain_row[None], inv_rms)


def rms_back(grad_rows, hidden, inv_rms, gain_row):
    scaled = grad_rows * gain_row[None]
    gain_grad = jnp.sum(grad_rows * hidden * inv_rms, axis=0)
    inner_mean = jnp.mean(scaled * hidden, axis=-1, keepdims=True)
    return (inv_rms * scaled - hidden * inv_rms**3 * inner_mean, gain_grad)


def apply_rows(left_side, weight):
    return jnp.einsum("fpd,pde->fpe", left_side, weight, preferred_element_type=jnp.float32)


def apply_back(grad_rows, weight):
    return jnp.einsum("fpe,pde->fpd", grad_rows, weight, preferred_element_type=jnp.float32)


def outer_sum(left_side, grad_rows):
    return jnp.einsum("fpd,fpe->pde", left_side, grad_rows, preferred_element_type=jnp.float32)


def split_heads(rows):
    return rows.reshape(rows.shape[0], rows.shape[1], HEADS, HEAD_DIM)


def attention_weights(attn_gain, qkv_weight, out_weight, layer_idx):
    return (
        lax.all_gather(attn_gain[layer_idx], "fsdp", axis=1, tiled=True),
        lax.all_gather(qkv_weight[layer_idx], "fsdp", axis=1, tiled=True),
        lax.all_gather(out_weight[layer_idx], "fsdp", axis=1, tiled=True),
    )


def ffn_weights(ffn_gain, gate_up_weight, down_weight, layer_idx):
    return (
        lax.all_gather(ffn_gain[layer_idx], "fsdp", axis=1, tiled=True),
        lax.all_gather(gate_up_weight[layer_idx], "fsdp", axis=1, tiled=True),
        lax.all_gather(down_weight[layer_idx], "fsdp", axis=1, tiled=True),
    )


def attention_forward(qkv_rows):
    frames, places = (qkv_rows.shape[0], qkv_rows.shape[1])
    pos_count = lax.axis_size("pos")
    frame_part = frames // pos_count
    outgoing = qkv_rows.reshape(pos_count, frame_part, places, 3 * D)
    frame_qkv = lax.all_to_all(outgoing, "pos", split_axis=0, concat_axis=2, tiled=True)[0].astype(
        jnp.float32
    )
    whole_places = frame_qkv.shape[1]
    queries = split_heads(frame_qkv[..., :D])
    keys_all = split_heads(frame_qkv[..., D : 2 * D])
    values_all = split_heads(frame_qkv[..., 2 * D :])
    scores = jnp.einsum("fphe,fjhe->fhpj", queries, keys_all, precision=PRECISE) / math.sqrt(
        HEAD_DIM
    )
    causal = jnp.arange(whole_places)[:, None] >= jnp.arange(whole_places)[None, :]
    scores = jnp.where(causal, scores, MASKED)
    row_max = jnp.max(scores, axis=-1, keepdims=True)
    exponent = jnp.exp(scores - row_max)
    attn_probs = exponent / jnp.sum(exponent, axis=-1, keepdims=True)
    mixed_heads = jnp.einsum("fhpj,fjhe->fphe", attn_probs, values_all, precision=PRECISE)
    mixed_frames = mixed_heads.reshape(frame_part, whole_places, D).astype(jnp.bfloat16)
    returned = lax.all_to_all(mixed_frames[None], "pos", split_axis=2, concat_axis=0, tiled=True)
    return (returned.reshape(frames, places, D), (queries, keys_all, values_all, attn_probs))


def attention_backward(grad_mixed, attn_keep):
    queries, keys_all, values_all, attn_probs = attn_keep
    frames, places = (grad_mixed.shape[0], grad_mixed.shape[1])
    pos_count = lax.axis_size("pos")
    frame_part = frames // pos_count
    outgoing = grad_mixed.reshape(pos_count, frame_part, places, D)
    grad_frames = lax.all_to_all(
        outgoing.astype(jnp.bfloat16), "pos", split_axis=0, concat_axis=2, tiled=True
    ).astype(outgoing.dtype)[0]
    whole_places = grad_frames.shape[1]
    grad_heads = split_heads(grad_frames)
    grad_values = jnp.einsum("fhpj,fphe->fjhe", attn_probs, grad_heads, precision=PRECISE)
    grad_probs = jnp.einsum("fphe,fjhe->fhpj", grad_heads, values_all, precision=PRECISE)
    grad_scores = (
        attn_probs
        * (grad_probs - jnp.sum(attn_probs * grad_probs, axis=-1, keepdims=True))
        / math.sqrt(HEAD_DIM)
    )
    grad_queries = jnp.einsum("fhpj,fjhe->fphe", grad_scores, keys_all, precision=PRECISE)
    grad_keys = jnp.einsum("fhpj,fphe->fjhe", grad_scores, queries, precision=PRECISE)
    frame_grads = jnp.concatenate(
        [
            grad_queries.reshape(frame_part, whole_places, D),
            grad_keys.reshape(frame_part, whole_places, D),
            grad_values.reshape(frame_part, whole_places, D),
        ],
        axis=-1,
    ).astype(jnp.bfloat16)
    returned = lax.all_to_all(frame_grads[None], "pos", split_axis=2, concat_axis=0, tiled=True)
    return returned.reshape(frames, places, 3 * D)


def layer_forward(hidden, frame_mask, attn_set, ffn_set):
    gain_one, qkv_full, out_full = attn_set
    gain_two, gate_up_full, down_full = ffn_set
    normed, inv_one = rms_parts(hidden, gain_one.astype(jnp.float32))
    normed_low = normed.astype(jnp.bfloat16)
    qkv_rows = apply_rows(normed_low, qkv_full).astype(jnp.bfloat16)
    mixed_low, attn_keep = attention_forward(qkv_rows)
    hidden_mid = hidden + apply_rows(mixed_low, out_full)
    normed_two, inv_two = rms_parts(hidden_mid, gain_two.astype(jnp.float32))
    normed_two_low = normed_two.astype(jnp.bfloat16)
    gate_up = apply_rows(normed_two_low, gate_up_full)
    gate_part = gate_up[..., :FF]
    up_part = gate_up[..., FF:]
    act_low = (jax.nn.silu(gate_part) * up_part).astype(jnp.bfloat16)
    result = frame_mask * (hidden_mid + apply_rows(act_low, down_full))
    kept_state = (
        hidden,
        inv_one,
        normed_low,
        attn_keep,
        mixed_low,
        hidden_mid,
        inv_two,
        normed_two_low,
        gate_part,
        up_part,
        act_low,
    )
    return (result, kept_state)


def layer_backward(grad_out, frame_mask, kept_state, ffn_set, fetch_attn):
    (
        hidden,
        inv_one,
        normed_low,
        attn_keep,
        mixed_low,
        hidden_mid,
        inv_two,
        normed_two_low,
        gate_part,
        up_part,
        act_low,
    ) = kept_state
    gain_two, gate_up_full, down_full = ffn_set
    grad_sum = frame_mask * grad_out
    grad_ffn = grad_sum.astype(jnp.bfloat16)
    down_grad = outer_sum(act_low, grad_ffn)
    down_shard = lax.psum_scatter(down_grad, "fsdp", scatter_dimension=1, tiled=True)
    grad_act = apply_back(grad_ffn, down_full)
    sigmoid_gate = jax.nn.sigmoid(gate_part)
    grad_gate = grad_act * up_part * sigmoid_gate * (1.0 + gate_part * (1.0 - sigmoid_gate))
    grad_up = grad_act * gate_part * sigmoid_gate
    grad_gu = jnp.concatenate([grad_gate, grad_up], axis=-1).astype(jnp.bfloat16)
    gate_up_grad = outer_sum(normed_two_low, grad_gu)
    grad_norm_two = apply_back(grad_gu, gate_up_full)
    grad_mid_norm, gain_two_grad = rms_back(
        grad_norm_two, hidden_mid, inv_two, gain_two.astype(jnp.float32)
    )
    ffn_shards = (
        lax.psum_scatter(gain_two_grad, "fsdp", scatter_dimension=1, tiled=True),
        lax.psum_scatter(gate_up_grad, "fsdp", scatter_dimension=1, tiled=True),
    )
    gain_one, qkv_full, out_full = fetch_attn()
    grad_mid = grad_sum + grad_mid_norm
    grad_attn = grad_mid.astype(jnp.bfloat16)
    out_grad = outer_sum(mixed_low, grad_attn)
    grad_mixed = apply_back(grad_attn, out_full)
    grad_qkv = attention_backward(grad_mixed, attn_keep)
    qkv_grad = outer_sum(normed_low, grad_qkv)
    grad_norm_one = apply_back(grad_qkv, qkv_full)
    grad_in_norm, gain_one_grad = rms_back(
        grad_norm_one, hidden, inv_one, gain_one.astype(jnp.float32)
    )
    attn_shards = (
        lax.psum_scatter(gain_one_grad, "fsdp", scatter_dimension=1, tiled=True),
        lax.psum_scatter(qkv_grad, "fsdp", scatter_dimension=1, tiled=True),
        lax.psum_scatter(out_grad, "fsdp", scatter_dimension=1, tiled=True),
    )
    grad_in = grad_mid + grad_in_norm
    return (
        grad_in,
        (attn_shards[0], attn_shards[1], attn_shards[2], ffn_shards[0], ffn_shards[1], down_shard),
    )


def on_device(
    inputs,
    frame_flags,
    attn_gain,
    qkv_weight,
    out_weight,
    ffn_gain,
    gate_up_weight,
    down_weight,
    cotangent,
):
    layer_total = qkv_weight.shape[0]
    frame_mask = frame_flags.astype(jnp.float32)[:, None, None]
    hidden = inputs.astype(jnp.float32)
    layer_idx = 0
    attn_set = attention_weights(attn_gain, qkv_weight, out_weight, layer_idx)
    ffn_set = ffn_weights(ffn_gain, gate_up_weight, down_weight, layer_idx)
    hidden, kept_state = layer_forward(hidden, frame_mask, attn_set, ffn_set)
    states_all = [kept_state]
    grad_rows = cotangent.astype(jnp.float32)
    layer_grads = [None] * layer_total
    for layer_idx in reversed(range(layer_total)):
        ffn_set = ffn_weights(ffn_gain, gate_up_weight, down_weight, layer_idx)
        fetch_attn = gather_later(attn_gain, qkv_weight, out_weight, layer_idx)
        grad_rows, layer_grads[layer_idx] = layer_backward(
            grad_rows, frame_mask, states_all[layer_idx], ffn_set, fetch_attn
        )
    stacked = [jnp.stack([grad_set[column] for grad_set in layer_grads]) for column in range(6)]
    return (
        hidden.astype(jnp.bfloat16),
        grad_rows,
        stacked[0],
        stacked[1],
        stacked[2],
        stacked[3],
        stacked[4],
        stacked[5],
    )


def gather_later(attn_gain, qkv_weight, out_weight, layer_idx):

    def fetched():
        return attention_weights(attn_gain, qkv_weight, out_weight, layer_idx)

    return fetched


KEY, VALUE, QUERY, OUT = 0, 1, 2, 3
GROUPS = {"k": KEY, "v": VALUE, "q": QUERY, "o": OUT}
SEND_SEMS, RECV_SEMS = 51, 89
ROUTES = {"p0": "z", "p1": "z", "u0": "x", "u1": "x"}
MESH = pl.DeviceIdType.MESH


class Names:
    def __getattr__(self, name):
        return name


step = Names()

ORDER = (
    step.v_to_c, step.k_to_x, step.mask, step.k_to_z, step.k_to_c, step.v_to_x, step.o_to_z, step.k_to_s,
    step.v_to_s, step.q_to_s, step.o_to_c, step.gx, step.k_from_s, step.q_to_c, step.v_to_z, step.q_to_x,
    step.o_to_s, step.k_from_sz, step.k_from_z, step.v_from_s, step.q_to_z, step.v_from_sz, step.o_from_s,
    step.norm, step.gz, step.q_from_z, step.v_from_z, step.gs, step.q_from_s, step.v_from_x, step.v_from_c,
    step.ends, step.gz_from, step.d_to, step.k_from_x, step.gd, step.v_rows, step.q_from_sz, step.cz, step.o_to_x,
    step.cx, step.g_own, step.q_from_x, step.o_from_z, step.o_from_sz, step.g_own_from, step.q_from_c,
    step.k_from_c, step.gx_from, step.k_rows, step.q_rows, step.gzs_from, step.attn, step.o_from_x, step.o_from_c,
    step.mid, step.czx, step.gd_from, step.d_from, step.gs_from, step.nz, step.nx, step.gxs_from, step.gds_from,
    step.nzx, step.ffn, step.f2, step.p1n, step.f1, step.b1, step.u1n, step.p0n, step.b2, step.f0, step.f3,
    step.p1f, step.u0n, step.b3, step.w11, step.w01, step.p0f, step.u0f, step.y11, step.w10, step.p1t, step.b0,
    step.w00, step.u0t, step.p0t, step.u1f, step.dg, step.dy, step.gmid, step.gmix, step.Wo, step.gk, step.u1t,
    step.Xo, step.y01, step.Wq, step.y10, step.Wv, step.Xq, step.Xv, step.Zo, step.Wk, step.Xk, step.ig, step.Zq,
    step.out, step.Zv, step.Sq, step.So, step.Zk, step.Sv, step.y00, step.gain, step.Sk,
)


def flip(bit, change):
    return bit + change - 2 * bit * change


def square_kernel(
    x_in, cot_in, flags_ref, gain_one_ref, gain_two_ref, wqkv, wout, wgu, wd,
    out_hbm, ig_hbm, gain_one_out, gain_two_out, gu_out, down_out, attn_out,
    wa, wgu_all, wd_all, n2_all, g_all, act_all, ggu_all,
    po_s, po_r, pg_s, pg_r, gu_core, gu_cross, down_core, attn_core, attn_x, attn_z,
    normed, qb, kb, vb, krem, vrem, mixed, hmid, gv_s, gk_s, gv_r, gk_r,
    gq, gk, gv, gmid, gattn, hold_k, gwide, mask, gain_ref, p_own, p_rem, r_one, r_two,
    gain_r, gain_f, gsum_s, gsum_r, ends, ends_t,
    x_ref, cot_ref, out_ref, ig_ref, ssem, rsem, lsem, gsem,
):
    tokens, width = x_ref.shape
    rows = width // 16
    block = 4 * width // 4
    half = block // 2
    ff = 4 * width
    f = lax.axis_index("fsdp")
    y = lax.axis_index("pos")
    c = f % 2
    x = (f // 2) % 2
    z = (f // 4) % 2
    s = f // 8
    f32, bf16 = jnp.float32, jnp.bfloat16
    every = slice(None)
    steps = tokens // rows
    tile = 256
    tiles = width // tile
    scale = 1.0 / math.sqrt(HEAD_DIM)
    lane_block = 128
    per_block = lane_block // rows

    def peer(ds=0, dz=0, dx=0, dc=0):
        return flip(s, ds) * 8 + flip(z, dz) * 4 + flip(x, dx) * 2 + flip(c, dc)

    def slab(ds=0, dz=0, dx=0, dc=0):
        return flip(s, ds), flip(z, dz), flip(x, dx), flip(c, dc)

    counter = [0, 0, 0]
    sent = {}
    actions = {}

    def action(name):
        def keep(fn):
            actions[name] = fn

        return keep

    groups = {}
    freed = set()

    def take(which, group=None):
        if group is not None and (which, group) in groups:
            return groups[which, group]
        counter[which] += 1
        assert counter[which] <= (SEND_SEMS, RECV_SEMS)[which]
        groups[which, group] = counter[which] - 1
        return counter[which] - 1

    def link(name, src, dst, to, to_y=None, send_group=None, recv_group=None):
        copy = pltpu.make_async_remote_copy(
            src_ref=src, dst_ref=dst, send_sem=ssem.at[take(0, send_group)], recv_sem=rsem.at[take(1, recv_group)],
            device_id=(to, y if to_y is None else to_y), device_id_type=MESH,
        )
        copy.start()
        sent[name] = copy
        if send_group is not None:
            freed.add(name)

    def local(name, src, dst):
        counter[2] += 1
        copy = pltpu.make_async_copy(src, dst, lsem.at[counter[2] - 1])
        copy.start()
        sent[name] = copy

    def wait_block(ref, sem):
        pltpu.make_async_copy(ref, ref, sem).wait()

    def free(*names):
        for name in names:
            if name not in freed:
                freed.add(name)
                sent[name].wait_send()

    def dot(a, b):
        return jnp.dot(a, b, preferred_element_type=f32)

    def dot_nt(a, b):
        return lax.dot_general(a, b, (((1,), (1,)), ((), ())), preferred_element_type=f32)

    def split(v):
        high = v.astype(bf16)
        return high, (v - high.astype(f32)).astype(bf16)

    def head_sum(v):
        high, low = split(v)
        return dot(high, ends[...]) + dot(low, ends[...])

    def head_spread(p):
        high, low = split(p)
        return dot(high, ends_t[...]) + dot(low, ends_t[...])

    def add_rows(ref, came):
        ref[...] = (ref[...].astype(f32) + came[...].astype(f32)).astype(bf16)

    local("x_in", x_in, x_ref)
    local("cot_in", cot_in, cot_ref)

    barrier = pltpu.get_barrier_semaphore()

    @pl.loop(1, 16)
    def _(r):
        pl.semaphore_signal(barrier, inc=1, device_id=(lax.rem(f + r, 16), y), device_id_type=MESH)

    pl.semaphore_signal(barrier, inc=1, device_id=(f, 1 - y), device_id_type=MESH)

    lanes = lax.broadcasted_iota(jnp.int32, gain_ref.shape, 1) // rows == f % per_block
    sublane = lax.broadcasted_iota(jnp.int32, gain_ref.shape, 0)

    def lane_tile(ref):
        return jnp.concatenate([ref[...].astype(f32)] * per_block, axis=1)

    gains = jnp.where(sublane == 0, lane_tile(gain_one_ref), jnp.where(sublane == 1, lane_tile(gain_two_ref), 0.0))
    gain_ref[...] = jnp.where(lanes, gains, 0.0).astype(bf16)

    pl.semaphore_wait(barrier, 16)

    def gain_copy(r):
        return pltpu.make_async_remote_copy(
            src_ref=gain_ref, dst_ref=gain_r.at[r - 1], send_sem=gsem.at[0], recv_sem=gsem.at[1],
            device_id=(lax.rem(f + r, 16), y), device_id_type=MESH,
        )

    def gain_row(which):
        return jnp.concatenate([gain_f[i, which : which + 1, :] for i in range(gain_f.shape[0])], axis=1)

    def add_gain(which, value):
        for i in range(gsum_s.shape[0]):
            gsum_s[i, which : which + 1, :] += value[:, i * 128 : (i + 1) * 128]

    @pl.loop(1, 16)
    def _(r):
        gain_copy(r).start()

    own_cols = (
        wqkv.at[:, pl.ds(width, width)],
        wqkv.at[:, pl.ds(2 * width, width)],
        wqkv.at[:, pl.ds(0, width)],
        wout,
    )
    ways = {"s": (1, 0, 0, 0), "z": (0, 1, 0, 0), "x": (0, 0, 1, 0), "c": (0, 0, 0, 1)}

    def gather_actions(letter, g):
        def send(name, way, src, dst):
            recv_group = letter + "c" if way == "c" else None
            link(letter + name, src, dst, peer(*ways[way]), send_group=letter + way, recv_group=recv_group)

        def own(way):
            @action(letter + "_to_" + way)
            def _():
                send(way, way, own_cols[g], wa.at[(g,) + slab()])
                if way == "c":
                    local(letter + "own", own_cols[g], wa.at[(g,) + slab()])

        for way in ways:
            own(way)

        def pass_on(name, at, way):
            ref = wa.at[(g,) + slab(*at)]
            send(name, way, ref, ref)

        @action(letter + "_from_s")
        def _():
            sent[letter + "s"].wait_recv()
            pass_on("sz", (1, 0, 0, 0), "z")
            pass_on("sx", (1, 0, 0, 0), "x")
            pass_on("sc", (1, 0, 0, 0), "c")

        @action(letter + "_from_z")
        def _():
            sent[letter + "z"].wait_recv()
            pass_on("zx", (0, 1, 0, 0), "x")
            pass_on("zc", (0, 1, 0, 0), "c")

        @action(letter + "_from_sz")
        def _():
            sent[letter + "sz"].wait_recv()
            pass_on("szx", (1, 1, 0, 0), "x")
            pass_on("szc", (1, 1, 0, 0), "c")

        @action(letter + "_from_x")
        def _():
            for name, at in (("x", (0, 0, 1, 0)), ("sx", (1, 0, 1, 0)), ("zx", (0, 1, 1, 0)), ("szx", (1, 1, 1, 0))):
                sent[letter + name].wait_recv()
                pass_on(name + "c", at, "c")

        @action(letter + "_from_c")
        def _():
            sent[letter + "own"].wait()
            wait_block(wa.at[g, :, :, :, flip(c, 1)], rsem.at[take(1, letter + "c")])

    for letter, g in GROUPS.items():
        gather_actions(letter, g)

    @action("ends")
    def _():
        ends[...] = (
            lax.broadcasted_iota(jnp.int32, ends.shape, 0) // HEAD_DIM
            == lax.broadcasted_iota(jnp.int32, ends.shape, 1)
        ).astype(bf16)
        ends_t[...] = (
            lax.broadcasted_iota(jnp.int32, ends_t.shape, 1) // HEAD_DIM
            == lax.broadcasted_iota(jnp.int32, ends_t.shape, 0)
        ).astype(bf16)

    @action("mask")
    def _():
        sent["cot_in"].wait()
        for i in range(tokens // 128):
            flags = flags_ref[i : i + 1, :].astype(f32)
            mask[i * 128 : (i + 1) * 128] = jnp.broadcast_to(flags, (128, 128)).T
        g_all[z, x] = (cot_ref[...].astype(f32) * mask[:, :1]).astype(bf16).reshape(2, 2, rows, width)

    @action("norm")
    def _():
        sent["x_in"].wait()
        gain_f[...] = jnp.zeros_like(gain_f)
        gain_f[f // per_block] += gain_ref[...].astype(f32)

        wait_block(gain_r, gsem.at[0])
        wait_block(gain_r, gsem.at[1])

        @pl.loop(1, 16)
        def _(r):
            gain_f[lax.rem(f + 16 - r, 16) // per_block] += gain_r[r - 1].astype(f32)

        @pl.loop(0, steps, unroll=True)
        def _(i):
            part = pl.ds(i * rows, rows)
            hidden = x_ref[part].astype(f32)
            inv = lax.rsqrt(jnp.mean(hidden * hidden, axis=-1, keepdims=True) + EPSILON)
            r_one[part] = jnp.broadcast_to(inv, (rows, 128))
            normed[part] = (hidden * inv * gain_row(0)).astype(bf16)

    def project(left, g, dest):
        @pl.loop(0, tiles, unroll=True)
        def _(t):
            cols = pl.ds(pl.multiple_of(t * tile, tile), tile)
            dest[:, cols] = dot(left[...], wa[g, :, :, :, :, :, cols].reshape(width, tile)).astype(dest.dtype)

    @action("k_rows")
    def _():
        project(normed, KEY, kb)
        link("key", kb, krem, f, to_y=1 - y)

    @action("v_rows")
    def _():
        project(normed, VALUE, vb)
        link("value", vb, vrem, f, to_y=1 - y)

    @action("q_rows")
    def _():
        project(normed, QUERY, qb)

    blocks = {"s": (1, 0, 0), "x": (0, 0, 1), "z": (0, 1, 0), "d": (0, 1, 1)}
    gu_sems = {}

    def gu_in(flips):
        j = flip(z, flips[1]) * 2 + flip(x, flips[2])
        for u in range(2):
            for part in range(2):
                src = wgu.at[:, pl.ds(pl.multiple_of(u * ff + part * (ff // 2) + j * half, half), half)]
                yield src, wgu_all.at[s, z, x, c, :, pl.ds(u * block + part * half, half)]

    def pieces(flips, pairs):
        sem = take(0), take(1)
        for src, dst in pairs:
            pltpu.make_async_remote_copy(
                src_ref=src, dst_ref=dst, send_sem=ssem.at[sem[0]], recv_sem=rsem.at[sem[1]],
                device_id=(peer(*flips), y), device_id_type=MESH,
            ).start()
        return sem

    def pieces_local(pairs):
        counter[2] += 1
        sem = lsem.at[counter[2] - 1]
        for src, dst in pairs:
            pltpu.make_async_copy(src, dst, sem).start()
        return sem

    def gu_core_send(ref):
        link("gc", ref, ref, peer(dc=1), send_group="g", recv_group="g")

    def gu_actions(way, flips):
        @action("g" + way)
        def _():
            gu_sems[flips] = pieces(flips, gu_in(flips))

        @action("g" + way + "_from")
        def _():
            ref = wgu_all.at[slab(*flips)]
            wait_block(ref, rsem.at[gu_sems[flips][1]])
            if way != "s":
                link("g" + way + "s", ref, ref, peer(ds=1))
            gu_core_send(ref)

        @action("g" + way + "s_from")
        def _():
            sent["g" + way + "s"].wait_recv()
            ref = wgu_all.at[slab(1, flips[1], flips[2])]
            gu_core_send(ref)

    for way, flips in blocks.items():
        gu_actions(way, flips)

    @action("g_own")
    def _():
        gu_sems["own"] = pieces_local(gu_in((0, 0, 0)))

    @action("g_own_from")
    def _():
        ref = wgu_all.at[slab()]
        wait_block(ref, gu_sems["own"])
        gu_core_send(ref)

    @action("d_to")
    def _():
        own = wd_all.at[s, c]
        link("ds", wd, own, peer(ds=1))
        link("dc", wd, own, peer(dc=1))
        local("down", wd, own)

    @action("d_from")
    def _():
        sent["ds"].wait_recv()
        ref = wd_all.at[flip(s, 1), c]
        link("dsc", ref, ref, peer(dc=1))

    @action("ffn")
    def _():
        wait_block(wgu_all.at[:, :, :, flip(c, 1)], rsem.at[take(1, "g")])
        sent["down"].wait()
        sent["dc"].wait_recv()
        sent["dsc"].wait_recv()

    @action("cx")
    def _():
        link("cx", g_all.at[z, x], g_all.at[z, x], peer(dx=1))

    @action("cz")
    def _():
        link("cz", g_all.at[z, x], g_all.at[z, x], peer(dz=1))

    @action("czx")
    def _():
        sent["cz"].wait_recv()
        ref = g_all.at[flip(z, 1), x]
        link("czx", ref, ref, peer(dx=1))

    @action("attn")
    def _():
        sent["key"].wait_recv()
        sent["value"].wait_recv()

        @pl.loop(0, steps, unroll=True)
        def _(i):
            part = pl.ds(i * rows, rows)
            query = qb[part].astype(f32)
            own = head_sum(query * kb[part].astype(f32)) * scale
            far = jnp.where(y > 0, head_sum(query * krem[part].astype(f32)) * scale, MASKED)
            top = jnp.maximum(own, far)
            own = jnp.exp(own - top)
            far = jnp.exp(far - top)
            total = own + far
            own = own / total
            far = far / total
            p_own[part] = own
            p_rem[part] = far
            values = head_spread(own) * vb[part].astype(f32) + head_spread(far) * vrem[part].astype(f32)
            mixed[part] = values.astype(bf16)

    @action("mid")
    def _():
        project(mixed, OUT, hmid)

        @pl.loop(0, steps, unroll=True)
        def _(i):
            part = pl.ds(i * rows, rows)
            hidden = x_ref[part].astype(f32) + hmid[part]
            hmid[part] = hidden
            inv = lax.rsqrt(jnp.mean(hidden * hidden, axis=-1, keepdims=True) + EPSILON)
            r_two[part] = jnp.broadcast_to(inv, (rows, 128))
            n2_all[z, x, i // 2, i % 2] = (hidden * inv * gain_row(1)).astype(bf16)

    @action("nx")
    def _():
        link("nx", n2_all.at[z, x], n2_all.at[z, x], peer(dx=1))

    @action("nz")
    def _():
        link("nz", n2_all.at[z, x], n2_all.at[z, x], peer(dz=1))

    @action("nzx")
    def _():
        sent["nz"].wait_recv()
        ref = n2_all.at[flip(z, 1), x]
        link("nzx", ref, ref, peer(dx=1))

    def chunk_actions(i):
        dz, dx = i // 2, i % 2
        cz, cx = flip(z, dz), flip(x, dx)

        @action("f%d" % i)
        def _():
            if i == 1:
                sent["cx"].wait_recv()
                sent["nx"].wait_recv()
            if i == 3:
                sent["czx"].wait_recv()
                sent["nzx"].wait_recv()

            @pl.loop(0, tiles, unroll=True)
            def _(t):
                first = pl.multiple_of(t * tile, tile)
                cols = pl.ds(first, tile)
                n2 = n2_all[cz, cx].reshape(tokens, width)
                gate = dot(n2, wgu_all[:, :, :, :, :, cols].reshape(width, tile))
                up = dot(n2, wgu_all[:, :, :, :, :, pl.ds(block + first, tile)].reshape(width, tile))
                g_act = dot_nt(g_all[cz, cx].reshape(tokens, width), wd_all[t // 2, t % 2].reshape(tile, width))
                sig = 1.0 / (1.0 + jnp.exp(-gate))
                silu = gate * sig
                shape = (2, 2, rows, tile)
                act_all[cz, cx, :, :, :, cols] = (silu * up).astype(bf16).reshape(shape)
                g_gate = g_act * up * sig * (1.0 + gate * (1.0 - sig))
                ggu_all[cz, cx, :, :, :, cols] = g_gate.astype(bf16).reshape(shape)
                ggu_all[cz, cx, :, :, :, pl.ds(block + first, tile)] = (g_act * silu).astype(bf16).reshape(shape)

            @pl.loop(0, tiles, unroll=True)
            def _(t):
                cols = pl.ds(pl.multiple_of(t * tile, tile), tile)
                g_n2 = dot_nt(
                    ggu_all[cz, cx].reshape(tokens, 2 * block), wgu_all[t // 2, t % 2].reshape(tile, 2 * block)
                )
                pg_s[cz, cx, :, :, :, cols] = g_n2.astype(bf16).reshape(2, 2, rows, tile)

        @action("b%d" % i)
        def _():
            @pl.loop(0, tiles, unroll=True)
            def _(t):
                cols = pl.ds(pl.multiple_of(t * tile, tile), tile)
                part = dot(act_all[cz, cx].reshape(tokens, block), wd_all[:, :, :, :, :, cols].reshape(block, tile))
                po_s[cz, cx, :, :, :, cols] = part.astype(bf16).reshape(2, 2, rows, tile)

    for i in range(4):
        chunk_actions(i)

    def sum_actions(name, sums, came, h, way):
        first = {"x": (0, 1), "z": (1, 0)}[way]
        second = (first[1], first[0])
        one, two = peer(0, *first), peer(0, *second)

        def part(flips):
            return sums.at[flip(z, flips[0]), flip(x, flips[1]), h]

        @action(name + "n")
        def _():
            link(name + "n", part(first), came.at[0, h], one, send_group=name[0])

        @action(name + "f")
        def _():
            link(name + "f", part((1, 1)), came.at[1, h], one, send_group=name[0])

        @action(name + "t")
        def _():
            sent[name + "f"].wait_recv()

            @pl.loop(0, 2, unroll=True)
            def _(m):
                add_rows(part(second).at[m], came.at[1, h, m])

            link(name + "t", part(second), came.at[2, h], two, send_group=name[0])

    for name, way in ROUTES.items():
        sums, came = (pg_s, pg_r) if name[0] == "p" else (po_s, po_r)
        sum_actions(name, sums, came, int(name[1]), way)

    gu_grad = wgu_all
    down_grad = wd_all

    def gu_grad_out(flips):
        j = z * 2 + x
        for u in range(2):
            for part in range(2):
                src = gu_grad.at[slab(*flips) + (every, pl.ds(u * block + part * half, half))]
                cols = pl.ds(pl.multiple_of(u * ff + part * (ff // 2) + j * half, half), half)
                yield src, gu_out.at[:, cols]

    def tile_actions(ds, dz):
        tag = "%d%d" % (ds, dz)
        at = flip(s, ds), flip(z, dz)

        @action("w" + tag)
        def _():
            free("gxs", "gzs", "gds")
            if "tiles" not in freed:
                freed.add("tiles")
                wait_block(wgu_all.at[:, :, :, c], ssem.at[take(0, "g")])
            left = n2_all[:, :, :, :, :, pl.ds(pl.multiple_of((at[0] * 2 + at[1]) * tile, tile), tile)]
            left = left.reshape(4 * tokens, tile).T

            @pl.loop(0, block // tile, unroll=True)
            def _(n):
                wide = pl.ds(pl.multiple_of(n * 2 * tile, 2 * tile), 2 * tile)
                part = dot(left, ggu_all[:, :, :, :, :, wide].reshape(4 * tokens, 2 * tile))
                gu_grad[at[0], at[1], :, :, :, wide] = part.astype(bf16).reshape(2, 2, rows, 2 * tile)

            link("w" + tag, gu_grad.at[at[0], at[1], :, flip(c, 1)], gu_core.at[at], peer(dc=1), send_group="w")

        @action("y" + tag)
        def _():
            sent["w" + tag].wait_recv()
            if ds == 0:
                sent["y1%d" % dz].wait_recv()

            @pl.loop(0, 2, unroll=True)
            def _(m):
                ref = gu_grad.at[at[0], at[1], m, c]
                total = ref[...].astype(f32) + gu_core[at[0], at[1], m].astype(f32)
                if ds == 0:
                    total += gu_cross[at[1], m].astype(f32)
                ref[...] = total.astype(bf16)

            if ds == 1:
                link("y" + tag, gu_grad.at[at[0], at[1], :, c], gu_cross.at[at[1]], peer(ds=1))
                return
            for dx in (1, 0):
                flips = (0, dz, dx)
                if flips == (0, 0, 0):
                    gu_sems["keep"] = pieces_local(gu_grad_out(flips))
                else:
                    gu_sems[flips + (0,)] = pieces(flips, gu_grad_out(flips))

    for ds in (0, 1):
        for dz in (0, 1):
            tile_actions(ds, dz)

    @action("dg")
    def _():
        free("dsc")

        @pl.loop(0, tiles, unroll=True)
        def _(t):
            cols = pl.ds(pl.multiple_of(t * tile, tile), tile)
            left = act_all[:, :, :, :, :, cols].reshape(4 * tokens, tile).T

            @pl.loop(0, width // (2 * tile), unroll=True)
            def _(n):
                wide = pl.ds(pl.multiple_of(n * 2 * tile, 2 * tile), 2 * tile)
                part = dot(left, g_all[:, :, :, :, :, wide].reshape(4 * tokens, 2 * tile))
                down_grad[t // 2, t % 2, :, :, :, wide] = part.astype(bf16).reshape(2, 2, rows, 2 * tile)

        link("dg", down_grad.at[:, flip(c, 1)], down_core, peer(dc=1))

    @action("dy")
    def _():
        sent["dg"].wait_recv()

        @pl.loop(0, 8, unroll=2)
        def _(m):
            rest = ((m // 2) % 2, m % 2)
            add_rows(down_grad.at[(m // 4, c) + rest], down_core.at[(m // 4,) + rest])

        link("dy", down_grad.at[flip(s, 1), c], down_out.at[1], peer(ds=1))
        local("dkeep", down_grad.at[s, c], down_out.at[0])

    @action("gmid")
    def _():
        for name in ("p0n", "p1n", "p0t", "p1t"):
            sent[name].wait_recv()
        gsum_s[...] = jnp.zeros_like(gsum_s)

        @pl.loop(0, steps, unroll=True)
        def _(i):
            part = pl.ds(i * rows, rows)
            at = (i // 2, i % 2)
            g_n2 = pg_s[(z, x) + at].astype(f32)
            for k in (0, 2):
                g_n2 += pg_r[(k,) + at].astype(f32)
            hidden = hmid[part]
            inv = r_two[part][:, :1]
            add_gain(1, jnp.sum(g_n2 * hidden * inv, axis=0, keepdims=True))
            scaled = g_n2 * gain_row(1)
            inner = jnp.mean(scaled * hidden, axis=-1, keepdims=True)
            g_sum = cot_ref[part].astype(f32) * mask[part][:, :1]
            g_mid = g_sum + inv * scaled - hidden * (inv * inv * inv * inner)
            gmid[part] = g_mid
            gattn[part] = g_mid.astype(bf16)

    @action("gmix")
    def _():
        @pl.loop(0, tiles, unroll=True)
        def _(t):
            cols = pl.ds(pl.multiple_of(t * tile, tile), tile)
            gwide[:, cols] = dot_nt(gattn[...], wa[OUT, t // 2, t % 2].reshape(tile, width))

        @pl.loop(0, steps, unroll=True)
        def _(i):
            part = pl.ds(i * rows, rows)
            gv_s[part] = (head_spread(p_rem[part]) * gwide[part]).astype(bf16)

        link("gv", gv_s, gv_r, f, to_y=1 - y)

    @action("gk")
    def _():
        @pl.loop(0, steps, unroll=True)
        def _(i):
            part = pl.ds(i * rows, rows)
            gm = gwide[part]
            own, far = p_own[part], p_rem[part]
            gp_own = head_sum(gm * vb[part].astype(f32))
            gp_far = head_sum(gm * vrem[part].astype(f32))
            inner = own * gp_own + far * gp_far
            gs_own = head_spread(own * (gp_own - inner) * scale)
            gs_far = head_spread(far * (gp_far - inner) * scale)
            query = qb[part].astype(f32)
            gk_s[part] = (gs_far * query).astype(bf16)
            gq[part] = (gs_own * kb[part].astype(f32) + gs_far * krem[part].astype(f32)).astype(bf16)
            hold_k[part] = gs_own * query

        link("gk", gk_s, gk_r, f, to_y=1 - y)

    stage = {OUT: act_all, QUERY: n2_all, VALUE: g_all, KEY: ggu_all}
    out_cols = {QUERY: 0, KEY: 1, VALUE: 2, OUT: 3}

    def grad_actions(letter, g):
        def view(*at):
            ref = stage[g]
            if ref.shape[-1] != width:
                return ref.at[at + (every,) * (5 - len(at)) + (pl.ds(0, width),)]
            return ref.at[at]

        def add_into(count, at_of, came):
            @pl.loop(0, count, unroll=2)
            def _(m):
                add_rows(view(*at_of(m)), came(m))

        def weight_grad(left, right):
            @pl.loop(0, tiles, unroll=True)
            def _(t):
                cols = pl.ds(pl.multiple_of(t * tile, tile), tile)
                part = dot(left[:, cols].T, right[...])
                view(t // 2, t % 2)[...] = part.astype(bf16).reshape(2, 2, rows, width)

            link("W" + letter, view(every, every, every, flip(c, 1)), attn_core.at[g], peer(dc=1), send_group="W")

        @action("W" + letter)
        def _():
            if g == OUT:
                weight_grad(mixed, gattn)
            elif g == QUERY:
                free("nx", "nz", "nzx")
                weight_grad(normed, gq)
            elif g == VALUE:
                free("cx", "cz", "czx")
                sent["gv"].wait_recv()

                @pl.loop(0, steps, unroll=True)
                def _(i):
                    part = pl.ds(i * rows, rows)
                    gv[part] = (head_spread(p_own[part]) * gwide[part] + gv_r[part].astype(f32)).astype(bf16)

                weight_grad(normed, gv)
            else:
                sent["gk"].wait_recv()

                @pl.loop(0, steps, unroll=True)
                def _(i):
                    part = pl.ds(i * rows, rows)
                    gk[part] = (hold_k[part] + gk_r[part].astype(f32)).astype(bf16)

                weight_grad(normed, gk)

        @action("X" + letter)
        def _():
            sent["W" + letter].wait_recv()
            add_into(
                8,
                lambda m: (m // 4, (m // 2) % 2, m % 2, c),
                lambda m: attn_core.at[g, m // 4, (m // 2) % 2, m % 2],
            )
            link("X" + letter, view(every, every, flip(x, 1), c), attn_x.at[g], peer(dx=1), send_group="X")

        @action("Z" + letter)
        def _():
            sent["X" + letter].wait_recv()
            add_into(4, lambda m: (m // 2, m % 2, x, c), lambda m: attn_x.at[g, m // 2, m % 2])
            link("Z" + letter, view(every, flip(z, 1), x, c), attn_z.at[g], peer(dz=1), send_group="Z")

        @action("S" + letter)
        def _():
            sent["Z" + letter].wait_recv()
            add_into(2, lambda m: (m, z, x, c), lambda m: attn_z.at[g, m])
            cols = pl.ds(out_cols[g] * width, width)
            link("S" + letter, view(flip(s, 1), z, x, c), attn_out.at[1, :, cols], peer(ds=1), send_group="S", recv_group="S")
            local("keep" + letter, view(s, z, x, c), attn_out.at[0, :, cols])

    for letter, g in GROUPS.items():
        grad_actions(letter, g)

    def gain_sum_copy(r):
        to = lax.rem(f + r, 16)
        return pltpu.make_async_remote_copy(
            src_ref=gsum_s.at[to // per_block], dst_ref=gsum_r.at[r - 1],
            send_sem=gsem.at[2], recv_sem=gsem.at[3],
            device_id=(to, y), device_id_type=MESH,
        )

    @action("ig")
    def _():
        @pl.loop(0, tiles, unroll=True)
        def _(t):
            cols = pl.ds(pl.multiple_of(t * tile, tile), tile)
            at = (t // 2, t % 2)
            gwide[:, cols] = (
                dot_nt(gq[...], wa[(QUERY,) + at].reshape(tile, width))
                + dot_nt(gk[...], wa[(KEY,) + at].reshape(tile, width))
                + dot_nt(gv[...], wa[(VALUE,) + at].reshape(tile, width))
            )

        @pl.loop(0, steps, unroll=True)
        def _(i):
            part = pl.ds(i * rows, rows)
            hidden = x_ref[part].astype(f32)
            inv = r_one[part][:, :1]
            g_n1 = gwide[part]
            add_gain(0, jnp.sum(g_n1 * hidden * inv, axis=0, keepdims=True))
            scaled = g_n1 * gain_row(0)
            inner = jnp.mean(scaled * hidden, axis=-1, keepdims=True)
            grad = gmid[part] + inv * scaled - hidden * (inv * inv * inv * inner)
            for k in range(width // 128):
                spread = pl.ds(i * rows * (width // 128) + k, rows, width // 128)
                ig_ref[spread, :] = grad[:, k * 128 : (k + 1) * 128]

        local("keep_ig", ig_ref, ig_hbm)

        @pl.loop(1, 16)
        def _(r):
            gain_sum_copy(r).start()

    @action("gain")
    def _():
        gsum_r[15] = gsum_s[f // per_block]

        wait_block(gsum_r.at[pl.ds(0, 15)], gsem.at[2])
        wait_block(gsum_r.at[pl.ds(0, 15)], gsem.at[3])

        @pl.loop(1, 16)
        def _(r):
            gsum_r[15] += gsum_r[r - 1]

        gain_sum = jnp.where(f % per_block == 0, 1.0, 0.0) * gsum_r[15][:, :rows]
        for b in range(1, per_block):
            gain_sum += jnp.where(f % per_block == b, 1.0, 0.0) * gsum_r[15][:, b * rows : (b + 1) * rows]
        gain_one_out[...] = gain_sum[0:1]
        gain_two_out[...] = gain_sum[1:2]

    @action("out")
    def _():
        for name in ("u0n", "u1n", "u0t", "u1t"):
            sent[name].wait_recv()

        @pl.loop(0, steps, unroll=True)
        def _(i):
            part = pl.ds(i * rows, rows)
            at = (i // 2, i % 2)
            total = po_s[(z, x) + at].astype(f32)
            for k in (0, 2):
                total += po_r[(k,) + at].astype(f32)
            out_ref[part] = (mask[part][:, :1] * (hmid[part] + total)).astype(bf16)

        local("keep_out", out_ref, out_hbm)

    for name in ORDER:
        actions[name]()

    for letter, g in GROUPS.items():
        wait_block(wa.at[g, :, :, :, c], ssem.at[take(0, letter + "c")])
        wait_block(wa.at[g, :, :, x, c], ssem.at[take(0, letter + "x")])
        wait_block(wa.at[g, :, z, x, c], ssem.at[take(0, letter + "z")])
        wait_block(wa.at[(g,) + slab()], ssem.at[take(0, letter + "s")])
    for flips in blocks.values():
        wait_block(wgu_all.at[slab()], ssem.at[gu_sems[flips][0]])
    local_only = ("down", "x_in", "cot_in")
    free(*(name for name in sent if name not in local_only and not name.startswith(("keep", "dkeep")) and name[1:] != "own"))
    for ref, group in ((pg_r, "p"), (po_r, "u"), (gu_core, "w"), (attn_core, "W"), (attn_x, "X"), (attn_z, "Z")):
        wait_block(ref, ssem.at[take(0, group)])
    sent["dy"].wait_recv()
    sent["dkeep"].wait()
    sent["keep_out"].wait()
    sent["keep_ig"].wait()
    wait_block(gu_grad.at[slab()], gu_sems["keep"])
    for flips in blocks.values():
        if flips[0] == 0:
            wait_block(gu_grad.at[slab()], ssem.at[gu_sems[flips + (0,)][0]])
            wait_block(gu_grad.at[slab()], rsem.at[gu_sems[flips + (0,)][1]])
    for letter in GROUPS:
        sent["keep" + letter].wait()
    wait_block(attn_z.at[pl.ds(0, 2)], ssem.at[take(0, "S")])
    wait_block(attn_out.at[1], rsem.at[take(1, "S")])


def square_layer(inputs, frame_flags, attn_gain, qkv_weight, out_weight, ffn_gain, gate_up_weight, down_weight, cotangent):
    tokens, _, width = inputs.shape
    rows = qkv_weight.shape[2]
    block = width
    f32, bf16 = jnp.float32, jnp.bfloat16
    lane_block = 128
    lane_blocks = width // lane_block
    vmem = pl.BlockSpec(memory_space=pltpu.VMEM)
    anywhere = pl.BlockSpec(memory_space=pl.ANY)
    unit = (2, 2, 2, 2, rows, width)
    double = (2, 2, 2, 2, rows, 2 * block)
    own = (tokens, width)
    scratch = [
        pltpu.VMEM((4,) + unit, bf16),
        pltpu.VMEM(double, bf16),
        pltpu.VMEM(unit, bf16),
        pltpu.VMEM(unit, bf16),
        pltpu.VMEM(unit, bf16),
        pltpu.VMEM(unit, bf16),
        pltpu.VMEM(double, bf16),
        pltpu.VMEM(unit, bf16),
        pltpu.VMEM((3, 2, 2, rows, width), bf16),
        pltpu.VMEM(unit, bf16),
        pltpu.VMEM((3, 2, 2, rows, width), bf16),
        pltpu.VMEM((2, 2, 2, rows, 2 * block), bf16),
        pltpu.VMEM((2, 2, rows, 2 * block), bf16),
        pltpu.VMEM((2, 2, 2, rows, width), bf16),
        pltpu.VMEM((4, 2, 2, 2, rows, width), bf16),
        pltpu.VMEM((4, 2, 2, rows, width), bf16),
        pltpu.VMEM((4, 2, rows, width), bf16),
        pltpu.VMEM(own, bf16),
        pltpu.VMEM(own, bf16),
        pltpu.VMEM(own, bf16),
        pltpu.VMEM(own, bf16),
        pltpu.VMEM(own, bf16),
        pltpu.VMEM(own, bf16),
        pltpu.VMEM(own, bf16),
        pltpu.VMEM(own, f32),
        pltpu.VMEM(own, bf16),
        pltpu.VMEM(own, bf16),
        pltpu.VMEM(own, bf16),
        pltpu.VMEM(own, bf16),
        pltpu.VMEM(own, bf16),
        pltpu.VMEM(own, bf16),
        pltpu.VMEM(own, bf16),
        pltpu.VMEM(own, f32),
        pltpu.VMEM(own, bf16),
        pltpu.VMEM(own, f32),
        pltpu.VMEM(own, f32),
        pltpu.VMEM((tokens, 128), f32),
        pltpu.VMEM((16, lane_block), bf16),
        pltpu.VMEM((tokens, 128), f32),
        pltpu.VMEM((tokens, 128), f32),
        pltpu.VMEM((tokens, 128), f32),
        pltpu.VMEM((tokens, 128), f32),
        pltpu.VMEM((15, 16, lane_block), bf16),
        pltpu.VMEM((lane_blocks, 16, lane_block), f32),
        pltpu.VMEM((lane_blocks, 8, lane_block), f32),
        pltpu.VMEM((16, 8, lane_block), f32),
        pltpu.VMEM((width, 128), bf16),
        pltpu.VMEM((128, width), bf16),
        pltpu.VMEM(own, bf16),
        pltpu.VMEM(own, bf16),
        pltpu.VMEM(own, bf16),
        pltpu.VMEM((tokens * lane_blocks, lane_block), f32),
        pltpu.SemaphoreType.DMA((SEND_SEMS,)),
        pltpu.SemaphoreType.DMA((RECV_SEMS,)),
        pltpu.SemaphoreType.DMA((16,)),
        pltpu.SemaphoreType.DMA((4,)),
    ]
    outs = pl.pallas_call(
        square_kernel,
        out_shape=(
            jax.ShapeDtypeStruct(own, bf16),
            jax.ShapeDtypeStruct((tokens * lane_blocks, lane_block), f32),
            jax.ShapeDtypeStruct((1, rows), f32),
            jax.ShapeDtypeStruct((1, rows), f32),
            jax.ShapeDtypeStruct((rows, 8 * block), bf16),
            jax.ShapeDtypeStruct((2, 2, 2, rows, width), bf16),
            jax.ShapeDtypeStruct((2, rows, 4 * width), bf16),
        ),
        in_specs=[anywhere] * 2 + [vmem] * 3 + [anywhere] * 4,
        out_specs=(anywhere, anywhere, vmem, vmem, anywhere, anywhere, anywhere),
        scratch_shapes=scratch,
        compiler_params=pltpu.CompilerParams(
            collective_id=0, has_side_effects=True, vmem_limit_bytes=VMEM_BYTES
        ),
        cost_estimate=pl.CostEstimate(flops=26 * 10**9, bytes_accessed=2**23, transcendentals=2**21),
    )(
        inputs[:, 0], cotangent[:, 0], frame_flags.reshape(tokens // lane_block, lane_block), attn_gain[0], ffn_gain[0],
        qkv_weight[0, 0], out_weight[0, 0], gate_up_weight[0, 0], down_weight[0, 0].reshape(2, 2, rows, width),
    )
    result, input_grad, gain_one, gain_two, gu, down, attn = outs
    grid = 2

    def by_rows(shape):
        return pl.BlockSpec((shape[0] // grid,) + shape[1:], lambda i: (i, 0))

    def pair(shape):
        return pl.BlockSpec((2, shape[0] // grid) + shape[1:], lambda i: (0, i, 0))

    whole = pl.BlockSpec((1, rows), lambda i: (0, 0))
    thin = (tokens * lane_blocks, lane_block)
    result, input_grad, qkv, out, gu, down, gain_one, gain_two = pl.pallas_call(
        finish_kernel,
        grid=(grid,),
        out_shape=(
            jax.ShapeDtypeStruct(own, bf16),
            jax.ShapeDtypeStruct(thin, f32),
            jax.ShapeDtypeStruct((rows, 3 * width), f32),
            jax.ShapeDtypeStruct((rows, width), f32),
            jax.ShapeDtypeStruct((rows, 8 * block), f32),
            jax.ShapeDtypeStruct(own, f32),
            jax.ShapeDtypeStruct((1, rows), f32),
            jax.ShapeDtypeStruct((1, rows), f32),
        ),
        in_specs=[by_rows(own), by_rows(thin), whole, whole, by_rows((rows, 8 * block)), pair(own), pair((rows, 4 * width))],
        out_specs=[by_rows(own), by_rows(thin), by_rows((rows, 3 * width)), by_rows((rows, width)),
                   by_rows((rows, 8 * block)), by_rows(own), whole, whole],
        compiler_params=pltpu.CompilerParams(vmem_limit_bytes=VMEM_BYTES),
    )(result, input_grad, gain_one, gain_two, gu, down.reshape((2,) + own), attn)
    return (
        result[:, None],
        input_grad.reshape(tokens, 1, width),
        gain_one[None],
        qkv[None, None],
        out[None, None],
        gain_two[None],
        gu[None, None],
        down[None, None],
    )


def finish_kernel(
    result, input_grad, gain_one, gain_two, gu, down, attn,
    result_out, input_grad_out, qkv_out, out_out, gu_out, down_out, gain_one_out, gain_two_out,
):
    f32 = jnp.float32
    width = out_out.shape[1]
    result_out[...] = result[...]
    input_grad_out[...] = input_grad[...]
    gu_out[...] = gu[...].astype(f32)
    down_out[...] = down[0].astype(f32) + down[1].astype(f32)
    total = attn[0].astype(f32) + attn[1].astype(f32)
    qkv_out[...] = total[:, : 3 * width]
    out_out[...] = total[:, 3 * width :]
    gain_one_out[...] = gain_one[...]
    gain_two_out[...] = gain_two[...]


VMEM_BYTES = 62 * 2**20


def run_layer(axes, *args):
    inputs, qkv_weight, down_weight = args[0], args[3], args[7]
    tokens, places, width = inputs.shape
    rows = qkv_weight.shape[2]
    square = (
        axes["fsdp"] == 16
        and axes["pos"] == 2
        and places == 1
        and qkv_weight.shape[0] == 1
        and tokens == 4 * rows
        and down_weight.shape[2] == 4 * rows
        and 128 % rows == 0
    )
    return square_layer(*args) if square else on_device(*args)


def solution(mesh):
    in_specs = (
        P("fsdp", "pos", None),
        P("fsdp"),
        P(None, "pos", "fsdp"),
        P(None, "pos", "fsdp", None),
        P(None, "pos", "fsdp", None),
        P(None, "pos", "fsdp"),
        P(None, "pos", "fsdp", None),
        P(None, "pos", "fsdp", None),
        P("fsdp", "pos", None),
    )
    out_specs = (
        P("fsdp", "pos", None),
        P("fsdp", "pos", None),
        P(None, "pos", "fsdp"),
        P(None, "pos", "fsdp", None),
        P(None, "pos", "fsdp", None),
        P(None, "pos", "fsdp"),
        P(None, "pos", "fsdp", None),
        P(None, "pos", "fsdp", None),
    )
    return jax.shard_map(
        functools.partial(run_layer, dict(mesh.shape)), mesh=mesh, in_specs=in_specs, out_specs=out_specs, check_vma=False
    )
```

```python
import functools
import math

import jax
import jax.numpy as jnp
from jax import lax
from jax.experimental import pallas as pl
from jax.experimental.pallas import tpu as pltpu
from jax.sharding import PartitionSpec as P

D = 1024
HEADS = 16
HEAD_DIM = 64
FF = 4096


EPSILON = 1e-06
MASKED = -1e30
PRECISE = lax.Precision.HIGHEST


def rms_parts(hidden, gain_row):
    inv_rms = lax.rsqrt(jnp.mean(hidden * hidden, axis=-1, keepdims=True) + EPSILON)
    return (hidden * inv_rms * gain_row[None], inv_rms)


def rms_back(grad_rows, hidden, inv_rms, gain_row):
    scaled = grad_rows * gain_row[None]
    gain_grad = jnp.sum(grad_rows * hidden * inv_rms, axis=0)
    inner_mean = jnp.mean(scaled * hidden, axis=-1, keepdims=True)
    return (inv_rms * scaled - hidden * inv_rms**3 * inner_mean, gain_grad)


def apply_rows(left_side, weight):
    return jnp.einsum("fpd,pde->fpe", left_side, weight, preferred_element_type=jnp.float32)


def apply_back(grad_rows, weight):
    return jnp.einsum("fpe,pde->fpd", grad_rows, weight, preferred_element_type=jnp.float32)


def outer_sum(left_side, grad_rows):
    return jnp.einsum("fpd,fpe->pde", left_side, grad_rows, preferred_element_type=jnp.float32)


def split_heads(rows):
    return rows.reshape(rows.shape[0], rows.shape[1], HEADS, HEAD_DIM)


def attention_weights(attn_gain, qkv_weight, out_weight, layer_idx):
    return (
        lax.all_gather(attn_gain[layer_idx], "fsdp", axis=1, tiled=True),
        lax.all_gather(qkv_weight[layer_idx], "fsdp", axis=1, tiled=True),
        lax.all_gather(out_weight[layer_idx], "fsdp", axis=1, tiled=True),
    )


def ffn_weights(ffn_gain, gate_up_weight, down_weight, layer_idx):
    return (
        lax.all_gather(ffn_gain[layer_idx], "fsdp", axis=1, tiled=True),
        lax.all_gather(gate_up_weight[layer_idx], "fsdp", axis=1, tiled=True),
        lax.all_gather(down_weight[layer_idx], "fsdp", axis=1, tiled=True),
    )


def attention_forward(qkv_rows):
    frames, places = (qkv_rows.shape[0], qkv_rows.shape[1])
    pos_count = lax.axis_size("pos")
    frame_part = frames // pos_count
    outgoing = qkv_rows.reshape(pos_count, frame_part, places, 3 * D)
    frame_qkv = lax.all_to_all(outgoing, "pos", split_axis=0, concat_axis=2, tiled=True)[0].astype(
        jnp.float32
    )
    whole_places = frame_qkv.shape[1]
    queries = split_heads(frame_qkv[..., :D])
    keys_all = split_heads(frame_qkv[..., D : 2 * D])
    values_all = split_heads(frame_qkv[..., 2 * D :])
    scores = jnp.einsum("fphe,fjhe->fhpj", queries, keys_all, precision=PRECISE) / math.sqrt(
        HEAD_DIM
    )
    causal = jnp.arange(whole_places)[:, None] >= jnp.arange(whole_places)[None, :]
    scores = jnp.where(causal, scores, MASKED)
    row_max = jnp.max(scores, axis=-1, keepdims=True)
    exponent = jnp.exp(scores - row_max)
    attn_probs = exponent / jnp.sum(exponent, axis=-1, keepdims=True)
    mixed_heads = jnp.einsum("fhpj,fjhe->fphe", attn_probs, values_all, precision=PRECISE)
    mixed_frames = mixed_heads.reshape(frame_part, whole_places, D).astype(jnp.bfloat16)
    returned = lax.all_to_all(mixed_frames[None], "pos", split_axis=2, concat_axis=0, tiled=True)
    return (returned.reshape(frames, places, D), (queries, keys_all, values_all, attn_probs))


def attention_backward(grad_mixed, attn_keep):
    queries, keys_all, values_all, attn_probs = attn_keep
    frames, places = (grad_mixed.shape[0], grad_mixed.shape[1])
    pos_count = lax.axis_size("pos")
    frame_part = frames // pos_count
    outgoing = grad_mixed.reshape(pos_count, frame_part, places, D)
    grad_frames = lax.all_to_all(
        outgoing.astype(jnp.bfloat16), "pos", split_axis=0, concat_axis=2, tiled=True
    ).astype(outgoing.dtype)[0]
    whole_places = grad_frames.shape[1]
    grad_heads = split_heads(grad_frames)
    grad_values = jnp.einsum("fhpj,fphe->fjhe", attn_probs, grad_heads, precision=PRECISE)
    grad_probs = jnp.einsum("fphe,fjhe->fhpj", grad_heads, values_all, precision=PRECISE)
    grad_scores = (
        attn_probs
        * (grad_probs - jnp.sum(attn_probs * grad_probs, axis=-1, keepdims=True))
        / math.sqrt(HEAD_DIM)
    )
    grad_queries = jnp.einsum("fhpj,fjhe->fphe", grad_scores, keys_all, precision=PRECISE)
    grad_keys = jnp.einsum("fhpj,fphe->fjhe", grad_scores, queries, precision=PRECISE)
    frame_grads = jnp.concatenate(
        [
            grad_queries.reshape(frame_part, whole_places, D),
            grad_keys.reshape(frame_part, whole_places, D),
            grad_values.reshape(frame_part, whole_places, D),
        ],
        axis=-1,
    ).astype(jnp.bfloat16)
    returned = lax.all_to_all(frame_grads[None], "pos", split_axis=2, concat_axis=0, tiled=True)
    return returned.reshape(frames, places, 3 * D)


def layer_forward(hidden, frame_mask, attn_set, ffn_set):
    gain_one, qkv_full, out_full = attn_set
    gain_two, gate_up_full, down_full = ffn_set
    normed, inv_one = rms_parts(hidden, gain_one.astype(jnp.float32))
    normed_low = normed.astype(jnp.bfloat16)
    qkv_rows = apply_rows(normed_low, qkv_full).astype(jnp.bfloat16)
    mixed_low, attn_keep = attention_forward(qkv_rows)
    hidden_mid = hidden + apply_rows(mixed_low, out_full)
    normed_two, inv_two = rms_parts(hidden_mid, gain_two.astype(jnp.float32))
    normed_two_low = normed_two.astype(jnp.bfloat16)
    gate_up = apply_rows(normed_two_low, gate_up_full)
    gate_part = gate_up[..., :FF]
    up_part = gate_up[..., FF:]
    act_low = (jax.nn.silu(gate_part) * up_part).astype(jnp.bfloat16)
    result = frame_mask * (hidden_mid + apply_rows(act_low, down_full))
    kept_state = (
        hidden,
        inv_one,
        normed_low,
        attn_keep,
        mixed_low,
        hidden_mid,
        inv_two,
        normed_two_low,
        gate_part,
        up_part,
        act_low,
    )
    return (result, kept_state)


def layer_backward(grad_out, frame_mask, kept_state, ffn_set, fetch_attn):
    (
        hidden,
        inv_one,
        normed_low,
        attn_keep,
        mixed_low,
        hidden_mid,
        inv_two,
        normed_two_low,
        gate_part,
        up_part,
        act_low,
    ) = kept_state
    gain_two, gate_up_full, down_full = ffn_set
    grad_sum = frame_mask * grad_out
    grad_ffn = grad_sum.astype(jnp.bfloat16)
    down_grad = outer_sum(act_low, grad_ffn)
    down_shard = lax.psum_scatter(down_grad, "fsdp", scatter_dimension=1, tiled=True)
    grad_act = apply_back(grad_ffn, down_full)
    sigmoid_gate = jax.nn.sigmoid(gate_part)
    grad_gate = grad_act * up_part * sigmoid_gate * (1.0 + gate_part * (1.0 - sigmoid_gate))
    grad_up = grad_act * gate_part * sigmoid_gate
    grad_gu = jnp.concatenate([grad_gate, grad_up], axis=-1).astype(jnp.bfloat16)
    gate_up_grad = outer_sum(normed_two_low, grad_gu)
    grad_norm_two = apply_back(grad_gu, gate_up_full)
    grad_mid_norm, gain_two_grad = rms_back(
        grad_norm_two, hidden_mid, inv_two, gain_two.astype(jnp.float32)
    )
    ffn_shards = (
        lax.psum_scatter(gain_two_grad, "fsdp", scatter_dimension=1, tiled=True),
        lax.psum_scatter(gate_up_grad, "fsdp", scatter_dimension=1, tiled=True),
    )
    gain_one, qkv_full, out_full = fetch_attn()
    grad_mid = grad_sum + grad_mid_norm
    grad_attn = grad_mid.astype(jnp.bfloat16)
    out_grad = outer_sum(mixed_low, grad_attn)
    grad_mixed = apply_back(grad_attn, out_full)
    grad_qkv = attention_backward(grad_mixed, attn_keep)
    qkv_grad = outer_sum(normed_low, grad_qkv)
    grad_norm_one = apply_back(grad_qkv, qkv_full)
    grad_in_norm, gain_one_grad = rms_back(
        grad_norm_one, hidden, inv_one, gain_one.astype(jnp.float32)
    )
    attn_shards = (
        lax.psum_scatter(gain_one_grad, "fsdp", scatter_dimension=1, tiled=True),
        lax.psum_scatter(qkv_grad, "fsdp", scatter_dimension=1, tiled=True),
        lax.psum_scatter(out_grad, "fsdp", scatter_dimension=1, tiled=True),
    )
    grad_in = grad_mid + grad_in_norm
    return (
        grad_in,
        (attn_shards[0], attn_shards[1], attn_shards[2], ffn_shards[0], ffn_shards[1], down_shard),
    )


def on_device(
    inputs,
    frame_flags,
    attn_gain,
    qkv_weight,
    out_weight,
    ffn_gain,
    gate_up_weight,
    down_weight,
    cotangent,
):
    layer_total = qkv_weight.shape[0]
    frame_mask = frame_flags.astype(jnp.float32)[:, None, None]
    hidden = inputs.astype(jnp.float32)
    layer_idx = 0
    attn_set = attention_weights(attn_gain, qkv_weight, out_weight, layer_idx)
    ffn_set = ffn_weights(ffn_gain, gate_up_weight, down_weight, layer_idx)
    hidden, kept_state = layer_forward(hidden, frame_mask, attn_set, ffn_set)
    states_all = [kept_state]
    grad_rows = cotangent.astype(jnp.float32)
    layer_grads = [None] * layer_total
    for layer_idx in reversed(range(layer_total)):
        ffn_set = ffn_weights(ffn_gain, gate_up_weight, down_weight, layer_idx)
        fetch_attn = gather_later(attn_gain, qkv_weight, out_weight, layer_idx)
        grad_rows, layer_grads[layer_idx] = layer_backward(
            grad_rows, frame_mask, states_all[layer_idx], ffn_set, fetch_attn
        )
    stacked = [jnp.stack([grad_set[column] for grad_set in layer_grads]) for column in range(6)]
    return (
        hidden.astype(jnp.bfloat16),
        grad_rows,
        stacked[0],
        stacked[1],
        stacked[2],
        stacked[3],
        stacked[4],
        stacked[5],
    )


def gather_later(attn_gain, qkv_weight, out_weight, layer_idx):

    def fetched():
        return attention_weights(attn_gain, qkv_weight, out_weight, layer_idx)

    return fetched


KEY, VALUE, QUERY, OUT = 0, 1, 2, 3
GROUPS = {"k": KEY, "v": VALUE, "q": QUERY, "o": OUT}
SEND_SEMS, RECV_SEMS = 51, 89
ROUTES = {"p0": "z", "p1": "z", "u0": "x", "u1": "x"}
MESH = pl.DeviceIdType.MESH


class Names:
    def __getattr__(self, name):
        return name


step = Names()

ORDER = (
    step.v_to_c, step.k_to_x, step.mask, step.k_to_z, step.k_to_c, step.v_to_x, step.o_to_z, step.k_to_s,
    step.v_to_s, step.q_to_s, step.o_to_c, step.gx, step.k_from_s, step.q_to_c, step.v_to_z, step.q_to_x,
    step.o_to_s, step.k_from_sz, step.k_from_z, step.v_from_s, step.q_to_z, step.v_from_sz, step.o_from_s,
    step.norm, step.gz, step.q_from_z, step.v_from_z, step.gs, step.q_from_s, step.v_from_x, step.v_from_c,
    step.ends, step.gz_from, step.d_to, step.k_from_x, step.gd, step.v_rows, step.q_from_sz, step.cz, step.o_to_x,
    step.cx, step.g_own, step.q_from_x, step.o_from_z, step.o_from_sz, step.g_own_from, step.q_from_c,
    step.k_from_c, step.gx_from, step.k_rows, step.q_rows, step.gzs_from, step.attn, step.o_from_x, step.o_from_c,
    step.mid, step.czx, step.gd_from, step.d_from, step.gs_from, step.nz, step.nx, step.gxs_from, step.gds_from,
    step.nzx, step.ffn, step.f2, step.p1n, step.f1, step.b1, step.u1n, step.p0n, step.b2, step.f0, step.f3,
    step.p1f, step.u0n, step.b3, step.w11, step.w01, step.p0f, step.u0f, step.y11, step.w10, step.p1t, step.b0,
    step.w00, step.u0t, step.p0t, step.u1f, step.dg, step.dy, step.gmid, step.gmix, step.Wo, step.gk, step.u1t,
    step.Xo, step.y01, step.Wq, step.y10, step.Wv, step.Xq, step.Xv, step.Zo, step.Wk, step.Xk, step.ig, step.Zq,
    step.out, step.Zv, step.Sq, step.So, step.Zk, step.Sv, step.y00, step.gain, step.Sk,
)


def flip(bit, change):
    return bit + change - 2 * bit * change


def square_kernel(
    x_in, cot_in, flags_ref, gain_one_ref, gain_two_ref, wqkv, wout, wgu, wd,
    out_hbm, ig_hbm, gain_one_out, gain_two_out, gu_out, down_out, attn_out,
    wa, wgu_all, wd_all, n2_all, g_all, act_all, ggu_all,
    po_s, po_r, pg_s, pg_r, gu_core, gu_cross, down_core, attn_core, attn_x, attn_z,
    normed, qb, kb, vb, krem, vrem, mixed, hmid, gv_s, gk_s, gv_r, gk_r,
    gq, gk, gv, gmid, gattn, hold_k, gwide, mask, gain_ref, p_own, p_rem, r_one, r_two,
    gain_r, gain_f, gsum_s, gsum_r, ends, ends_t,
    x_ref, cot_ref, out_ref, ig_ref, ssem, rsem, lsem, gsem,
):
    tokens, width = x_ref.shape
    rows = width // 16
    block = 4 * width // 4
    half = block // 2
    ff = 4 * width
    f = lax.axis_index("fsdp")
    y = lax.axis_index("pos")
    c = f % 2
    x = (f // 2) % 2
    z = (f // 4) % 2
    s = f // 8
    f32, bf16 = jnp.float32, jnp.bfloat16
    every = slice(None)
    steps = tokens // rows
    tile = 256
    tiles = width // tile
    scale = 1.0 / math.sqrt(HEAD_DIM)
    lane_block = 128
    per_block = lane_block // rows

    def peer(ds=0, dz=0, dx=0, dc=0):
        return flip(s, ds) * 8 + flip(z, dz) * 4 + flip(x, dx) * 2 + flip(c, dc)

    def slab(ds=0, dz=0, dx=0, dc=0):
        return flip(s, ds), flip(z, dz), flip(x, dx), flip(c, dc)

    counter = [0, 0, 0]
    sent = {}
    actions = {}

    def action(name):
        def keep(fn):
            actions[name] = fn

        return keep

    groups = {}
    freed = set()

    def take(which, group=None):
        if group is not None and (which, group) in groups:
            return groups[which, group]
        counter[which] += 1
        assert counter[which] <= (SEND_SEMS, RECV_SEMS)[which]
        groups[which, group] = counter[which] - 1
        return counter[which] - 1

    def link(name, src, dst, to, to_y=None, send_group=None, recv_group=None):
        copy = pltpu.make_async_remote_copy(
            src_ref=src, dst_ref=dst, send_sem=ssem.at[take(0, send_group)], recv_sem=rsem.at[take(1, recv_group)],
            device_id=(to, y if to_y is None else to_y), device_id_type=MESH,
        )
        copy.start()
        sent[name] = copy
        if send_group is not None:
            freed.add(name)

    def local(name, src, dst):
        counter[2] += 1
        copy = pltpu.make_async_copy(src, dst, lsem.at[counter[2] - 1])
        copy.start()
        sent[name] = copy

    def wait_block(ref, sem):
        pltpu.make_async_copy(ref, ref, sem).wait()

    def free(*names):
        for name in names:
            if name not in freed:
                freed.add(name)
                sent[name].wait_send()

    def dot(a, b):
        return jnp.dot(a, b, preferred_element_type=f32)

    def dot_nt(a, b):
        return lax.dot_general(a, b, (((1,), (1,)), ((), ())), preferred_element_type=f32)

    def split(v):
        high = v.astype(bf16)
        return high, (v - high.astype(f32)).astype(bf16)

    def head_sum(v):
        high, low = split(v)
        return dot(high, ends[...]) + dot(low, ends[...])

    def head_spread(p):
        high, low = split(p)
        return dot(high, ends_t[...]) + dot(low, ends_t[...])

    def add_rows(ref, came):
        ref[...] = (ref[...].astype(f32) + came[...].astype(f32)).astype(bf16)

    local("x_in", x_in, x_ref)
    local("cot_in", cot_in, cot_ref)

    barrier = pltpu.get_barrier_semaphore()

    @pl.loop(1, 16)
    def _(r):
        pl.semaphore_signal(barrier, inc=1, device_id=(lax.rem(f + r, 16), y), device_id_type=MESH)

    pl.semaphore_signal(barrier, inc=1, device_id=(f, 1 - y), device_id_type=MESH)

    lanes = lax.broadcasted_iota(jnp.int32, gain_ref.shape, 1) // rows == f % per_block
    sublane = lax.broadcasted_iota(jnp.int32, gain_ref.shape, 0)

    def lane_tile(ref):
        return jnp.concatenate([ref[...].astype(f32)] * per_block, axis=1)

    gains = jnp.where(sublane == 0, lane_tile(gain_one_ref), jnp.where(sublane == 1, lane_tile(gain_two_ref), 0.0))
    gain_ref[...] = jnp.where(lanes, gains, 0.0).astype(bf16)

    pl.semaphore_wait(barrier, 16)

    def gain_copy(r):
        return pltpu.make_async_remote_copy(
            src_ref=gain_ref, dst_ref=gain_r.at[r - 1], send_sem=gsem.at[0], recv_sem=gsem.at[1],
            device_id=(lax.rem(f + r, 16), y), device_id_type=MESH,
        )

    def gain_row(which):
        return jnp.concatenate([gain_f[i, which : which + 1, :] for i in range(gain_f.shape[0])], axis=1)

    def add_gain(which, value):
        for i in range(gsum_s.shape[0]):
            gsum_s[i, which : which + 1, :] += value[:, i * 128 : (i + 1) * 128]

    @pl.loop(1, 16)
    def _(r):
        gain_copy(r).start()

    own_cols = (
        wqkv.at[:, pl.ds(width, width)],
        wqkv.at[:, pl.ds(2 * width, width)],
        wqkv.at[:, pl.ds(0, width)],
        wout,
    )
    ways = {"s": (1, 0, 0, 0), "z": (0, 1, 0, 0), "x": (0, 0, 1, 0), "c": (0, 0, 0, 1)}

    def gather_actions(letter, g):
        def send(name, way, src, dst):
            recv_group = letter + "c" if way == "c" else None
            link(letter + name, src, dst, peer(*ways[way]), send_group=letter + way, recv_group=recv_group)

        def own(way):
            @action(letter + "_to_" + way)
            def _():
                send(way, way, own_cols[g], wa.at[(g,) + slab()])
                if way == "c":
                    local(letter + "own", own_cols[g], wa.at[(g,) + slab()])

        for way in ways:
            own(way)

        def pass_on(name, at, way):
            ref = wa.at[(g,) + slab(*at)]
            send(name, way, ref, ref)

        @action(letter + "_from_s")
        def _():
            sent[letter + "s"].wait_recv()
            pass_on("sz", (1, 0, 0, 0), "z")
            pass_on("sx", (1, 0, 0, 0), "x")
            pass_on("sc", (1, 0, 0, 0), "c")

        @action(letter + "_from_z")
        def _():
            sent[letter + "z"].wait_recv()
            pass_on("zx", (0, 1, 0, 0), "x")
            pass_on("zc", (0, 1, 0, 0), "c")

        @action(letter + "_from_sz")
        def _():
            sent[letter + "sz"].wait_recv()
            pass_on("szx", (1, 1, 0, 0), "x")
            pass_on("szc", (1, 1, 0, 0), "c")

        @action(letter + "_from_x")
        def _():
            for name, at in (("x", (0, 0, 1, 0)), ("sx", (1, 0, 1, 0)), ("zx", (0, 1, 1, 0)), ("szx", (1, 1, 1, 0))):
                sent[letter + name].wait_recv()
                pass_on(name + "c", at, "c")

        @action(letter + "_from_c")
        def _():
            sent[letter + "own"].wait()
            wait_block(wa.at[g, :, :, :, flip(c, 1)], rsem.at[take(1, letter + "c")])

    for letter, g in GROUPS.items():
        gather_actions(letter, g)

    @action("ends")
    def _():
        ends[...] = (
            lax.broadcasted_iota(jnp.int32, ends.shape, 0) // HEAD_DIM
            == lax.broadcasted_iota(jnp.int32, ends.shape, 1)
        ).astype(bf16)
        ends_t[...] = (
            lax.broadcasted_iota(jnp.int32, ends_t.shape, 1) // HEAD_DIM
            == lax.broadcasted_iota(jnp.int32, ends_t.shape, 0)
        ).astype(bf16)

    @action("mask")
    def _():
        sent["cot_in"].wait()
        for i in range(tokens // 128):
            flags = flags_ref[i : i + 1, :].astype(f32)
            mask[i * 128 : (i + 1) * 128] = jnp.broadcast_to(flags, (128, 128)).T
        g_all[z, x] = (cot_ref[...].astype(f32) * mask[:, :1]).astype(bf16).reshape(2, 2, rows, width)

    @action("norm")
    def _():
        sent["x_in"].wait()
        gain_f[...] = jnp.zeros_like(gain_f)
        gain_f[f // per_block] += gain_ref[...].astype(f32)

        wait_block(gain_r, gsem.at[0])
        wait_block(gain_r, gsem.at[1])

        @pl.loop(1, 16)
        def _(r):
            gain_f[lax.rem(f + 16 - r, 16) // per_block] += gain_r[r - 1].astype(f32)

        @pl.loop(0, steps, unroll=True)
        def _(i):
            part = pl.ds(i * rows, rows)
            hidden = x_ref[part].astype(f32)
            inv = lax.rsqrt(jnp.mean(hidden * hidden, axis=-1, keepdims=True) + EPSILON)
            r_one[part] = jnp.broadcast_to(inv, (rows, 128))
            normed[part] = (hidden * inv * gain_row(0)).astype(bf16)

    def project(left, g, dest):
        @pl.loop(0, tiles, unroll=True)
        def _(t):
            cols = pl.ds(pl.multiple_of(t * tile, tile), tile)
            dest[:, cols] = dot(left[...], wa[g, :, :, :, :, :, cols].reshape(width, tile)).astype(dest.dtype)

    @action("k_rows")
    def _():
        project(normed, KEY, kb)
        link("key", kb, krem, f, to_y=1 - y)

    @action("v_rows")
    def _():
        project(normed, VALUE, vb)
        link("value", vb, vrem, f, to_y=1 - y)

    @action("q_rows")
    def _():
        project(normed, QUERY, qb)

    blocks = {"s": (1, 0, 0), "x": (0, 0, 1), "z": (0, 1, 0), "d": (0, 1, 1)}
    gu_sems = {}

    def gu_in(flips):
        j = flip(z, flips[1]) * 2 + flip(x, flips[2])
        for u in range(2):
            for part in range(2):
                src = wgu.at[:, pl.ds(pl.multiple_of(u * ff + part * (ff // 2) + j * half, half), half)]
                yield src, wgu_all.at[s, z, x, c, :, pl.ds(u * block + part * half, half)]

    def pieces(flips, pairs):
        sem = take(0), take(1)
        for src, dst in pairs:
            pltpu.make_async_remote_copy(
                src_ref=src, dst_ref=dst, send_sem=ssem.at[sem[0]], recv_sem=rsem.at[sem[1]],
                device_id=(peer(*flips), y), device_id_type=MESH,
            ).start()
        return sem

    def pieces_local(pairs):
        counter[2] += 1
        sem = lsem.at[counter[2] - 1]
        for src, dst in pairs:
            pltpu.make_async_copy(src, dst, sem).start()
        return sem

    def gu_core_send(ref):
        link("gc", ref, ref, peer(dc=1), send_group="g", recv_group="g")

    def gu_actions(way, flips):
        @action("g" + way)
        def _():
            gu_sems[flips] = pieces(flips, gu_in(flips))

        @action("g" + way + "_from")
        def _():
            ref = wgu_all.at[slab(*flips)]
            wait_block(ref, rsem.at[gu_sems[flips][1]])
            if way != "s":
                link("g" + way + "s", ref, ref, peer(ds=1))
            gu_core_send(ref)

        @action("g" + way + "s_from")
        def _():
            sent["g" + way + "s"].wait_recv()
            ref = wgu_all.at[slab(1, flips[1], flips[2])]
            gu_core_send(ref)

    for way, flips in blocks.items():
        gu_actions(way, flips)

    @action("g_own")
    def _():
        gu_sems["own"] = pieces_local(gu_in((0, 0, 0)))

    @action("g_own_from")
    def _():
        ref = wgu_all.at[slab()]
        wait_block(ref, gu_sems["own"])
        gu_core_send(ref)

    @action("d_to")
    def _():
        own = wd_all.at[s, c]
        link("ds", wd, own, peer(ds=1))
        link("dc", wd, own, peer(dc=1))
        local("down", wd, own)

    @action("d_from")
    def _():
        sent["ds"].wait_recv()
        ref = wd_all.at[flip(s, 1), c]
        link("dsc", ref, ref, peer(dc=1))

    @action("ffn")
    def _():
        wait_block(wgu_all.at[:, :, :, flip(c, 1)], rsem.at[take(1, "g")])
        sent["down"].wait()
        sent["dc"].wait_recv()
        sent["dsc"].wait_recv()

    @action("cx")
    def _():
        link("cx", g_all.at[z, x], g_all.at[z, x], peer(dx=1))

    @action("cz")
    def _():
        link("cz", g_all.at[z, x], g_all.at[z, x], peer(dz=1))

    @action("czx")
    def _():
        sent["cz"].wait_recv()
        ref = g_all.at[flip(z, 1), x]
        link("czx", ref, ref, peer(dx=1))

    @action("attn")
    def _():
        sent["key"].wait_recv()
        sent["value"].wait_recv()

        @pl.loop(0, steps, unroll=True)
        def _(i):
            part = pl.ds(i * rows, rows)
            query = qb[part].astype(f32)
            own = head_sum(query * kb[part].astype(f32)) * scale
            far = jnp.where(y > 0, head_sum(query * krem[part].astype(f32)) * scale, MASKED)
            top = jnp.maximum(own, far)
            own = jnp.exp(own - top)
            far = jnp.exp(far - top)
            total = own + far
            own = own / total
            far = far / total
            p_own[part] = own
            p_rem[part] = far
            values = head_spread(own) * vb[part].astype(f32) + head_spread(far) * vrem[part].astype(f32)
            mixed[part] = values.astype(bf16)

    @action("mid")
    def _():
        project(mixed, OUT, hmid)

        @pl.loop(0, steps, unroll=True)
        def _(i):
            part = pl.ds(i * rows, rows)
            hidden = x_ref[part].astype(f32) + hmid[part]
            hmid[part] = hidden
            inv = lax.rsqrt(jnp.mean(hidden * hidden, axis=-1, keepdims=True) + EPSILON)
            r_two[part] = jnp.broadcast_to(inv, (rows, 128))
            n2_all[z, x, i // 2, i % 2] = (hidden * inv * gain_row(1)).astype(bf16)

    @action("nx")
    def _():
        link("nx", n2_all.at[z, x], n2_all.at[z, x], peer(dx=1))

    @action("nz")
    def _():
        link("nz", n2_all.at[z, x], n2_all.at[z, x], peer(dz=1))

    @action("nzx")
    def _():
        sent["nz"].wait_recv()
        ref = n2_all.at[flip(z, 1), x]
        link("nzx", ref, ref, peer(dx=1))

    def chunk_actions(i):
        dz, dx = i // 2, i % 2
        cz, cx = flip(z, dz), flip(x, dx)

        @action("f%d" % i)
        def _():
            if i == 1:
                sent["cx"].wait_recv()
                sent["nx"].wait_recv()
            if i == 3:
                sent["czx"].wait_recv()
                sent["nzx"].wait_recv()

            @pl.loop(0, tiles, unroll=True)
            def _(t):
                first = pl.multiple_of(t * tile, tile)
                cols = pl.ds(first, tile)
                n2 = n2_all[cz, cx].reshape(tokens, width)
                gate = dot(n2, wgu_all[:, :, :, :, :, cols].reshape(width, tile))
                up = dot(n2, wgu_all[:, :, :, :, :, pl.ds(block + first, tile)].reshape(width, tile))
                g_act = dot_nt(g_all[cz, cx].reshape(tokens, width), wd_all[t // 2, t % 2].reshape(tile, width))
                sig = 1.0 / (1.0 + jnp.exp(-gate))
                silu = gate * sig
                shape = (2, 2, rows, tile)
                act_all[cz, cx, :, :, :, cols] = (silu * up).astype(bf16).reshape(shape)
                g_gate = g_act * up * sig * (1.0 + gate * (1.0 - sig))
                ggu_all[cz, cx, :, :, :, cols] = g_gate.astype(bf16).reshape(shape)
                ggu_all[cz, cx, :, :, :, pl.ds(block + first, tile)] = (g_act * silu).astype(bf16).reshape(shape)

            @pl.loop(0, tiles, unroll=True)
            def _(t):
                cols = pl.ds(pl.multiple_of(t * tile, tile), tile)
                g_n2 = dot_nt(
                    ggu_all[cz, cx].reshape(tokens, 2 * block), wgu_all[t // 2, t % 2].reshape(tile, 2 * block)
                )
                pg_s[cz, cx, :, :, :, cols] = g_n2.astype(bf16).reshape(2, 2, rows, tile)

        @action("b%d" % i)
        def _():
            @pl.loop(0, tiles, unroll=True)
            def _(t):
                cols = pl.ds(pl.multiple_of(t * tile, tile), tile)
                part = dot(act_all[cz, cx].reshape(tokens, block), wd_all[:, :, :, :, :, cols].reshape(block, tile))
                po_s[cz, cx, :, :, :, cols] = part.astype(bf16).reshape(2, 2, rows, tile)

    for i in range(4):
        chunk_actions(i)

    def sum_actions(name, sums, came, h, way):
        first = {"x": (0, 1), "z": (1, 0)}[way]
        second = (first[1], first[0])
        one, two = peer(0, *first), peer(0, *second)

        def part(flips):
            return sums.at[flip(z, flips[0]), flip(x, flips[1]), h]

        @action(name + "n")
        def _():
            link(name + "n", part(first), came.at[0, h], one, send_group=name[0])

        @action(name + "f")
        def _():
            link(name + "f", part((1, 1)), came.at[1, h], one, send_group=name[0])

        @action(name + "t")
        def _():
            sent[name + "f"].wait_recv()

            @pl.loop(0, 2, unroll=True)
            def _(m):
                add_rows(part(second).at[m], came.at[1, h, m])

            link(name + "t", part(second), came.at[2, h], two, send_group=name[0])

    for name, way in ROUTES.items():
        sums, came = (pg_s, pg_r) if name[0] == "p" else (po_s, po_r)
        sum_actions(name, sums, came, int(name[1]), way)

    gu_grad = wgu_all
    down_grad = wd_all

    def gu_grad_out(flips):
        j = z * 2 + x
        for u in range(2):
            for part in range(2):
                src = gu_grad.at[slab(*flips) + (every, pl.ds(u * block + part * half, half))]
                cols = pl.ds(pl.multiple_of(u * ff + part * (ff // 2) + j * half, half), half)
                yield src, gu_out.at[:, cols]

    def tile_actions(ds, dz):
        tag = "%d%d" % (ds, dz)
        at = flip(s, ds), flip(z, dz)

        @action("w" + tag)
        def _():
            free("gxs", "gzs", "gds")
            if "tiles" not in freed:
                freed.add("tiles")
                wait_block(wgu_all.at[:, :, :, c], ssem.at[take(0, "g")])
            left = n2_all[:, :, :, :, :, pl.ds(pl.multiple_of((at[0] * 2 + at[1]) * tile, tile), tile)]
            left = left.reshape(4 * tokens, tile).T

            @pl.loop(0, block // tile, unroll=True)
            def _(n):
                wide = pl.ds(pl.multiple_of(n * 2 * tile, 2 * tile), 2 * tile)
                part = dot(left, ggu_all[:, :, :, :, :, wide].reshape(4 * tokens, 2 * tile))
                gu_grad[at[0], at[1], :, :, :, wide] = part.astype(bf16).reshape(2, 2, rows, 2 * tile)

            link("w" + tag, gu_grad.at[at[0], at[1], :, flip(c, 1)], gu_core.at[at], peer(dc=1), send_group="w")

        @action("y" + tag)
        def _():
            sent["w" + tag].wait_recv()
            if ds == 0:
                sent["y1%d" % dz].wait_recv()

            @pl.loop(0, 2, unroll=True)
            def _(m):
                ref = gu_grad.at[at[0], at[1], m, c]
                total = ref[...].astype(f32) + gu_core[at[0], at[1], m].astype(f32)
                if ds == 0:
                    total += gu_cross[at[1], m].astype(f32)
                ref[...] = total.astype(bf16)

            if ds == 1:
                link("y" + tag, gu_grad.at[at[0], at[1], :, c], gu_cross.at[at[1]], peer(ds=1))
                return
            for dx in (1, 0):
                flips = (0, dz, dx)
                if flips == (0, 0, 0):
                    gu_sems["keep"] = pieces_local(gu_grad_out(flips))
                else:
                    gu_sems[flips + (0,)] = pieces(flips, gu_grad_out(flips))

    for ds in (0, 1):
        for dz in (0, 1):
            tile_actions(ds, dz)

    @action("dg")
    def _():
        free("dsc")

        @pl.loop(0, tiles, unroll=True)
        def _(t):
            cols = pl.ds(pl.multiple_of(t * tile, tile), tile)
            left = act_all[:, :, :, :, :, cols].reshape(4 * tokens, tile).T

            @pl.loop(0, width // (2 * tile), unroll=True)
            def _(n):
                wide = pl.ds(pl.multiple_of(n * 2 * tile, 2 * tile), 2 * tile)
                part = dot(left, g_all[:, :, :, :, :, wide].reshape(4 * tokens, 2 * tile))
                down_grad[t // 2, t % 2, :, :, :, wide] = part.astype(bf16).reshape(2, 2, rows, 2 * tile)

        link("dg", down_grad.at[:, flip(c, 1)], down_core, peer(dc=1))

    @action("dy")
    def _():
        sent["dg"].wait_recv()

        @pl.loop(0, 8, unroll=2)
        def _(m):
            rest = ((m // 2) % 2, m % 2)
            add_rows(down_grad.at[(m // 4, c) + rest], down_core.at[(m // 4,) + rest])

        link("dy", down_grad.at[flip(s, 1), c], down_out.at[1], peer(ds=1))
        local("dkeep", down_grad.at[s, c], down_out.at[0])

    @action("gmid")
    def _():
        for name in ("p0n", "p1n", "p0t", "p1t"):
            sent[name].wait_recv()
        gsum_s[...] = jnp.zeros_like(gsum_s)

        @pl.loop(0, steps, unroll=True)
        def _(i):
            part = pl.ds(i * rows, rows)
            at = (i // 2, i % 2)
            g_n2 = pg_s[(z, x) + at].astype(f32)
            for k in (0, 2):
                g_n2 += pg_r[(k,) + at].astype(f32)
            hidden = hmid[part]
            inv = r_two[part][:, :1]
            add_gain(1, jnp.sum(g_n2 * hidden * inv, axis=0, keepdims=True))
            scaled = g_n2 * gain_row(1)
            inner = jnp.mean(scaled * hidden, axis=-1, keepdims=True)
            g_sum = cot_ref[part].astype(f32) * mask[part][:, :1]
            g_mid = g_sum + inv * scaled - hidden * (inv * inv * inv * inner)
            gmid[part] = g_mid
            gattn[part] = g_mid.astype(bf16)

    @action("gmix")
    def _():
        @pl.loop(0, tiles, unroll=True)
        def _(t):
            cols = pl.ds(pl.multiple_of(t * tile, tile), tile)
            gwide[:, cols] = dot_nt(gattn[...], wa[OUT, t // 2, t % 2].reshape(tile, width))

        @pl.loop(0, steps, unroll=True)
        def _(i):
            part = pl.ds(i * rows, rows)
            gv_s[part] = (head_spread(p_rem[part]) * gwide[part]).astype(bf16)

        link("gv", gv_s, gv_r, f, to_y=1 - y)

    @action("gk")
    def _():
        @pl.loop(0, steps, unroll=True)
        def _(i):
            part = pl.ds(i * rows, rows)
            gm = gwide[part]
            own, far = p_own[part], p_rem[part]
            gp_own = head_sum(gm * vb[part].astype(f32))
            gp_far = head_sum(gm * vrem[part].astype(f32))
            inner = own * gp_own + far * gp_far
            gs_own = head_spread(own * (gp_own - inner) * scale)
            gs_far = head_spread(far * (gp_far - inner) * scale)
            query = qb[part].astype(f32)
            gk_s[part] = (gs_far * query).astype(bf16)
            gq[part] = (gs_own * kb[part].astype(f32) + gs_far * krem[part].astype(f32)).astype(bf16)
            hold_k[part] = gs_own * query

        link("gk", gk_s, gk_r, f, to_y=1 - y)

    stage = {OUT: act_all, QUERY: n2_all, VALUE: g_all, KEY: ggu_all}
    out_cols = {QUERY: 0, KEY: 1, VALUE: 2, OUT: 3}

    def grad_actions(letter, g):
        def view(*at):
            ref = stage[g]
            if ref.shape[-1] != width:
                return ref.at[at + (every,) * (5 - len(at)) + (pl.ds(0, width),)]
            return ref.at[at]

        def add_into(count, at_of, came):
            @pl.loop(0, count, unroll=2)
            def _(m):
                add_rows(view(*at_of(m)), came(m))

        def weight_grad(left, right):
            @pl.loop(0, tiles, unroll=True)
            def _(t):
                cols = pl.ds(pl.multiple_of(t * tile, tile), tile)
                part = dot(left[:, cols].T, right[...])
                view(t // 2, t % 2)[...] = part.astype(bf16).reshape(2, 2, rows, width)

            link("W" + letter, view(every, every, every, flip(c, 1)), attn_core.at[g], peer(dc=1), send_group="W")

        @action("W" + letter)
        def _():
            if g == OUT:
                weight_grad(mixed, gattn)
            elif g == QUERY:
                free("nx", "nz", "nzx")
                weight_grad(normed, gq)
            elif g == VALUE:
                free("cx", "cz", "czx")
                sent["gv"].wait_recv()

                @pl.loop(0, steps, unroll=True)
                def _(i):
                    part = pl.ds(i * rows, rows)
                    gv[part] = (head_spread(p_own[part]) * gwide[part] + gv_r[part].astype(f32)).astype(bf16)

                weight_grad(normed, gv)
            else:
                sent["gk"].wait_recv()

                @pl.loop(0, steps, unroll=True)
                def _(i):
                    part = pl.ds(i * rows, rows)
                    gk[part] = (hold_k[part] + gk_r[part].astype(f32)).astype(bf16)

                weight_grad(normed, gk)

        @action("X" + letter)
        def _():
            sent["W" + letter].wait_recv()
            add_into(
                8,
                lambda m: (m // 4, (m // 2) % 2, m % 2, c),
                lambda m: attn_core.at[g, m // 4, (m // 2) % 2, m % 2],
            )
            link("X" + letter, view(every, every, flip(x, 1), c), attn_x.at[g], peer(dx=1), send_group="X")

        @action("Z" + letter)
        def _():
            sent["X" + letter].wait_recv()
            add_into(4, lambda m: (m // 2, m % 2, x, c), lambda m: attn_x.at[g, m // 2, m % 2])
            link("Z" + letter, view(every, flip(z, 1), x, c), attn_z.at[g], peer(dz=1), send_group="Z")

        @action("S" + letter)
        def _():
            sent["Z" + letter].wait_recv()
            add_into(2, lambda m: (m, z, x, c), lambda m: attn_z.at[g, m])
            cols = pl.ds(out_cols[g] * width, width)
            link("S" + letter, view(flip(s, 1), z, x, c), attn_out.at[1, :, cols], peer(ds=1), send_group="S", recv_group="S")
            local("keep" + letter, view(s, z, x, c), attn_out.at[0, :, cols])

    for letter, g in GROUPS.items():
        grad_actions(letter, g)

    def gain_sum_copy(r):
        to = lax.rem(f + r, 16)
        return pltpu.make_async_remote_copy(
            src_ref=gsum_s.at[to // per_block], dst_ref=gsum_r.at[r - 1],
            send_sem=gsem.at[2], recv_sem=gsem.at[3],
            device_id=(to, y), device_id_type=MESH,
        )

    @action("ig")
    def _():
        @pl.loop(0, tiles, unroll=True)
        def _(t):
            cols = pl.ds(pl.multiple_of(t * tile, tile), tile)
            at = (t // 2, t % 2)
            gwide[:, cols] = (
                dot_nt(gq[...], wa[(QUERY,) + at].reshape(tile, width))
                + dot_nt(gk[...], wa[(KEY,) + at].reshape(tile, width))
                + dot_nt(gv[...], wa[(VALUE,) + at].reshape(tile, width))
            )

        @pl.loop(0, steps, unroll=True)
        def _(i):
            part = pl.ds(i * rows, rows)
            hidden = x_ref[part].astype(f32)
            inv = r_one[part][:, :1]
            g_n1 = gwide[part]
            add_gain(0, jnp.sum(g_n1 * hidden * inv, axis=0, keepdims=True))
            scaled = g_n1 * gain_row(0)
            inner = jnp.mean(scaled * hidden, axis=-1, keepdims=True)
            grad = gmid[part] + inv * scaled - hidden * (inv * inv * inv * inner)
            for k in range(width // 128):
                spread = pl.ds(i * rows * (width // 128) + k, rows, width // 128)
                ig_ref[spread, :] = grad[:, k * 128 : (k + 1) * 128]

        local("keep_ig", ig_ref.at[pl.ds(0, ig_hbm.shape[0])], ig_hbm)

        @pl.loop(1, 16)
        def _(r):
            gain_sum_copy(r).start()

    @action("gain")
    def _():
        gsum_r[15] = gsum_s[f // per_block]

        wait_block(gsum_r.at[pl.ds(0, 15)], gsem.at[2])
        wait_block(gsum_r.at[pl.ds(0, 15)], gsem.at[3])

        @pl.loop(1, 16)
        def _(r):
            gsum_r[15] += gsum_r[r - 1]

        gain_sum = jnp.where(f % per_block == 0, 1.0, 0.0) * gsum_r[15][:, :rows]
        for b in range(1, per_block):
            gain_sum += jnp.where(f % per_block == b, 1.0, 0.0) * gsum_r[15][:, b * rows : (b + 1) * rows]
        gain_one_out[...] = gain_sum[0:1]
        gain_two_out[...] = gain_sum[1:2]

    @action("out")
    def _():
        for name in ("u0n", "u1n", "u0t", "u1t"):
            sent[name].wait_recv()

        @pl.loop(0, steps, unroll=True)
        def _(i):
            part = pl.ds(i * rows, rows)
            at = (i // 2, i % 2)
            total = po_s[(z, x) + at].astype(f32)
            for k in (0, 2):
                total += po_r[(k,) + at].astype(f32)
            out_ref[part] = (mask[part][:, :1] * (hmid[part] + total)).astype(bf16)

        local("keep_out", out_ref, out_hbm)

    for name in ORDER:
        actions[name]()

    for letter, g in GROUPS.items():
        wait_block(wa.at[g, :, :, :, c], ssem.at[take(0, letter + "c")])
        wait_block(wa.at[g, :, :, x, c], ssem.at[take(0, letter + "x")])
        wait_block(wa.at[g, :, z, x, c], ssem.at[take(0, letter + "z")])
        wait_block(wa.at[(g,) + slab()], ssem.at[take(0, letter + "s")])
    for flips in blocks.values():
        wait_block(wgu_all.at[slab()], ssem.at[gu_sems[flips][0]])
    local_only = ("down", "x_in", "cot_in")
    free(*(name for name in sent if name not in local_only and not name.startswith(("keep", "dkeep")) and name[1:] != "own"))
    for ref, group in ((pg_r, "p"), (po_r, "u"), (gu_core, "w"), (attn_core, "W"), (attn_x, "X"), (attn_z, "Z")):
        wait_block(ref, ssem.at[take(0, group)])
    sent["dy"].wait_recv()
    sent["dkeep"].wait()
    sent["keep_out"].wait()
    sent["keep_ig"].wait()
    wait_block(gu_grad.at[slab()], gu_sems["keep"])
    for flips in blocks.values():
        if flips[0] == 0:
            wait_block(gu_grad.at[slab()], ssem.at[gu_sems[flips + (0,)][0]])
            wait_block(gu_grad.at[slab()], rsem.at[gu_sems[flips + (0,)][1]])
    for letter in GROUPS:
        sent["keep" + letter].wait()
    wait_block(attn_z.at[pl.ds(0, 2)], ssem.at[take(0, "S")])
    wait_block(attn_out.at[1], rsem.at[take(1, "S")])


def square_layer(inputs, frame_flags, attn_gain, qkv_weight, out_weight, ffn_gain, gate_up_weight, down_weight, cotangent):
    tokens, _, width = inputs.shape
    rows = qkv_weight.shape[2]
    block = width
    f32, bf16 = jnp.float32, jnp.bfloat16
    lane_block = 128
    lane_blocks = width // lane_block
    vmem = pl.BlockSpec(memory_space=pltpu.VMEM)
    anywhere = pl.BlockSpec(memory_space=pl.ANY)
    unit = (2, 2, 2, 2, rows, width)
    double = (2, 2, 2, 2, rows, 2 * block)
    own = (tokens, width)
    scratch = [
        pltpu.VMEM((4,) + unit, bf16),
        pltpu.VMEM(double, bf16),
        pltpu.VMEM(unit, bf16),
        pltpu.VMEM(unit, bf16),
        pltpu.VMEM(unit, bf16),
        pltpu.VMEM(unit, bf16),
        pltpu.VMEM(double, bf16),
        pltpu.VMEM(unit, bf16),
        pltpu.VMEM((3, 2, 2, rows, width), bf16),
        pltpu.VMEM(unit, bf16),
        pltpu.VMEM((3, 2, 2, rows, width), bf16),
        pltpu.VMEM((2, 2, 2, rows, 2 * block), bf16),
        pltpu.VMEM((2, 2, rows, 2 * block), bf16),
        pltpu.VMEM((2, 2, 2, rows, width), bf16),
        pltpu.VMEM((4, 2, 2, 2, rows, width), bf16),
        pltpu.VMEM((4, 2, 2, rows, width), bf16),
        pltpu.VMEM((4, 2, rows, width), bf16),
        pltpu.VMEM(own, bf16),
        pltpu.VMEM(own, bf16),
        pltpu.VMEM(own, bf16),
        pltpu.VMEM(own, bf16),
        pltpu.VMEM(own, bf16),
        pltpu.VMEM(own, bf16),
        pltpu.VMEM(own, bf16),
        pltpu.VMEM(own, f32),
        pltpu.VMEM(own, bf16),
        pltpu.VMEM(own, bf16),
        pltpu.VMEM(own, bf16),
        pltpu.VMEM(own, bf16),
        pltpu.VMEM(own, bf16),
        pltpu.VMEM(own, bf16),
        pltpu.VMEM(own, bf16),
        pltpu.VMEM(own, f32),
        pltpu.VMEM(own, bf16),
        pltpu.VMEM(own, f32),
        pltpu.VMEM(own, f32),
        pltpu.VMEM((tokens, 128), f32),
        pltpu.VMEM((16, lane_block), bf16),
        pltpu.VMEM((tokens, 128), f32),
        pltpu.VMEM((tokens, 128), f32),
        pltpu.VMEM((tokens, 128), f32),
        pltpu.VMEM((tokens, 128), f32),
        pltpu.VMEM((15, 16, lane_block), bf16),
        pltpu.VMEM((lane_blocks, 16, lane_block), f32),
        pltpu.VMEM((lane_blocks, 8, lane_block), f32),
        pltpu.VMEM((16, 8, lane_block), f32),
        pltpu.VMEM((width, 128), bf16),
        pltpu.VMEM((128, width), bf16),
        pltpu.VMEM(own, bf16),
        pltpu.VMEM(own, bf16),
        pltpu.VMEM(own, bf16),
        pltpu.VMEM(((tokens + 1) * lane_blocks, lane_block), f32),
        pltpu.SemaphoreType.DMA((SEND_SEMS,)),
        pltpu.SemaphoreType.DMA((RECV_SEMS,)),
        pltpu.SemaphoreType.DMA((16,)),
        pltpu.SemaphoreType.DMA((4,)),
    ]
    outs = pl.pallas_call(
        square_kernel,
        out_shape=(
            jax.ShapeDtypeStruct(own, bf16),
            jax.ShapeDtypeStruct((tokens * lane_blocks, lane_block), f32),
            jax.ShapeDtypeStruct((1, rows), f32),
            jax.ShapeDtypeStruct((1, rows), f32),
            jax.ShapeDtypeStruct((rows, 8 * block), bf16),
            jax.ShapeDtypeStruct((2, 2, 2, rows, width), bf16),
            jax.ShapeDtypeStruct((2, rows, 4 * width), bf16),
        ),
        in_specs=[anywhere] * 2 + [vmem] * 3 + [anywhere] * 4,
        out_specs=(anywhere, anywhere, vmem, vmem, anywhere, anywhere, anywhere),
        scratch_shapes=scratch,
        compiler_params=pltpu.CompilerParams(
            collective_id=0, has_side_effects=True, vmem_limit_bytes=VMEM_BYTES
        ),
        cost_estimate=pl.CostEstimate(flops=26 * 10**9, bytes_accessed=2**23, transcendentals=2**21),
    )(
        inputs[:, 0], cotangent[:, 0], frame_flags.reshape(tokens // lane_block, lane_block), attn_gain[0], ffn_gain[0],
        qkv_weight[0, 0], out_weight[0, 0], gate_up_weight[0, 0], down_weight[0, 0].reshape(2, 2, rows, width),
    )
    result, input_grad, gain_one, gain_two, gu, down, attn = outs
    grid = 2

    def by_rows(shape):
        return pl.BlockSpec((shape[0] // grid,) + shape[1:], lambda i: (i, 0))

    def pair(shape):
        return pl.BlockSpec((2, shape[0] // grid) + shape[1:], lambda i: (0, i, 0))

    whole = pl.BlockSpec((1, rows), lambda i: (0, 0))
    thin = (tokens * lane_blocks, lane_block)
    result, input_grad, qkv, out, gu, down, gain_one, gain_two = pl.pallas_call(
        finish_kernel,
        grid=(grid,),
        out_shape=(
            jax.ShapeDtypeStruct(own, bf16),
            jax.ShapeDtypeStruct(thin, f32),
            jax.ShapeDtypeStruct((rows, 3 * width), f32),
            jax.ShapeDtypeStruct((rows, width), f32),
            jax.ShapeDtypeStruct((rows, 8 * block), f32),
            jax.ShapeDtypeStruct(own, f32),
            jax.ShapeDtypeStruct((1, rows), f32),
            jax.ShapeDtypeStruct((1, rows), f32),
        ),
        in_specs=[by_rows(own), by_rows(thin), whole, whole, by_rows((rows, 8 * block)), pair(own), pair((rows, 4 * width))],
        out_specs=[by_rows(own), by_rows(thin), by_rows((rows, 3 * width)), by_rows((rows, width)),
                   by_rows((rows, 8 * block)), by_rows(own), whole, whole],
        compiler_params=pltpu.CompilerParams(vmem_limit_bytes=VMEM_BYTES),
    )(result, input_grad, gain_one, gain_two, gu, down.reshape((2,) + own), attn)
    return (
        result[:, None],
        input_grad.reshape(tokens, 1, width),
        gain_one[None],
        qkv[None, None],
        out[None, None],
        gain_two[None],
        gu[None, None],
        down[None, None],
    )


def finish_kernel(
    result, input_grad, gain_one, gain_two, gu, down, attn,
    result_out, input_grad_out, qkv_out, out_out, gu_out, down_out, gain_one_out, gain_two_out,
):
    f32 = jnp.float32
    width = out_out.shape[1]
    result_out[...] = result[...]
    input_grad_out[...] = input_grad[...]
    gu_out[...] = gu[...].astype(f32)
    down_out[...] = down[0].astype(f32) + down[1].astype(f32)
    total = attn[0].astype(f32) + attn[1].astype(f32)
    qkv_out[...] = total[:, : 3 * width]
    out_out[...] = total[:, 3 * width :]
    gain_one_out[...] = gain_one[...]
    gain_two_out[...] = gain_two[...]


VMEM_BYTES = 62 * 2**20


def run_layer(axes, *args):
    inputs, qkv_weight, down_weight = args[0], args[3], args[7]
    tokens, places, width = inputs.shape
    rows = qkv_weight.shape[2]
    square = (
        axes["fsdp"] == 16
        and axes["pos"] == 2
        and places == 1
        and qkv_weight.shape[0] == 1
        and tokens == 4 * rows
        and down_weight.shape[2] == 4 * rows
        and 128 % rows == 0
    )
    return square_layer(*args) if square else on_device(*args)


def solution(mesh):
    in_specs = (
        P("fsdp", "pos", None),
        P("fsdp"),
        P(None, "pos", "fsdp"),
        P(None, "pos", "fsdp", None),
        P(None, "pos", "fsdp", None),
        P(None, "pos", "fsdp"),
        P(None, "pos", "fsdp", None),
        P(None, "pos", "fsdp", None),
        P("fsdp", "pos", None),
    )
    out_specs = (
        P("fsdp", "pos", None),
        P("fsdp", "pos", None),
        P(None, "pos", "fsdp"),
        P(None, "pos", "fsdp", None),
        P(None, "pos", "fsdp", None),
        P(None, "pos", "fsdp"),
        P(None, "pos", "fsdp", None),
        P(None, "pos", "fsdp", None),
    )
    return jax.shard_map(
        functools.partial(run_layer, dict(mesh.shape)), mesh=mesh, in_specs=in_specs, out_specs=out_specs, check_vma=False
    )
```

```python
import functools
import math

import jax
import jax.numpy as jnp
from jax import lax
from jax.experimental import pallas as pl
from jax.experimental.pallas import tpu as pltpu
from jax.sharding import PartitionSpec as P

D = 1024
HEADS = 16
HEAD_DIM = 64
FF = 4096


EPSILON = 1e-06
MASKED = -1e30
PRECISE = lax.Precision.HIGHEST


def rms_parts(hidden, gain_row):
    inv_rms = lax.rsqrt(jnp.mean(hidden * hidden, axis=-1, keepdims=True) + EPSILON)
    return (hidden * inv_rms * gain_row[None], inv_rms)


def rms_back(grad_rows, hidden, inv_rms, gain_row):
    scaled = grad_rows * gain_row[None]
    gain_grad = jnp.sum(grad_rows * hidden * inv_rms, axis=0)
    inner_mean = jnp.mean(scaled * hidden, axis=-1, keepdims=True)
    return (inv_rms * scaled - hidden * inv_rms**3 * inner_mean, gain_grad)


def apply_rows(left_side, weight):
    return jnp.einsum("fpd,pde->fpe", left_side, weight, preferred_element_type=jnp.float32)


def apply_back(grad_rows, weight):
    return jnp.einsum("fpe,pde->fpd", grad_rows, weight, preferred_element_type=jnp.float32)


def outer_sum(left_side, grad_rows):
    return jnp.einsum("fpd,fpe->pde", left_side, grad_rows, preferred_element_type=jnp.float32)


def split_heads(rows):
    return rows.reshape(rows.shape[0], rows.shape[1], HEADS, HEAD_DIM)


def attention_weights(attn_gain, qkv_weight, out_weight, layer_idx):
    return (
        lax.all_gather(attn_gain[layer_idx], "fsdp", axis=1, tiled=True),
        lax.all_gather(qkv_weight[layer_idx], "fsdp", axis=1, tiled=True),
        lax.all_gather(out_weight[layer_idx], "fsdp", axis=1, tiled=True),
    )


def ffn_weights(ffn_gain, gate_up_weight, down_weight, layer_idx):
    return (
        lax.all_gather(ffn_gain[layer_idx], "fsdp", axis=1, tiled=True),
        lax.all_gather(gate_up_weight[layer_idx], "fsdp", axis=1, tiled=True),
        lax.all_gather(down_weight[layer_idx], "fsdp", axis=1, tiled=True),
    )


def attention_forward(qkv_rows):
    frames, places = (qkv_rows.shape[0], qkv_rows.shape[1])
    pos_count = lax.axis_size("pos")
    frame_part = frames // pos_count
    outgoing = qkv_rows.reshape(pos_count, frame_part, places, 3 * D)
    frame_qkv = lax.all_to_all(outgoing, "pos", split_axis=0, concat_axis=2, tiled=True)[0].astype(
        jnp.float32
    )
    whole_places = frame_qkv.shape[1]
    queries = split_heads(frame_qkv[..., :D])
    keys_all = split_heads(frame_qkv[..., D : 2 * D])
    values_all = split_heads(frame_qkv[..., 2 * D :])
    scores = jnp.einsum("fphe,fjhe->fhpj", queries, keys_all, precision=PRECISE) / math.sqrt(
        HEAD_DIM
    )
    causal = jnp.arange(whole_places)[:, None] >= jnp.arange(whole_places)[None, :]
    scores = jnp.where(causal, scores, MASKED)
    row_max = jnp.max(scores, axis=-1, keepdims=True)
    exponent = jnp.exp(scores - row_max)
    attn_probs = exponent / jnp.sum(exponent, axis=-1, keepdims=True)
    mixed_heads = jnp.einsum("fhpj,fjhe->fphe", attn_probs, values_all, precision=PRECISE)
    mixed_frames = mixed_heads.reshape(frame_part, whole_places, D).astype(jnp.bfloat16)
    returned = lax.all_to_all(mixed_frames[None], "pos", split_axis=2, concat_axis=0, tiled=True)
    return (returned.reshape(frames, places, D), (queries, keys_all, values_all, attn_probs))


def attention_backward(grad_mixed, attn_keep):
    queries, keys_all, values_all, attn_probs = attn_keep
    frames, places = (grad_mixed.shape[0], grad_mixed.shape[1])
    pos_count = lax.axis_size("pos")
    frame_part = frames // pos_count
    outgoing = grad_mixed.reshape(pos_count, frame_part, places, D)
    grad_frames = lax.all_to_all(
        outgoing.astype(jnp.bfloat16), "pos", split_axis=0, concat_axis=2, tiled=True
    ).astype(outgoing.dtype)[0]
    whole_places = grad_frames.shape[1]
    grad_heads = split_heads(grad_frames)
    grad_values = jnp.einsum("fhpj,fphe->fjhe", attn_probs, grad_heads, precision=PRECISE)
    grad_probs = jnp.einsum("fphe,fjhe->fhpj", grad_heads, values_all, precision=PRECISE)
    grad_scores = (
        attn_probs
        * (grad_probs - jnp.sum(attn_probs * grad_probs, axis=-1, keepdims=True))
        / math.sqrt(HEAD_DIM)
    )
    grad_queries = jnp.einsum("fhpj,fjhe->fphe", grad_scores, keys_all, precision=PRECISE)
    grad_keys = jnp.einsum("fhpj,fphe->fjhe", grad_scores, queries, precision=PRECISE)
    frame_grads = jnp.concatenate(
        [
            grad_queries.reshape(frame_part, whole_places, D),
            grad_keys.reshape(frame_part, whole_places, D),
            grad_values.reshape(frame_part, whole_places, D),
        ],
        axis=-1,
    ).astype(jnp.bfloat16)
    returned = lax.all_to_all(frame_grads[None], "pos", split_axis=2, concat_axis=0, tiled=True)
    return returned.reshape(frames, places, 3 * D)


def layer_forward(hidden, frame_mask, attn_set, ffn_set):
    gain_one, qkv_full, out_full = attn_set
    gain_two, gate_up_full, down_full = ffn_set
    normed, inv_one = rms_parts(hidden, gain_one.astype(jnp.float32))
    normed_low = normed.astype(jnp.bfloat16)
    qkv_rows = apply_rows(normed_low, qkv_full).astype(jnp.bfloat16)
    mixed_low, attn_keep = attention_forward(qkv_rows)
    hidden_mid = hidden + apply_rows(mixed_low, out_full)
    normed_two, inv_two = rms_parts(hidden_mid, gain_two.astype(jnp.float32))
    normed_two_low = normed_two.astype(jnp.bfloat16)
    gate_up = apply_rows(normed_two_low, gate_up_full)
    gate_part = gate_up[..., :FF]
    up_part = gate_up[..., FF:]
    act_low = (jax.nn.silu(gate_part) * up_part).astype(jnp.bfloat16)
    result = frame_mask * (hidden_mid + apply_rows(act_low, down_full))
    kept_state = (
        hidden,
        inv_one,
        normed_low,
        attn_keep,
        mixed_low,
        hidden_mid,
        inv_two,
        normed_two_low,
        gate_part,
        up_part,
        act_low,
    )
    return (result, kept_state)


def layer_backward(grad_out, frame_mask, kept_state, ffn_set, fetch_attn):
    (
        hidden,
        inv_one,
        normed_low,
        attn_keep,
        mixed_low,
        hidden_mid,
        inv_two,
        normed_two_low,
        gate_part,
        up_part,
        act_low,
    ) = kept_state
    gain_two, gate_up_full, down_full = ffn_set
    grad_sum = frame_mask * grad_out
    grad_ffn = grad_sum.astype(jnp.bfloat16)
    down_grad = outer_sum(act_low, grad_ffn)
    down_shard = lax.psum_scatter(down_grad, "fsdp", scatter_dimension=1, tiled=True)
    grad_act = apply_back(grad_ffn, down_full)
    sigmoid_gate = jax.nn.sigmoid(gate_part)
    grad_gate = grad_act * up_part * sigmoid_gate * (1.0 + gate_part * (1.0 - sigmoid_gate))
    grad_up = grad_act * gate_part * sigmoid_gate
    grad_gu = jnp.concatenate([grad_gate, grad_up], axis=-1).astype(jnp.bfloat16)
    gate_up_grad = outer_sum(normed_two_low, grad_gu)
    grad_norm_two = apply_back(grad_gu, gate_up_full)
    grad_mid_norm, gain_two_grad = rms_back(
        grad_norm_two, hidden_mid, inv_two, gain_two.astype(jnp.float32)
    )
    ffn_shards = (
        lax.psum_scatter(gain_two_grad, "fsdp", scatter_dimension=1, tiled=True),
        lax.psum_scatter(gate_up_grad, "fsdp", scatter_dimension=1, tiled=True),
    )
    gain_one, qkv_full, out_full = fetch_attn()
    grad_mid = grad_sum + grad_mid_norm
    grad_attn = grad_mid.astype(jnp.bfloat16)
    out_grad = outer_sum(mixed_low, grad_attn)
    grad_mixed = apply_back(grad_attn, out_full)
    grad_qkv = attention_backward(grad_mixed, attn_keep)
    qkv_grad = outer_sum(normed_low, grad_qkv)
    grad_norm_one = apply_back(grad_qkv, qkv_full)
    grad_in_norm, gain_one_grad = rms_back(
        grad_norm_one, hidden, inv_one, gain_one.astype(jnp.float32)
    )
    attn_shards = (
        lax.psum_scatter(gain_one_grad, "fsdp", scatter_dimension=1, tiled=True),
        lax.psum_scatter(qkv_grad, "fsdp", scatter_dimension=1, tiled=True),
        lax.psum_scatter(out_grad, "fsdp", scatter_dimension=1, tiled=True),
    )
    grad_in = grad_mid + grad_in_norm
    return (
        grad_in,
        (attn_shards[0], attn_shards[1], attn_shards[2], ffn_shards[0], ffn_shards[1], down_shard),
    )


def on_device(
    inputs,
    frame_flags,
    attn_gain,
    qkv_weight,
    out_weight,
    ffn_gain,
    gate_up_weight,
    down_weight,
    cotangent,
):
    layer_total = qkv_weight.shape[0]
    frame_mask = frame_flags.astype(jnp.float32)[:, None, None]
    hidden = inputs.astype(jnp.float32)
    layer_idx = 0
    attn_set = attention_weights(attn_gain, qkv_weight, out_weight, layer_idx)
    ffn_set = ffn_weights(ffn_gain, gate_up_weight, down_weight, layer_idx)
    hidden, kept_state = layer_forward(hidden, frame_mask, attn_set, ffn_set)
    states_all = [kept_state]
    grad_rows = cotangent.astype(jnp.float32)
    layer_grads = [None] * layer_total
    for layer_idx in reversed(range(layer_total)):
        ffn_set = ffn_weights(ffn_gain, gate_up_weight, down_weight, layer_idx)
        fetch_attn = gather_later(attn_gain, qkv_weight, out_weight, layer_idx)
        grad_rows, layer_grads[layer_idx] = layer_backward(
            grad_rows, frame_mask, states_all[layer_idx], ffn_set, fetch_attn
        )
    stacked = [jnp.stack([grad_set[column] for grad_set in layer_grads]) for column in range(6)]
    return (
        hidden.astype(jnp.bfloat16),
        grad_rows,
        stacked[0],
        stacked[1],
        stacked[2],
        stacked[3],
        stacked[4],
        stacked[5],
    )


def gather_later(attn_gain, qkv_weight, out_weight, layer_idx):

    def fetched():
        return attention_weights(attn_gain, qkv_weight, out_weight, layer_idx)

    return fetched


KEY, VALUE, QUERY, OUT = 0, 1, 2, 3
GROUPS = {"k": KEY, "v": VALUE, "q": QUERY, "o": OUT}
SEND_SEMS, RECV_SEMS = 51, 89
ROUTES = {"p0": "z", "p1": "z", "u0": "x", "u1": "x"}
MESH = pl.DeviceIdType.MESH


class Names:
    def __getattr__(self, name):
        return name


step = Names()

ORDER = (
    step.v_to_c, step.mask, step.k_to_x, step.k_to_z, step.k_to_c, step.v_to_x, step.o_to_z, step.k_to_s,
    step.v_to_s, step.q_to_s, step.o_to_c, step.norm, step.gx, step.k_from_s, step.q_to_c, step.v_to_z,
    step.q_to_x, step.o_to_s, step.k_from_sz, step.k_from_z, step.v_from_s, step.q_to_z, step.v_from_sz,
    step.o_from_s, step.gz, step.q_from_z, step.v_from_z, step.gs, step.q_from_s, step.v_from_x, step.v_from_c,
    step.ends, step.gz_from, step.d_to, step.k_from_x, step.gd, step.v_rows, step.q_from_sz, step.cz, step.o_to_x,
    step.cx, step.g_own, step.q_from_x, step.o_from_z, step.o_from_sz, step.g_own_from, step.q_from_c,
    step.k_from_c, step.gx_from, step.k_rows, step.q_rows, step.gzs_from, step.attn, step.o_from_x, step.o_from_c,
    step.mid, step.czx, step.gd_from, step.d_from, step.gs_from, step.nz, step.nx, step.gxs_from, step.gds_from,
    step.nzx, step.ffn, step.f2, step.p1n, step.f1, step.b1, step.u1n, step.p0n, step.b2, step.f0, step.f3,
    step.p1f, step.u0n, step.b3, step.w11, step.w01, step.p0f, step.u0f, step.y11, step.w10, step.p1t, step.b0,
    step.w00, step.u0t, step.p0t, step.u1f, step.dg, step.dy, step.gmid, step.gmix, step.Wo, step.gk, step.u1t,
    step.Xo, step.y01, step.Wq, step.y10, step.Wv, step.Xq, step.Xv, step.Zo, step.Wk, step.Xk, step.ig, step.Zq,
    step.out, step.Zv, step.Sq, step.So, step.Zk, step.Sv, step.y00, step.gain, step.Sk,
)


def flip(bit, change):
    return bit + change - 2 * bit * change


def square_kernel(
    x_in, cot_in, flags_ref, gain_one_ref, gain_two_ref, wqkv, wout, wgu, wd,
    out_hbm, ig_hbm, gain_one_out, gain_two_out, gu_out, down_out, attn_out,
    wa, wgu_all, wd_all, n2_all, g_all, act_all, ggu_all,
    po_s, po_r, pg_s, pg_r, gu_core, gu_cross, down_core, attn_core, attn_x, attn_z,
    normed, qb, kb, vb, krem, vrem, mixed, hmid, gv_s, gk_s, gv_r, gk_r,
    gq, gk, gv, gmid, gattn, hold_k, gwide, mask, gain_ref, p_own, p_rem, r_one, r_two,
    gain_r, gain_f, gsum_s, gsum_r, ends, ends_t,
    x_ref, cot_ref, out_ref, ig_ref, ssem, rsem, lsem, gsem,
):
    tokens, width = x_ref.shape
    rows = width // 16
    block = 4 * width // 4
    half = block // 2
    ff = 4 * width
    f = lax.axis_index("fsdp")
    y = lax.axis_index("pos")
    c = f % 2
    x = (f // 2) % 2
    z = (f // 4) % 2
    s = f // 8
    f32, bf16 = jnp.float32, jnp.bfloat16
    every = slice(None)
    steps = tokens // rows
    tile = 256
    tiles = width // tile
    scale = 1.0 / math.sqrt(HEAD_DIM)
    lane_block = 128
    per_block = lane_block // rows

    def peer(ds=0, dz=0, dx=0, dc=0):
        return flip(s, ds) * 8 + flip(z, dz) * 4 + flip(x, dx) * 2 + flip(c, dc)

    def slab(ds=0, dz=0, dx=0, dc=0):
        return flip(s, ds), flip(z, dz), flip(x, dx), flip(c, dc)

    counter = [0, 0, 0]
    sent = {}
    actions = {}

    def action(name):
        def keep(fn):
            actions[name] = fn

        return keep

    groups = {}
    freed = set()

    def take(which, group=None):
        if group is not None and (which, group) in groups:
            return groups[which, group]
        counter[which] += 1
        assert counter[which] <= (SEND_SEMS, RECV_SEMS)[which]
        groups[which, group] = counter[which] - 1
        return counter[which] - 1

    def link(name, src, dst, to, to_y=None, send_group=None, recv_group=None):
        copy = pltpu.make_async_remote_copy(
            src_ref=src, dst_ref=dst, send_sem=ssem.at[take(0, send_group)], recv_sem=rsem.at[take(1, recv_group)],
            device_id=(to, y if to_y is None else to_y), device_id_type=MESH,
        )
        copy.start()
        sent[name] = copy
        if send_group is not None:
            freed.add(name)

    def local(name, src, dst):
        counter[2] += 1
        copy = pltpu.make_async_copy(src, dst, lsem.at[counter[2] - 1])
        copy.start()
        sent[name] = copy

    def wait_block(ref, sem):
        pltpu.make_async_copy(ref, ref, sem).wait()

    def free(*names):
        for name in names:
            if name not in freed:
                freed.add(name)
                sent[name].wait_send()

    def dot(a, b):
        return jnp.dot(a, b, preferred_element_type=f32)

    def dot_nt(a, b):
        return lax.dot_general(a, b, (((1,), (1,)), ((), ())), preferred_element_type=f32)

    def split(v):
        high = v.astype(bf16)
        return high, (v - high.astype(f32)).astype(bf16)

    def head_sum(v):
        high, low = split(v)
        return dot(high, ends[...]) + dot(low, ends[...])

    def head_spread(p):
        high, low = split(p)
        return dot(high, ends_t[...]) + dot(low, ends_t[...])

    def add_rows(ref, came):
        ref[...] = (ref[...].astype(f32) + came[...].astype(f32)).astype(bf16)

    local("x_in", x_in, x_ref)
    local("cot_in", cot_in, cot_ref)

    barrier = pltpu.get_barrier_semaphore()

    @pl.loop(1, 16)
    def _(r):
        pl.semaphore_signal(barrier, inc=1, device_id=(lax.rem(f + r, 16), y), device_id_type=MESH)

    pl.semaphore_signal(barrier, inc=1, device_id=(f, 1 - y), device_id_type=MESH)

    lanes = lax.broadcasted_iota(jnp.int32, gain_ref.shape, 1) // rows == f % per_block
    sublane = lax.broadcasted_iota(jnp.int32, gain_ref.shape, 0)

    def lane_tile(ref):
        return jnp.concatenate([ref[...].astype(f32)] * per_block, axis=1)

    gains = jnp.where(sublane == 0, lane_tile(gain_one_ref), jnp.where(sublane == 1, lane_tile(gain_two_ref), 0.0))
    gain_ref[...] = jnp.where(lanes, gains, 0.0).astype(bf16)

    pl.semaphore_wait(barrier, 16)

    def gain_copy(r):
        return pltpu.make_async_remote_copy(
            src_ref=gain_ref, dst_ref=gain_r.at[r - 1], send_sem=gsem.at[0], recv_sem=gsem.at[1],
            device_id=(lax.rem(f + r, 16), y), device_id_type=MESH,
        )

    def gain_row(which):
        return jnp.concatenate([gain_f[i, which : which + 1, :] for i in range(gain_f.shape[0])], axis=1)

    def add_gain(which, value):
        for i in range(gsum_s.shape[0]):
            gsum_s[i, which : which + 1, :] += value[:, i * 128 : (i + 1) * 128]

    @pl.loop(1, 16)
    def _(r):
        gain_copy(r).start()

    own_cols = (
        wqkv.at[:, pl.ds(width, width)],
        wqkv.at[:, pl.ds(2 * width, width)],
        wqkv.at[:, pl.ds(0, width)],
        wout,
    )
    ways = {"s": (1, 0, 0, 0), "z": (0, 1, 0, 0), "x": (0, 0, 1, 0), "c": (0, 0, 0, 1)}

    def gather_actions(letter, g):
        def send(name, way, src, dst):
            recv_group = letter + "c" if way == "c" else None
            link(letter + name, src, dst, peer(*ways[way]), send_group=letter + way, recv_group=recv_group)

        def own(way):
            @action(letter + "_to_" + way)
            def _():
                send(way, way, own_cols[g], wa.at[(g,) + slab()])
                if way == "c":
                    local(letter + "own", own_cols[g], wa.at[(g,) + slab()])

        for way in ways:
            own(way)

        def pass_on(name, at, way):
            ref = wa.at[(g,) + slab(*at)]
            send(name, way, ref, ref)

        @action(letter + "_from_s")
        def _():
            sent[letter + "s"].wait_recv()
            pass_on("sz", (1, 0, 0, 0), "z")
            pass_on("sx", (1, 0, 0, 0), "x")
            pass_on("sc", (1, 0, 0, 0), "c")

        @action(letter + "_from_z")
        def _():
            sent[letter + "z"].wait_recv()
            pass_on("zx", (0, 1, 0, 0), "x")
            pass_on("zc", (0, 1, 0, 0), "c")

        @action(letter + "_from_sz")
        def _():
            sent[letter + "sz"].wait_recv()
            pass_on("szx", (1, 1, 0, 0), "x")
            pass_on("szc", (1, 1, 0, 0), "c")

        @action(letter + "_from_x")
        def _():
            for name, at in (("x", (0, 0, 1, 0)), ("sx", (1, 0, 1, 0)), ("zx", (0, 1, 1, 0)), ("szx", (1, 1, 1, 0))):
                sent[letter + name].wait_recv()
                pass_on(name + "c", at, "c")

        @action(letter + "_from_c")
        def _():
            sent[letter + "own"].wait()
            wait_block(wa.at[g, :, :, :, flip(c, 1)], rsem.at[take(1, letter + "c")])

    for letter, g in GROUPS.items():
        gather_actions(letter, g)

    @action("ends")
    def _():
        ends[...] = (
            lax.broadcasted_iota(jnp.int32, ends.shape, 0) // HEAD_DIM
            == lax.broadcasted_iota(jnp.int32, ends.shape, 1)
        ).astype(bf16)
        ends_t[...] = (
            lax.broadcasted_iota(jnp.int32, ends_t.shape, 1) // HEAD_DIM
            == lax.broadcasted_iota(jnp.int32, ends_t.shape, 0)
        ).astype(bf16)

    @action("mask")
    def _():
        sent["cot_in"].wait()
        for i in range(tokens // 128):
            flags = flags_ref[i : i + 1, :].astype(f32)
            mask[i * 128 : (i + 1) * 128] = jnp.broadcast_to(flags, (128, 128)).T
        g_all[z, x] = (cot_ref[...].astype(f32) * mask[:, :1]).astype(bf16).reshape(2, 2, rows, width)

    @action("norm")
    def _():
        sent["x_in"].wait()
        gain_f[...] = jnp.zeros_like(gain_f)
        gain_f[f // per_block] += gain_ref[...].astype(f32)

        wait_block(gain_r, gsem.at[0])
        wait_block(gain_r, gsem.at[1])

        @pl.loop(1, 16)
        def _(r):
            gain_f[lax.rem(f + 16 - r, 16) // per_block] += gain_r[r - 1].astype(f32)

        @pl.loop(0, steps, unroll=True)
        def _(i):
            part = pl.ds(i * rows, rows)
            hidden = x_ref[part].astype(f32)
            inv = lax.rsqrt(jnp.mean(hidden * hidden, axis=-1, keepdims=True) + EPSILON)
            r_one[part] = jnp.broadcast_to(inv, (rows, 128))
            normed[part] = (hidden * inv * gain_row(0)).astype(bf16)

    def project(left, g, dest):
        @pl.loop(0, tiles, unroll=True)
        def _(t):
            cols = pl.ds(pl.multiple_of(t * tile, tile), tile)
            dest[:, cols] = dot(left[...], wa[g, :, :, :, :, :, cols].reshape(width, tile)).astype(dest.dtype)

    @action("k_rows")
    def _():
        project(normed, KEY, kb)
        link("key", kb, krem, f, to_y=1 - y)

    @action("v_rows")
    def _():
        project(normed, VALUE, vb)
        link("value", vb, vrem, f, to_y=1 - y)

    @action("q_rows")
    def _():
        project(normed, QUERY, qb)

    blocks = {"s": (1, 0, 0), "x": (0, 0, 1), "z": (0, 1, 0), "d": (0, 1, 1)}
    gu_sems = {}

    def gu_in(flips):
        j = flip(z, flips[1]) * 2 + flip(x, flips[2])
        for u in range(2):
            for part in range(2):
                src = wgu.at[:, pl.ds(pl.multiple_of(u * ff + part * (ff // 2) + j * half, half), half)]
                yield src, wgu_all.at[s, z, x, c, :, pl.ds(u * block + part * half, half)]

    def pieces(flips, pairs):
        sem = take(0), take(1)
        for src, dst in pairs:
            pltpu.make_async_remote_copy(
                src_ref=src, dst_ref=dst, send_sem=ssem.at[sem[0]], recv_sem=rsem.at[sem[1]],
                device_id=(peer(*flips), y), device_id_type=MESH,
            ).start()
        return sem

    def pieces_local(pairs):
        counter[2] += 1
        sem = lsem.at[counter[2] - 1]
        for src, dst in pairs:
            pltpu.make_async_copy(src, dst, sem).start()
        return sem

    def gu_core_send(ref):
        link("gc", ref, ref, peer(dc=1), send_group="g", recv_group="g")

    def gu_actions(way, flips):
        @action("g" + way)
        def _():
            gu_sems[flips] = pieces(flips, gu_in(flips))

        @action("g" + way + "_from")
        def _():
            ref = wgu_all.at[slab(*flips)]
            wait_block(ref, rsem.at[gu_sems[flips][1]])
            if way != "s":
                link("g" + way + "s", ref, ref, peer(ds=1))
            gu_core_send(ref)

        @action("g" + way + "s_from")
        def _():
            sent["g" + way + "s"].wait_recv()
            ref = wgu_all.at[slab(1, flips[1], flips[2])]
            gu_core_send(ref)

    for way, flips in blocks.items():
        gu_actions(way, flips)

    @action("g_own")
    def _():
        gu_sems["own"] = pieces_local(gu_in((0, 0, 0)))

    @action("g_own_from")
    def _():
        ref = wgu_all.at[slab()]
        wait_block(ref, gu_sems["own"])
        gu_core_send(ref)

    @action("d_to")
    def _():
        own = wd_all.at[s, c]
        link("ds", wd, own, peer(ds=1))
        link("dc", wd, own, peer(dc=1))
        local("down", wd, own)

    @action("d_from")
    def _():
        sent["ds"].wait_recv()
        ref = wd_all.at[flip(s, 1), c]
        link("dsc", ref, ref, peer(dc=1))

    @action("ffn")
    def _():
        wait_block(wgu_all.at[:, :, :, flip(c, 1)], rsem.at[take(1, "g")])
        sent["down"].wait()
        sent["dc"].wait_recv()
        sent["dsc"].wait_recv()

    @action("cx")
    def _():
        link("cx", g_all.at[z, x], g_all.at[z, x], peer(dx=1))

    @action("cz")
    def _():
        link("cz", g_all.at[z, x], g_all.at[z, x], peer(dz=1))

    @action("czx")
    def _():
        sent["cz"].wait_recv()
        ref = g_all.at[flip(z, 1), x]
        link("czx", ref, ref, peer(dx=1))

    @action("attn")
    def _():
        sent["key"].wait_recv()
        sent["value"].wait_recv()

        @pl.loop(0, steps, unroll=True)
        def _(i):
            part = pl.ds(i * rows, rows)
            query = qb[part].astype(f32)
            own = head_sum(query * kb[part].astype(f32)) * scale
            far = jnp.where(y > 0, head_sum(query * krem[part].astype(f32)) * scale, MASKED)
            top = jnp.maximum(own, far)
            own = jnp.exp(own - top)
            far = jnp.exp(far - top)
            total = own + far
            own = own / total
            far = far / total
            p_own[part] = own
            p_rem[part] = far
            values = head_spread(own) * vb[part].astype(f32) + head_spread(far) * vrem[part].astype(f32)
            mixed[part] = values.astype(bf16)

    @action("mid")
    def _():
        project(mixed, OUT, hmid)

        @pl.loop(0, steps, unroll=True)
        def _(i):
            part = pl.ds(i * rows, rows)
            hidden = x_ref[part].astype(f32) + hmid[part]
            hmid[part] = hidden
            inv = lax.rsqrt(jnp.mean(hidden * hidden, axis=-1, keepdims=True) + EPSILON)
            r_two[part] = jnp.broadcast_to(inv, (rows, 128))
            n2_all[z, x, i // 2, i % 2] = (hidden * inv * gain_row(1)).astype(bf16)

    @action("nx")
    def _():
        link("nx", n2_all.at[z, x], n2_all.at[z, x], peer(dx=1))

    @action("nz")
    def _():
        link("nz", n2_all.at[z, x], n2_all.at[z, x], peer(dz=1))

    @action("nzx")
    def _():
        sent["nz"].wait_recv()
        ref = n2_all.at[flip(z, 1), x]
        link("nzx", ref, ref, peer(dx=1))

    def chunk_actions(i):
        dz, dx = i // 2, i % 2
        cz, cx = flip(z, dz), flip(x, dx)

        @action("f%d" % i)
        def _():
            if i == 1:
                sent["cx"].wait_recv()
                sent["nx"].wait_recv()
            if i == 3:
                sent["czx"].wait_recv()
                sent["nzx"].wait_recv()

            @pl.loop(0, tiles, unroll=True)
            def _(t):
                first = pl.multiple_of(t * tile, tile)
                cols = pl.ds(first, tile)
                n2 = n2_all[cz, cx].reshape(tokens, width)
                gate = dot(n2, wgu_all[:, :, :, :, :, cols].reshape(width, tile))
                up = dot(n2, wgu_all[:, :, :, :, :, pl.ds(block + first, tile)].reshape(width, tile))
                g_act = dot_nt(g_all[cz, cx].reshape(tokens, width), wd_all[t // 2, t % 2].reshape(tile, width))
                sig = 1.0 / (1.0 + jnp.exp(-gate))
                silu = gate * sig
                shape = (2, 2, rows, tile)
                act_all[cz, cx, :, :, :, cols] = (silu * up).astype(bf16).reshape(shape)
                g_gate = g_act * up * sig * (1.0 + gate * (1.0 - sig))
                ggu_all[cz, cx, :, :, :, cols] = g_gate.astype(bf16).reshape(shape)
                ggu_all[cz, cx, :, :, :, pl.ds(block + first, tile)] = (g_act * silu).astype(bf16).reshape(shape)

            @pl.loop(0, tiles, unroll=True)
            def _(t):
                cols = pl.ds(pl.multiple_of(t * tile, tile), tile)
                g_n2 = dot_nt(
                    ggu_all[cz, cx].reshape(tokens, 2 * block), wgu_all[t // 2, t % 2].reshape(tile, 2 * block)
                )
                pg_s[cz, cx, :, :, :, cols] = g_n2.astype(bf16).reshape(2, 2, rows, tile)

        @action("b%d" % i)
        def _():
            @pl.loop(0, tiles, unroll=True)
            def _(t):
                cols = pl.ds(pl.multiple_of(t * tile, tile), tile)
                part = dot(act_all[cz, cx].reshape(tokens, block), wd_all[:, :, :, :, :, cols].reshape(block, tile))
                po_s[cz, cx, :, :, :, cols] = part.astype(bf16).reshape(2, 2, rows, tile)

    for i in range(4):
        chunk_actions(i)

    def sum_actions(name, sums, came, h, way):
        first = {"x": (0, 1), "z": (1, 0)}[way]
        second = (first[1], first[0])
        one, two = peer(0, *first), peer(0, *second)

        def part(flips):
            return sums.at[flip(z, flips[0]), flip(x, flips[1]), h]

        @action(name + "n")
        def _():
            link(name + "n", part(first), came.at[0, h], one, send_group=name[0])

        @action(name + "f")
        def _():
            link(name + "f", part((1, 1)), came.at[1, h], one, send_group=name[0])

        @action(name + "t")
        def _():
            sent[name + "f"].wait_recv()

            @pl.loop(0, 2, unroll=True)
            def _(m):
                add_rows(part(second).at[m], came.at[1, h, m])

            link(name + "t", part(second), came.at[2, h], two, send_group=name[0])

    for name, way in ROUTES.items():
        sums, came = (pg_s, pg_r) if name[0] == "p" else (po_s, po_r)
        sum_actions(name, sums, came, int(name[1]), way)

    gu_grad = wgu_all
    down_grad = wd_all

    def gu_grad_out(flips):
        j = z * 2 + x
        for u in range(2):
            for part in range(2):
                src = gu_grad.at[slab(*flips) + (every, pl.ds(u * block + part * half, half))]
                cols = pl.ds(pl.multiple_of(u * ff + part * (ff // 2) + j * half, half), half)
                yield src, gu_out.at[:, cols]

    def tile_actions(ds, dz):
        tag = "%d%d" % (ds, dz)
        at = flip(s, ds), flip(z, dz)

        @action("w" + tag)
        def _():
            free("gxs", "gzs", "gds")
            if "tiles" not in freed:
                freed.add("tiles")
                wait_block(wgu_all.at[:, :, :, c], ssem.at[take(0, "g")])
            left = n2_all[:, :, :, :, :, pl.ds(pl.multiple_of((at[0] * 2 + at[1]) * tile, tile), tile)]
            left = left.reshape(4 * tokens, tile).T

            @pl.loop(0, block // tile, unroll=True)
            def _(n):
                wide = pl.ds(pl.multiple_of(n * 2 * tile, 2 * tile), 2 * tile)
                part = dot(left, ggu_all[:, :, :, :, :, wide].reshape(4 * tokens, 2 * tile))
                gu_grad[at[0], at[1], :, :, :, wide] = part.astype(bf16).reshape(2, 2, rows, 2 * tile)

            link("w" + tag, gu_grad.at[at[0], at[1], :, flip(c, 1)], gu_core.at[at], peer(dc=1), send_group="w")

        @action("y" + tag)
        def _():
            sent["w" + tag].wait_recv()
            if ds == 0:
                sent["y1%d" % dz].wait_recv()

            @pl.loop(0, 2, unroll=True)
            def _(m):
                ref = gu_grad.at[at[0], at[1], m, c]
                total = ref[...].astype(f32) + gu_core[at[0], at[1], m].astype(f32)
                if ds == 0:
                    total += gu_cross[at[1], m].astype(f32)
                ref[...] = total.astype(bf16)

            if ds == 1:
                link("y" + tag, gu_grad.at[at[0], at[1], :, c], gu_cross.at[at[1]], peer(ds=1))
                return
            for dx in (1, 0):
                flips = (0, dz, dx)
                if flips == (0, 0, 0):
                    gu_sems["keep"] = pieces_local(gu_grad_out(flips))
                else:
                    gu_sems[flips + (0,)] = pieces(flips, gu_grad_out(flips))

    for ds in (0, 1):
        for dz in (0, 1):
            tile_actions(ds, dz)

    @action("dg")
    def _():
        free("dsc")

        @pl.loop(0, tiles, unroll=True)
        def _(t):
            cols = pl.ds(pl.multiple_of(t * tile, tile), tile)
            left = act_all[:, :, :, :, :, cols].reshape(4 * tokens, tile).T

            @pl.loop(0, width // (2 * tile), unroll=True)
            def _(n):
                wide = pl.ds(pl.multiple_of(n * 2 * tile, 2 * tile), 2 * tile)
                part = dot(left, g_all[:, :, :, :, :, wide].reshape(4 * tokens, 2 * tile))
                down_grad[t // 2, t % 2, :, :, :, wide] = part.astype(bf16).reshape(2, 2, rows, 2 * tile)

        link("dg", down_grad.at[:, flip(c, 1)], down_core, peer(dc=1))

    @action("dy")
    def _():
        sent["dg"].wait_recv()

        @pl.loop(0, 8, unroll=2)
        def _(m):
            rest = ((m // 2) % 2, m % 2)
            add_rows(down_grad.at[(m // 4, c) + rest], down_core.at[(m // 4,) + rest])

        link("dy", down_grad.at[flip(s, 1), c], down_out.at[1], peer(ds=1))
        local("dkeep", down_grad.at[s, c], down_out.at[0])

    @action("gmid")
    def _():
        for name in ("p0n", "p1n", "p0t", "p1t"):
            sent[name].wait_recv()
        gsum_s[...] = jnp.zeros_like(gsum_s)

        @pl.loop(0, steps, unroll=True)
        def _(i):
            part = pl.ds(i * rows, rows)
            at = (i // 2, i % 2)
            g_n2 = pg_s[(z, x) + at].astype(f32)
            for k in (0, 2):
                g_n2 += pg_r[(k,) + at].astype(f32)
            hidden = hmid[part]
            inv = r_two[part][:, :1]
            add_gain(1, jnp.sum(g_n2 * hidden * inv, axis=0, keepdims=True))
            scaled = g_n2 * gain_row(1)
            inner = jnp.mean(scaled * hidden, axis=-1, keepdims=True)
            g_sum = cot_ref[part].astype(f32) * mask[part][:, :1]
            g_mid = g_sum + inv * scaled - hidden * (inv * inv * inv * inner)
            gmid[part] = g_mid
            gattn[part] = g_mid.astype(bf16)

    @action("gmix")
    def _():
        @pl.loop(0, tiles, unroll=True)
        def _(t):
            cols = pl.ds(pl.multiple_of(t * tile, tile), tile)
            gwide[:, cols] = dot_nt(gattn[...], wa[OUT, t // 2, t % 2].reshape(tile, width))

        @pl.loop(0, steps, unroll=True)
        def _(i):
            part = pl.ds(i * rows, rows)
            gv_s[part] = (head_spread(p_rem[part]) * gwide[part]).astype(bf16)

        link("gv", gv_s, gv_r, f, to_y=1 - y)

    @action("gk")
    def _():
        @pl.loop(0, steps, unroll=True)
        def _(i):
            part = pl.ds(i * rows, rows)
            gm = gwide[part]
            own, far = p_own[part], p_rem[part]
            gp_own = head_sum(gm * vb[part].astype(f32))
            gp_far = head_sum(gm * vrem[part].astype(f32))
            inner = own * gp_own + far * gp_far
            gs_own = head_spread(own * (gp_own - inner) * scale)
            gs_far = head_spread(far * (gp_far - inner) * scale)
            query = qb[part].astype(f32)
            gk_s[part] = (gs_far * query).astype(bf16)
            gq[part] = (gs_own * kb[part].astype(f32) + gs_far * krem[part].astype(f32)).astype(bf16)
            hold_k[part] = gs_own * query

        link("gk", gk_s, gk_r, f, to_y=1 - y)

    stage = {OUT: act_all, QUERY: n2_all, VALUE: g_all, KEY: ggu_all}
    out_cols = {QUERY: 0, KEY: 1, VALUE: 2, OUT: 3}

    def grad_actions(letter, g):
        def view(*at):
            ref = stage[g]
            if ref.shape[-1] != width:
                return ref.at[at + (every,) * (5 - len(at)) + (pl.ds(0, width),)]
            return ref.at[at]

        def add_into(count, at_of, came):
            @pl.loop(0, count, unroll=2)
            def _(m):
                add_rows(view(*at_of(m)), came(m))

        def weight_grad(left, right):
            @pl.loop(0, tiles, unroll=True)
            def _(t):
                cols = pl.ds(pl.multiple_of(t * tile, tile), tile)
                part = dot(left[:, cols].T, right[...])
                view(t // 2, t % 2)[...] = part.astype(bf16).reshape(2, 2, rows, width)

            link("W" + letter, view(every, every, every, flip(c, 1)), attn_core.at[g], peer(dc=1), send_group="W")

        @action("W" + letter)
        def _():
            if g == OUT:
                weight_grad(mixed, gattn)
            elif g == QUERY:
                free("nx", "nz", "nzx")
                weight_grad(normed, gq)
            elif g == VALUE:
                free("cx", "cz", "czx")
                sent["gv"].wait_recv()

                @pl.loop(0, steps, unroll=True)
                def _(i):
                    part = pl.ds(i * rows, rows)
                    gv[part] = (head_spread(p_own[part]) * gwide[part] + gv_r[part].astype(f32)).astype(bf16)

                weight_grad(normed, gv)
            else:
                sent["gk"].wait_recv()

                @pl.loop(0, steps, unroll=True)
                def _(i):
                    part = pl.ds(i * rows, rows)
                    gk[part] = (hold_k[part] + gk_r[part].astype(f32)).astype(bf16)

                weight_grad(normed, gk)

        @action("X" + letter)
        def _():
            sent["W" + letter].wait_recv()
            add_into(
                8,
                lambda m: (m // 4, (m // 2) % 2, m % 2, c),
                lambda m: attn_core.at[g, m // 4, (m // 2) % 2, m % 2],
            )
            link("X" + letter, view(every, every, flip(x, 1), c), attn_x.at[g], peer(dx=1), send_group="X")

        @action("Z" + letter)
        def _():
            sent["X" + letter].wait_recv()
            add_into(4, lambda m: (m // 2, m % 2, x, c), lambda m: attn_x.at[g, m // 2, m % 2])
            link("Z" + letter, view(every, flip(z, 1), x, c), attn_z.at[g], peer(dz=1), send_group="Z")

        @action("S" + letter)
        def _():
            sent["Z" + letter].wait_recv()
            add_into(2, lambda m: (m, z, x, c), lambda m: attn_z.at[g, m])
            cols = pl.ds(out_cols[g] * width, width)
            link("S" + letter, view(flip(s, 1), z, x, c), attn_out.at[1, :, cols], peer(ds=1), send_group="S", recv_group="S")
            local("keep" + letter, view(s, z, x, c), attn_out.at[0, :, cols])

    for letter, g in GROUPS.items():
        grad_actions(letter, g)

    def gain_sum_copy(r):
        to = lax.rem(f + r, 16)
        return pltpu.make_async_remote_copy(
            src_ref=gsum_s.at[to // per_block], dst_ref=gsum_r.at[r - 1],
            send_sem=gsem.at[2], recv_sem=gsem.at[3],
            device_id=(to, y), device_id_type=MESH,
        )

    @action("ig")
    def _():
        @pl.loop(0, tiles, unroll=True)
        def _(t):
            cols = pl.ds(pl.multiple_of(t * tile, tile), tile)
            at = (t // 2, t % 2)
            gwide[:, cols] = (
                dot_nt(gq[...], wa[(QUERY,) + at].reshape(tile, width))
                + dot_nt(gk[...], wa[(KEY,) + at].reshape(tile, width))
                + dot_nt(gv[...], wa[(VALUE,) + at].reshape(tile, width))
            )

        @pl.loop(0, steps, unroll=True)
        def _(i):
            part = pl.ds(i * rows, rows)
            hidden = x_ref[part].astype(f32)
            inv = r_one[part][:, :1]
            g_n1 = gwide[part]
            add_gain(0, jnp.sum(g_n1 * hidden * inv, axis=0, keepdims=True))
            scaled = g_n1 * gain_row(0)
            inner = jnp.mean(scaled * hidden, axis=-1, keepdims=True)
            grad = gmid[part] + inv * scaled - hidden * (inv * inv * inv * inner)
            for k in range(width // 128):
                spread = pl.ds(i * rows * (width // 128) + k, rows, width // 128)
                ig_ref[spread, :] = grad[:, k * 128 : (k + 1) * 128]

        local("keep_ig", ig_ref.at[pl.ds(0, ig_hbm.shape[0])], ig_hbm)

        @pl.loop(1, 16)
        def _(r):
            gain_sum_copy(r).start()

    @action("gain")
    def _():
        gsum_r[15] = gsum_s[f // per_block]

        wait_block(gsum_r.at[pl.ds(0, 15)], gsem.at[2])
        wait_block(gsum_r.at[pl.ds(0, 15)], gsem.at[3])

        @pl.loop(1, 16)
        def _(r):
            gsum_r[15] += gsum_r[r - 1]

        gain_sum = jnp.where(f % per_block == 0, 1.0, 0.0) * gsum_r[15][:, :rows]
        for b in range(1, per_block):
            gain_sum += jnp.where(f % per_block == b, 1.0, 0.0) * gsum_r[15][:, b * rows : (b + 1) * rows]
        gain_one_out[...] = gain_sum[0:1]
        gain_two_out[...] = gain_sum[1:2]

    @action("out")
    def _():
        for name in ("u0n", "u1n", "u0t", "u1t"):
            sent[name].wait_recv()

        @pl.loop(0, steps, unroll=True)
        def _(i):
            part = pl.ds(i * rows, rows)
            at = (i // 2, i % 2)
            total = po_s[(z, x) + at].astype(f32)
            for k in (0, 2):
                total += po_r[(k,) + at].astype(f32)
            out_ref[part] = (mask[part][:, :1] * (hmid[part] + total)).astype(bf16)

        local("keep_out", out_ref, out_hbm)

    for name in ORDER:
        actions[name]()

    for letter, g in GROUPS.items():
        wait_block(wa.at[g, :, :, :, c], ssem.at[take(0, letter + "c")])
        wait_block(wa.at[g, :, :, x, c], ssem.at[take(0, letter + "x")])
        wait_block(wa.at[g, :, z, x, c], ssem.at[take(0, letter + "z")])
        wait_block(wa.at[(g,) + slab()], ssem.at[take(0, letter + "s")])
    for flips in blocks.values():
        wait_block(wgu_all.at[slab()], ssem.at[gu_sems[flips][0]])
    local_only = ("down", "x_in", "cot_in")
    free(*(name for name in sent if name not in local_only and not name.startswith(("keep", "dkeep")) and name[1:] != "own"))
    for ref, group in ((pg_r, "p"), (po_r, "u"), (gu_core, "w"), (attn_core, "W"), (attn_x, "X"), (attn_z, "Z")):
        wait_block(ref, ssem.at[take(0, group)])
    sent["dy"].wait_recv()
    sent["dkeep"].wait()
    sent["keep_out"].wait()
    sent["keep_ig"].wait()
    wait_block(gu_grad.at[slab()], gu_sems["keep"])
    for flips in blocks.values():
        if flips[0] == 0:
            wait_block(gu_grad.at[slab()], ssem.at[gu_sems[flips + (0,)][0]])
            wait_block(gu_grad.at[slab()], rsem.at[gu_sems[flips + (0,)][1]])
    for letter in GROUPS:
        sent["keep" + letter].wait()
    wait_block(attn_z.at[pl.ds(0, 2)], ssem.at[take(0, "S")])
    wait_block(attn_out.at[1], rsem.at[take(1, "S")])


def square_layer(inputs, frame_flags, attn_gain, qkv_weight, out_weight, ffn_gain, gate_up_weight, down_weight, cotangent):
    tokens, _, width = inputs.shape
    rows = qkv_weight.shape[2]
    block = width
    f32, bf16 = jnp.float32, jnp.bfloat16
    lane_block = 128
    lane_blocks = width // lane_block
    vmem = pl.BlockSpec(memory_space=pltpu.VMEM)
    anywhere = pl.BlockSpec(memory_space=pl.ANY)
    unit = (2, 2, 2, 2, rows, width)
    double = (2, 2, 2, 2, rows, 2 * block)
    own = (tokens, width)
    scratch = [
        pltpu.VMEM((4,) + unit, bf16),
        pltpu.VMEM(double, bf16),
        pltpu.VMEM(unit, bf16),
        pltpu.VMEM(unit, bf16),
        pltpu.VMEM(unit, bf16),
        pltpu.VMEM(unit, bf16),
        pltpu.VMEM(double, bf16),
        pltpu.VMEM(unit, bf16),
        pltpu.VMEM((3, 2, 2, rows, width), bf16),
        pltpu.VMEM(unit, bf16),
        pltpu.VMEM((3, 2, 2, rows, width), bf16),
        pltpu.VMEM((2, 2, 2, rows, 2 * block), bf16),
        pltpu.VMEM((2, 2, rows, 2 * block), bf16),
        pltpu.VMEM((2, 2, 2, rows, width), bf16),
        pltpu.VMEM((4, 2, 2, 2, rows, width), bf16),
        pltpu.VMEM((4, 2, 2, rows, width), bf16),
        pltpu.VMEM((4, 2, rows, width), bf16),
        pltpu.VMEM(own, bf16),
        pltpu.VMEM(own, bf16),
        pltpu.VMEM(own, bf16),
        pltpu.VMEM(own, bf16),
        pltpu.VMEM(own, bf16),
        pltpu.VMEM(own, bf16),
        pltpu.VMEM(own, bf16),
        pltpu.VMEM(own, f32),
        pltpu.VMEM(own, bf16),
        pltpu.VMEM(own, bf16),
        pltpu.VMEM(own, bf16),
        pltpu.VMEM(own, bf16),
        pltpu.VMEM(own, bf16),
        pltpu.VMEM(own, bf16),
        pltpu.VMEM(own, bf16),
        pltpu.VMEM(own, f32),
        pltpu.VMEM(own, bf16),
        pltpu.VMEM(own, f32),
        pltpu.VMEM(own, f32),
        pltpu.VMEM((tokens, 128), f32),
        pltpu.VMEM((16, lane_block), bf16),
        pltpu.VMEM((tokens, 128), f32),
        pltpu.VMEM((tokens, 128), f32),
        pltpu.VMEM((tokens, 128), f32),
        pltpu.VMEM((tokens, 128), f32),
        pltpu.VMEM((15, 16, lane_block), bf16),
        pltpu.VMEM((lane_blocks, 16, lane_block), f32),
        pltpu.VMEM((lane_blocks, 8, lane_block), f32),
        pltpu.VMEM((16, 8, lane_block), f32),
        pltpu.VMEM((width, 128), bf16),
        pltpu.VMEM((128, width), bf16),
        pltpu.VMEM(own, bf16),
        pltpu.VMEM(own, bf16),
        pltpu.VMEM(own, bf16),
        pltpu.VMEM(((tokens + 1) * lane_blocks, lane_block), f32),
        pltpu.SemaphoreType.DMA((SEND_SEMS,)),
        pltpu.SemaphoreType.DMA((RECV_SEMS,)),
        pltpu.SemaphoreType.DMA((16,)),
        pltpu.SemaphoreType.DMA((4,)),
    ]
    outs = pl.pallas_call(
        square_kernel,
        out_shape=(
            jax.ShapeDtypeStruct(own, bf16),
            jax.ShapeDtypeStruct((tokens * lane_blocks, lane_block), f32),
            jax.ShapeDtypeStruct((1, rows), f32),
            jax.ShapeDtypeStruct((1, rows), f32),
            jax.ShapeDtypeStruct((rows, 8 * block), bf16),
            jax.ShapeDtypeStruct((2, 2, 2, rows, width), bf16),
            jax.ShapeDtypeStruct((2, rows, 4 * width), bf16),
        ),
        in_specs=[anywhere] * 2 + [vmem] * 3 + [anywhere] * 4,
        out_specs=(anywhere, anywhere, vmem, vmem, anywhere, anywhere, anywhere),
        scratch_shapes=scratch,
        compiler_params=pltpu.CompilerParams(
            collective_id=0, has_side_effects=True, vmem_limit_bytes=VMEM_BYTES
        ),
        cost_estimate=pl.CostEstimate(flops=26 * 10**9, bytes_accessed=2**23, transcendentals=2**21),
    )(
        inputs[:, 0], cotangent[:, 0], frame_flags.reshape(tokens // lane_block, lane_block), attn_gain[0], ffn_gain[0],
        qkv_weight[0, 0], out_weight[0, 0], gate_up_weight[0, 0], down_weight[0, 0].reshape(2, 2, rows, width),
    )
    result, input_grad, gain_one, gain_two, gu, down, attn = outs
    grid = 2

    def by_rows(shape):
        return pl.BlockSpec((shape[0] // grid,) + shape[1:], lambda i: (i, 0))

    def pair(shape):
        return pl.BlockSpec((2, shape[0] // grid) + shape[1:], lambda i: (0, i, 0))

    whole = pl.BlockSpec((1, rows), lambda i: (0, 0))
    thin = (tokens * lane_blocks, lane_block)
    result, input_grad, qkv, out, gu, down, gain_one, gain_two = pl.pallas_call(
        finish_kernel,
        grid=(grid,),
        out_shape=(
            jax.ShapeDtypeStruct(own, bf16),
            jax.ShapeDtypeStruct(thin, f32),
            jax.ShapeDtypeStruct((rows, 3 * width), f32),
            jax.ShapeDtypeStruct((rows, width), f32),
            jax.ShapeDtypeStruct((rows, 8 * block), f32),
            jax.ShapeDtypeStruct(own, f32),
            jax.ShapeDtypeStruct((1, rows), f32),
            jax.ShapeDtypeStruct((1, rows), f32),
        ),
        in_specs=[by_rows(own), by_rows(thin), whole, whole, by_rows((rows, 8 * block)), pair(own), pair((rows, 4 * width))],
        out_specs=[by_rows(own), by_rows(thin), by_rows((rows, 3 * width)), by_rows((rows, width)),
                   by_rows((rows, 8 * block)), by_rows(own), whole, whole],
        compiler_params=pltpu.CompilerParams(vmem_limit_bytes=VMEM_BYTES),
    )(result, input_grad, gain_one, gain_two, gu, down.reshape((2,) + own), attn)
    return (
        result[:, None],
        input_grad.reshape(tokens, 1, width),
        gain_one[None],
        qkv[None, None],
        out[None, None],
        gain_two[None],
        gu[None, None],
        down[None, None],
    )


def finish_kernel(
    result, input_grad, gain_one, gain_two, gu, down, attn,
    result_out, input_grad_out, qkv_out, out_out, gu_out, down_out, gain_one_out, gain_two_out,
):
    f32 = jnp.float32
    width = out_out.shape[1]
    result_out[...] = result[...]
    input_grad_out[...] = input_grad[...]
    gu_out[...] = gu[...].astype(f32)
    down_out[...] = down[0].astype(f32) + down[1].astype(f32)
    total = attn[0].astype(f32) + attn[1].astype(f32)
    qkv_out[...] = total[:, : 3 * width]
    out_out[...] = total[:, 3 * width :]
    gain_one_out[...] = gain_one[...]
    gain_two_out[...] = gain_two[...]


VMEM_BYTES = 62 * 2**20


def run_layer(axes, *args):
    inputs, qkv_weight, down_weight = args[0], args[3], args[7]
    tokens, places, width = inputs.shape
    rows = qkv_weight.shape[2]
    square = (
        axes["fsdp"] == 16
        and axes["pos"] == 2
        and places == 1
        and qkv_weight.shape[0] == 1
        and tokens == 4 * rows
        and down_weight.shape[2] == 4 * rows
        and 128 % rows == 0
    )
    return square_layer(*args) if square else on_device(*args)


def solution(mesh):
    in_specs = (
        P("fsdp", "pos", None),
        P("fsdp"),
        P(None, "pos", "fsdp"),
        P(None, "pos", "fsdp", None),
        P(None, "pos", "fsdp", None),
        P(None, "pos", "fsdp"),
        P(None, "pos", "fsdp", None),
        P(None, "pos", "fsdp", None),
        P("fsdp", "pos", None),
    )
    out_specs = (
        P("fsdp", "pos", None),
        P("fsdp", "pos", None),
        P(None, "pos", "fsdp"),
        P(None, "pos", "fsdp", None),
        P(None, "pos", "fsdp", None),
        P(None, "pos", "fsdp"),
        P(None, "pos", "fsdp", None),
        P(None, "pos", "fsdp", None),
    )
    return jax.shard_map(
        functools.partial(run_layer, dict(mesh.shape)), mesh=mesh, in_specs=in_specs, out_specs=out_specs, check_vma=False
    )
```
